256 devices in a mesh: lat: 64 (over y, x, z_lo), ch: 4 (over z_hi, core).
Axes of the slice: x: 4, y: 4, z: 8 (z_hi: 2, z_lo: 4; z = z_hi * 4 + z_lo), core: 2. Of those that a mesh axis runs over, the one named last changes fastest.
Arguments:
- fields: bfloat16 [256, 1440, 512], P('lat', None, 'ch'), may hold values from -90 to 90, as said below
- norm_gain: bfloat16 [512], P('ch'), may hold values from 0.099609375 to 1.8984375
- w_qkv: bfloat16 [512, 3, 512], P(None, None, 'ch'), may hold values from -0.25 to 0.25
- w_out: bfloat16 [512, 512], P(None, 'ch'), may hold values from -0.25 to 0.25
- rel_bias: float32 [8, 5, 17], P('ch'), may hold values from -2 to 300
- stencil_reach: int32 [256, 5], P('lat'), may hold values from 0 to 8, as said below
- mode_gain: float32 [96, 512], P(None, 'ch'), may hold values from 0.5 to 5
- w_spec: float32 [512, 512], P(None, 'ch'), may hold values from -0.25 to 0.25
Outputs:
- update: bfloat16 [256, 1440, 512], P('lat', None, 'ch')
The draws below stay inside these ranges and needn't reach their ends.
Inputs may be any that keep to these rules, and one draw needn't show every extreme that they name: `fields`: activations whose typical size differs between channels and cells. `stencil_reach`: each row offset's half-width is at least 0, the centre offset's at least 1; 8 is reached in every draw.
All inputs are finite; a program needn't handle non-finite values.
Results may differ from the reference program's by a relative error of at most 0.013.
Values may be sent and summed in bfloat16 or wider, within the bound.
A program may use at most 192 MiB of HBM per device.

```python
import math
import jax
import jax.numpy as jnp
from jax import lax

C = 512
HEADS = 8
NLON = 1440
DEGREES = 96
RAD = 2
WMAX = 8
LON_BLOCK = 160
NLAT = 256


def draw_fields(key, part):
    key = jax.random.fold_in(key, 1)
    column_key, row_key, base_key = jax.random.split(key, 3)
    channel_ramp = (jnp.arange(C, dtype=jnp.float32) + jax.random.uniform(column_key, (C,))) / C
    row_scale = 0.3 * jnp.exp(math.log(10.0) * jax.random.uniform(row_key, (NLAT, NLON, 1)))
    column_scale = 0.3 * jnp.exp(math.log(10.0) * channel_ramp)
    base_values = jnp.clip(jax.random.normal(base_key, (NLAT, NLON, C)), -5.0, 5.0)
    return (base_values * row_scale * column_scale).astype(jnp.bfloat16)


def draw_rel_bias(key, part):
    key = jax.random.fold_in(key, 2)
    small_key = jax.random.fold_in(key, 0)
    shape = (HEADS, 2 * RAD + 1, 2 * WMAX + 1)
    small_values = jax.random.uniform(small_key, shape, minval=-2.0, maxval=2.0)
    result = small_values
    return result.astype(jnp.float32)


def draw_stencil_reach(key, part):
    key = jax.random.fold_in(key, 3)
    radius_draw = jax.random.randint(key, (NLAT, 1), 1, 4)
    row_index = jnp.arange(NLAT, dtype=jnp.int32)
    pole_distance = jnp.minimum(row_index, NLAT - 1 - row_index)
    offset_size = jnp.abs(jnp.arange(2 * RAD + 1, dtype=jnp.int32) - RAD)
    polar_extra = WMAX * (NLAT // (pole_distance + 1)) // 8
    reach_values = jnp.maximum(radius_draw - offset_size[None, :], 0) + polar_extra[:, None]
    return jnp.minimum(reach_values, WMAX).astype(jnp.int32)


def steps_of(stream_key, shape, cuts, low, high):
    level = 1.0
    for dim, blocks in cuts:
        draws = jax.random.uniform(jax.random.fold_in(jax.random.fold_in(stream_key, 6), dim), (blocks,), jnp.float32, low / len(cuts), high / len(cuts))
        level = level * jnp.repeat(jnp.exp(draws), shape[dim] // blocks).reshape((-1,) + (1,) * (len(shape) - 1 - dim))
    return level


def gaussian(rng, dims, width, most, cuts=(), kind=jnp.bfloat16):
    values = width * jax.random.normal(rng, dims, jnp.float32)
    if cuts:
        values = values * steps_of(rng, dims, cuts, -0.22, 0.18)
    return jnp.clip(values, -most, most).astype(kind)


def setup_inputs(seed: int = 0) -> dict:
    key_of = jax.random.split(jax.random.key(seed), 9)
    fields = draw_fields(jax.random.fold_in(key_of[8], 71), 0)
    norm_gain = jnp.clip(1.0 + 0.18 * jax.random.normal(key_of[1], (C,), jnp.float32), 0.099609375, 1.8984375).astype(jnp.bfloat16)
    w_qkv = gaussian(key_of[2], (C, 3, C), C ** -0.5, 0.25, ((2, 4),))
    w_out = gaussian(key_of[3], (C, C), C ** -0.5, 0.25, ((1, 4),))
    rel_bias = draw_rel_bias(jax.random.fold_in(key_of[8], 71), 0)
    stencil_reach = draw_stencil_reach(jax.random.fold_in(key_of[8], 71), 0)
    mode_gain = jnp.clip(jnp.exp(math.log(5.0) - 2.3025851 * jax.random.uniform(key_of[6], (DEGREES, C), jnp.float32) ** steps_of(key_of[6], (DEGREES, C), ((1, 4),), -0.2, 0.2)), 0.5, 5.0)
    w_spec = gaussian(key_of[7], (C, C), C ** -0.5, 0.25, ((1, 4),), jnp.float32)
    return dict(fields=fields, norm_gain=norm_gain, w_qkv=w_qkv, w_out=w_out, rel_bias=rel_bias, stencil_reach=stencil_reach, mode_gain=mode_gain, w_spec=w_spec)


epsilon = 1e-05
highest = lax.Precision.HIGHEST

def legendre_table(colatitude, degree_count):
    cosine = jnp.cos(colatitude)[:, None]
    log_sine = jnp.log(jnp.sin(colatitude))[:, None]
    orders = jnp.arange(degree_count, dtype=jnp.float32)
    factors = jnp.arange(1, degree_count, dtype=jnp.float32)
    log_ratio = jnp.log((2.0 * factors - 1.0) / (2.0 * factors))
    log_product = jnp.concatenate([jnp.zeros((1,), jnp.float32), jnp.cumsum(log_ratio)])
    diagonal = jnp.exp(0.5 * (jnp.log((2.0 * orders + 1.0) / (4.0 * math.pi)) + log_product)[None, :] + orders[None, :] * log_sine)
    previous = jnp.zeros_like(diagonal)
    earlier = jnp.zeros_like(diagonal)
    levels = []
    for degree in range(degree_count):
        degree_value = float(degree)
        upper_coef = jnp.sqrt(max(4.0 * degree_value * degree_value - 1.0, 0.0) / jnp.maximum(degree_value * degree_value - orders * orders, 1.0))
        lower_coef = jnp.sqrt(jnp.maximum((degree_value - 1.0) ** 2 - orders * orders, 0.0) / max(4.0 * (degree_value - 1.0) ** 2 - 1.0, 1.0))
        step_value = upper_coef[None, :] * (cosine * previous - lower_coef[None, :] * earlier)
        current = jnp.where(orders[None, :] == degree_value, diagonal, jnp.where(orders[None, :] < degree_value, step_value, 0.0))
        levels.append(current)
        earlier = previous
        previous = current
    return jnp.stack(levels, axis=1)

def fourier_tables(degree_count, lon_count):
    lon_index = jnp.arange(lon_count, dtype=jnp.int32)
    order_index = jnp.arange(degree_count, dtype=jnp.int32)
    phases = (lon_index[:, None] * order_index[None, :] % lon_count).astype(jnp.float32) * (2.0 * math.pi / lon_count)
    cosine = jnp.cos(phases)
    sine_table = jnp.sin(phases)
    spacing = 2.0 * math.pi / lon_count
    forward = jnp.stack([cosine, -sine_table], axis=1) * spacing
    factor = jnp.where(order_index == 0, 1.0, 2.0).astype(jnp.float32)[:, None]
    inverse = jnp.stack([cosine.T * factor, -sine_table.T * factor], axis=0)
    return (forward, inverse)

def key_windows(row_block, half_width, lon_block):
    offset_count, lon_count, feature = row_block.shape
    block_count = lon_count // lon_block
    extended = jnp.concatenate([row_block[:, lon_count - half_width:], row_block, row_block[:, :lon_block + half_width]], axis=1)
    leading = extended[:, :lon_count].reshape(offset_count, block_count, lon_block, feature)
    trailing = extended[:, lon_block:lon_count + lon_block].reshape(offset_count, block_count, lon_block, feature)[:, :, :2 * half_width]
    return jnp.concatenate([leading, trailing], axis=2)

def make_tiles(rel_bias, lon_block):
    half_width = (rel_bias.shape[2] - 1) // 2
    query_pos = jnp.arange(lon_block, dtype=jnp.int32)[:, None]
    key_pos = jnp.arange(lon_block + 2 * half_width, dtype=jnp.int32)[None, :]
    distance = jnp.abs(key_pos - half_width - query_pos)
    onehot = ((key_pos - query_pos)[:, :, None] == jnp.arange(2 * half_width + 1, dtype=jnp.int32)[None, None, :]).astype(jnp.float32)
    bias_tiles = jnp.einsum('hre,pte->hrpt', rel_bias, onehot, precision=highest)
    return (bias_tiles, distance)

def attend_row(query_row, key_rows, value_rows, reach_row, valid_rows, bias_tiles, distance, half_width, lon_block):
    head_count = bias_tiles.shape[0]
    lon_count, feature = query_row.shape
    head_dim = feature // head_count
    block_count = lon_count // lon_block
    key_win = key_windows(key_rows, half_width, lon_block)
    value_win = key_windows(value_rows, half_width, lon_block)
    allowed = (distance[None] <= reach_row[:, None, None]) & valid_rows[:, None, None]
    score_scale = 1.0 / math.sqrt(head_dim)
    pieces = []
    for head_index in range(head_count):
        start_ch = head_index * head_dim
        stop_ch = start_ch + head_dim
        query_head = query_row[:, start_ch:stop_ch].reshape(block_count, lon_block, head_dim).astype(jnp.float32)
        scores = jnp.einsum('bpd,rbtd->rbpt', query_head, key_win[..., start_ch:stop_ch].astype(jnp.float32)) * score_scale + bias_tiles[head_index][:, None]
        scores = jnp.where(allowed[:, None], scores, -jnp.inf)
        largest = lax.optimization_barrier(jnp.max(scores, axis=(0, 3), keepdims=True))
        exponent = jnp.exp(scores - largest)
        weights = (exponent / lax.optimization_barrier(jnp.sum(exponent, axis=(0, 3), keepdims=True))).astype(jnp.bfloat16)
        head_out = jnp.einsum('rbpt,rbtd->bpd', weights.astype(jnp.float32), value_win[..., start_ch:stop_ch].astype(jnp.float32))
        pieces.append(head_out.reshape(lon_count, head_dim))
    return jnp.concatenate(pieces, axis=1).astype(jnp.bfloat16)

def reference(fields, norm_gain, w_qkv, w_out, rel_bias, stencil_reach, mode_gain, w_spec):
    lat_total, lon_count, channels = fields.shape
    offsets = 2 * RAD + 1
    fields_float = fields.astype(jnp.float32)
    mean_square = lax.optimization_barrier(jnp.sum(fields_float * fields_float, axis=-1, keepdims=True)) / channels
    normed = (fields_float * lax.rsqrt(mean_square + epsilon) * norm_gain.astype(jnp.float32)).astype(jnp.bfloat16)
    weight_flat = w_qkv.reshape(channels, 3 * channels)

    def project_row(normed_row):
        return jnp.dot(normed_row, weight_flat, preferred_element_type=jnp.float32).astype(jnp.bfloat16)
    projected = lax.map(project_row, normed).reshape(lat_total, lon_count, 3, channels)
    queries = projected[:, :, 0]
    key_padded = jnp.pad(projected[:, :, 1], ((RAD, RAD), (0, 0), (0, 0)))
    value_padded = jnp.pad(projected[:, :, 2], ((RAD, RAD), (0, 0), (0, 0)))
    bias_tiles, distance = make_tiles(rel_bias, LON_BLOCK)

    def attend_at(row_index):
        key_rows = lax.dynamic_slice_in_dim(key_padded, row_index, offsets, 0)
        value_rows = lax.dynamic_slice_in_dim(value_padded, row_index, offsets, 0)
        neighbour = row_index + jnp.arange(offsets, dtype=jnp.int32) - RAD
        valid_rows = (neighbour >= 0) & (neighbour < lat_total)
        reach_row = lax.dynamic_index_in_dim(stencil_reach, row_index, 0, keepdims=False)
        query_row = lax.dynamic_index_in_dim(queries, row_index, 0, keepdims=False)
        return attend_row(query_row, key_rows, value_rows, reach_row, valid_rows, bias_tiles, distance, WMAX, LON_BLOCK)
    attended = lax.map(attend_at, jnp.arange(lat_total, dtype=jnp.int32))
    colatitude = (jnp.arange(lat_total, dtype=jnp.int32).astype(jnp.float32) + 0.5) * (math.pi / lat_total)
    legendre = legendre_table(colatitude, DEGREES)
    weighted = legendre * (jnp.sin(colatitude) * (math.pi / lat_total))[:, None, None]
    forward, inverse = fourier_tables(DEGREES, lon_count)

    def transform_row(normed_row):
        return jnp.einsum('jc,jsm->smc', normed_row.astype(jnp.float32), forward, precision=highest)
    frequency = lax.map(transform_row, normed)
    coefficients = jnp.einsum('rlm,rsmc->lmsc', weighted, frequency, precision=highest)
    gained = coefficients * mode_gain[:, None, None, :]
    mixed_modes = jnp.einsum('lmsk,ko->lmso', gained, w_spec, precision=highest).astype(jnp.bfloat16)
    back_modes = jnp.einsum('rlm,lmsc->rsmc', legendre, mixed_modes.astype(jnp.float32), precision=highest)

    def finish_row(row_parts):
        attended_row, back_row = row_parts
        local_part = jnp.dot(attended_row, w_out, preferred_element_type=jnp.float32)
        spectral_part = jnp.einsum('smc,smj->jc', back_row, inverse, precision=highest)
        return (local_part + spectral_part).astype(jnp.bfloat16)
    return lax.map(finish_row, (attended, back_modes))
```

```python
import functools
import math

import jax
import jax.numpy as jnp
from jax import lax
from jax.experimental import pallas as pl
from jax.experimental.pallas import tpu as pltpu
from jax.sharding import PartitionSpec as P

MESH = pl.DeviceIdType.MESH
NLON = 1440
NLAT = 256
DEG = 96
LOG2E = 1.4426950408889634
NEG = -1e30
EPS = 1e-05
KB = 48
KEYS = 5 * KB


def win_start(w):
    return (w * 90 // 16) * 16


def ring_dev(w, group):
    return (group * 4 + w // 4, w % 4)


def mult16(v):
    return pl.multiple_of(v, 16)


def place():
    lat = lax.axis_index("lat")
    ch = lax.axis_index("ch")
    return lat, ch, lat // 4, lat % 4


def exchange_kernel(f_ref, m_ref, out_ref, mout_ref, lsem, ssem, rsem, hssem, hrsem, mssem, mrsem):
    lat, ch, group, zlo = place()
    me = zlo * 4 + ch
    bar = pltpu.get_barrier_semaphore()
    has_next = group < 15
    has_prev = group > 0
    for d in range(1, 16):
        w = (me + d) % 16
        pl.semaphore_signal(bar, inc=1, device_id=ring_dev(w, group), device_id_type=MESH)

    @pl.when(has_next)
    def _():
        for k in range(4):
            pl.semaphore_signal(bar, inc=1, device_id=((group + 1) * 4, k), device_id_type=MESH)

    @pl.when(has_prev)
    def _():
        for k in range(4):
            pl.semaphore_signal(bar, inc=1, device_id=((group - 1) * 4 + 3, k), device_id_type=MESH)

    edge = (has_next & (zlo == 3)) | (has_prev & (zlo == 0))
    pl.semaphore_wait(bar, jnp.where(edge, 31, 15))

    def pieces(w):
        s = win_start(w)
        a_src = jnp.where(w == 0, 0, s - 16)
        a_dst = jnp.where(w == 0, 16, 0)
        b_src = jnp.where(w == 0, NLON - 16, jnp.where(w == 15, 0, s + 96))
        b_dst = jnp.where(w == 0, 0, 112)
        return (mult16(a_src), mult16(a_dst), 112), (mult16(b_src), mult16(b_dst), 16)

    row0 = 2 + 4 * zlo

    def send(w, src_row, nrow, dst_row, to_group, ss, rs):
        for src, dst, n in pieces(w):
            pltpu.make_async_remote_copy(
                src_ref=f_ref.at[pl.ds(src_row, nrow), pl.ds(src, n)],
                dst_ref=out_ref.at[pl.ds(dst_row, nrow), ch, pl.ds(dst, n)],
                send_sem=ss,
                recv_sem=rs,
                device_id=ring_dev(w, to_group),
                device_id_type=MESH,
            ).start()

    @pl.when(has_next & (zlo == 3))
    def _():
        def body(d, c):
            send((me + d) % 16, 2, 2, 0, group + 1, hssem.at[0], hrsem.at[0])
            return c

        lax.fori_loop(0, 16, body, 0)

    @pl.when(has_prev & (zlo == 0))
    def _():
        def body(d, c):
            send((me + d) % 16, 0, 2, 18, group - 1, hssem.at[1], hrsem.at[1])
            return c

        lax.fori_loop(0, 16, body, 0)

    def body(d, c):
        w = (me + d) % 16
        pltpu.make_async_remote_copy(
            src_ref=m_ref,
            dst_ref=mout_ref.at[me],
            send_sem=mssem,
            recv_sem=mrsem,
            device_id=ring_dev(w, group),
            device_id_type=MESH,
        ).start()
        send(w, 0, 4, row0, group, ssem, rsem)
        return c

    lax.fori_loop(1, 16, body, 0)
    local = [pltpu.make_async_copy(m_ref, mout_ref.at[me], lsem.at[2])]
    for i, (src, dst, n) in enumerate(pieces(me)):
        local.append(
            pltpu.make_async_copy(
                f_ref.at[:, pl.ds(src, n)], out_ref.at[pl.ds(row0, 4), ch, pl.ds(dst, n)], lsem.at[i]
            )
        )
    for copy in local:
        copy.start()
    for copy in local:
        copy.wait()

    def wait_rows(sem, rows):
        ref = out_ref.at[pl.ds(0, rows // 4)]
        pltpu.make_async_copy(ref, ref, sem).wait()

    wait_rows(ssem, 60)
    wait_rows(rsem, 60)
    meta = mout_ref.at[pl.ds(0, 15)]
    pltpu.make_async_copy(meta, meta, mssem).wait()
    pltpu.make_async_copy(meta, meta, mrsem).wait()

    @pl.when(has_next & (zlo == 3))
    def _():
        wait_rows(hssem.at[0], 32)

    @pl.when(has_prev & (zlo == 0))
    def _():
        wait_rows(hssem.at[1], 32)

    @pl.when(has_prev)
    def _():
        wait_rows(hrsem.at[0], 8)

    @pl.when(has_next)
    def _():
        wait_rows(hrsem.at[1], 8)


def exchange(fields, meta):
    dma = pltpu.SemaphoreType.DMA
    return pl.pallas_call(
        exchange_kernel,
        out_shape=(
            jax.ShapeDtypeStruct((20, 4, 128, 128), jnp.bfloat16),
            jax.ShapeDtypeStruct((16, 8, 128), jnp.float32),
        ),
        in_specs=[pl.BlockSpec(memory_space=pl.ANY)] * 2,
        out_specs=[pl.BlockSpec(memory_space=pl.ANY)] * 2,
        scratch_shapes=[dma((3,)), dma, dma, dma((2,)), dma((2,)), dma, dma],
        compiler_params=pltpu.CompilerParams(collective_id=0, has_side_effects=True),
        name="exchange",
    )(fields, meta)


def back_kernel(y_ref, out_ref, lsem, ssem, rsem):
    lat, ch, group, zlo = place()
    me = zlo * 4 + ch
    bar = pltpu.get_barrier_semaphore()
    for d in range(1, 16):
        w = (me + d) % 16
        pl.semaphore_signal(bar, inc=1, device_id=ring_dev(w, group), device_id_type=MESH)
    pl.semaphore_wait(bar, 15)
    s = mult16(win_start(me))
    wide = win_start(me + 1) - win_start(me) == 96

    def body(d, c):
        w = (me + d) % 16
        for lo, n, cond in ((0, 80, None), (80, 16, wide)):

            def go(lo=lo, n=n):
                pltpu.make_async_remote_copy(
                    src_ref=y_ref.at[pl.ds((w // 4) * 4, 4), w % 4, pl.ds(lo, n)],
                    dst_ref=out_ref.at[:, pl.ds(mult16(s + lo), n)],
                    send_sem=ssem,
                    recv_sem=rsem,
                    device_id=ring_dev(w, group),
                    device_id_type=MESH,
                ).start()

            if cond is None:
                go()
            else:
                pl.when(cond)(go)
        return c

    lax.fori_loop(1, 16, body, 0)

    def local(lo, n):
        copy = pltpu.make_async_copy(
            y_ref.at[pl.ds(zlo * 4, 4), ch, pl.ds(lo, n)], out_ref.at[:, pl.ds(mult16(s + lo), n)], lsem
        )
        copy.start()
        copy.wait()

    local(0, 80)
    pl.when(wide)(lambda: local(80, 16))

    def wait_lons(sem, lons):
        ref = out_ref.at[:, pl.ds(0, lons)]
        pltpu.make_async_copy(ref, ref, sem).wait()

    @pl.when(wide)
    def _():
        wait_lons(ssem, 1440)
        wait_lons(rsem, 1344)

    @pl.when(jnp.logical_not(wide))
    def _():
        wait_lons(ssem, 1200)
        wait_lons(rsem, 1360)


def back(y):
    dma = pltpu.SemaphoreType.DMA
    return pl.pallas_call(
        back_kernel,
        out_shape=jax.ShapeDtypeStruct((4, NLON, 128), jnp.bfloat16),
        in_specs=[pl.BlockSpec(memory_space=pl.ANY)],
        out_specs=pl.BlockSpec(memory_space=pl.ANY),
        scratch_shapes=[dma, dma, dma],
        compiler_params=pltpu.CompilerParams(collective_id=1, has_side_effects=True),
        name="back",
    )(y)


def attend_kernel(x_ref, gain_ref, w_ref, wo_ref, bias_ref, reach_ref, y_ref, q_s, k_s, v_s, b_s, t_s, a_s):
    _, _, group, _ = place()
    lane = lax.broadcasted_iota(jnp.int32, (32, KEYS), 1)
    query = lax.broadcasted_iota(jnp.int32, (32, KEYS), 0)
    offset = sum((lane >= KB * a).astype(jnp.int32) for a in range(1, 5))
    delta = lane - KB * offset - query - 8
    dist = jnp.abs(delta).astype(jnp.float32)
    for h in range(8):
        tile = jnp.full((32, KEYS), NEG, jnp.float32)
        for b in range(17):
            tile = jnp.where(delta == b - 8, bias_ref[h, b : b + 1, :], tile)
        b_s[h // 2, (h % 2) * 32 : (h % 2) * 32 + 32, :] = tile

    def project(step, c):
        rows = pl.ds(step * 4, 4)
        parts = [x_ref[rows, k].reshape(512, 128).astype(jnp.float32) for k in range(4)]
        total = sum(p * p for p in parts)
        square = jnp.sum(total, axis=1, keepdims=True)
        scale = lax.rsqrt(square * (1.0 / 512.0) + EPS)
        outside = ((step == 0) & (group == 0), (step == 4) & (group == 15))
        row = lax.broadcasted_iota(jnp.int32, (512, 1), 0)
        drop = (outside[0] & (row < 256)) | (outside[1] & (row >= 256))
        normed = jnp.concatenate(
            [
                jnp.where(drop, 0.0, p * scale * gain_ref[k : k + 1, :]).astype(jnp.bfloat16)
                for k, p in enumerate(parts)
            ],
            axis=1,
        )
        for t, dst, lo, n, mul in ((0, q_s, 16, 96, LOG2E / 8.0), (1, k_s, 8, 112, None), (2, v_s, 8, 112, None)):
            out = jnp.dot(normed, w_ref[:, t * 512 : t * 512 + 512], preferred_element_type=jnp.float32)
            out = out.reshape(4, 128, 512)[:, lo : lo + n, :]
            if mul is not None:
                out = out * mul
            dst[rows] = out.astype(jnp.bfloat16)
        return c

    lax.fori_loop(0, 5, project, 0)
    left = lax.broadcasted_iota(jnp.int32, (32, 128), 1) < 64

    def attend_row(i, c):
        reach = reach_ref[pl.ds(i, 1), :]
        allowed = dist <= reach
        for hp in range(4):
            t_s[hp, 0:32, :] = jnp.where(allowed, b_s[hp, 0:32, :], NEG)
            t_s[hp, 32:64, :] = jnp.where(allowed, b_s[hp, 32:64, :], NEG)
        for j in range(3):
            for hp in range(4):
                cols = slice(hp * 128, hp * 128 + 128)
                qb = q_s[i + 2, j * 32 : j * 32 + 32, cols]
                zero = jnp.zeros_like(qb)
                qq = jnp.concatenate([jnp.where(left, qb, zero), jnp.where(left, zero, qb)], axis=0)
                kb = k_s[pl.ds(i, 5), j * 32 : j * 32 + KB, cols].reshape(KEYS, 128)
                vb = v_s[pl.ds(i, 5), j * 32 : j * 32 + KB, cols].reshape(KEYS, 128)
                s = lax.dot_general(qq, kb, (((1,), (1,)), ((), ())), preferred_element_type=jnp.float32)
                s = s + t_s[hp]
                top = jnp.max(s, axis=1, keepdims=True)
                p = jnp.exp2(s - top)
                total = jnp.sum(p, axis=1, keepdims=True)
                o = jnp.dot(p.astype(jnp.bfloat16), vb, preferred_element_type=jnp.float32)
                o = o / total
                o = jnp.where(left, o[:32], o[32:])
                a_s[i, j * 32 : j * 32 + 32, cols] = o.astype(jnp.bfloat16)
        return c

    lax.fori_loop(0, 16, attend_row, 0)

    def finish(step, c):
        rows = pl.ds(step * 4, 4)
        att = a_s[rows].reshape(384, 512)
        out = jnp.dot(att, wo_ref[...], preferred_element_type=jnp.float32)
        for k in range(4):
            y_ref[rows, k] = out[:, k * 128 : k * 128 + 128].reshape(4, 96, 128).astype(jnp.bfloat16)
        return c

    lax.fori_loop(0, 4, finish, 0)


def attend(x, gain, w, wo, bias, reach):
    bf = jnp.bfloat16
    vmem = pl.BlockSpec(memory_space=pltpu.VMEM)
    return pl.pallas_call(
        attend_kernel,
        out_shape=jax.ShapeDtypeStruct((16, 4, 96, 128), bf),
        in_specs=[vmem] * 6,
        out_specs=vmem,
        scratch_shapes=[
            pltpu.VMEM((20, 96, 512), bf),
            pltpu.VMEM((20, 112, 512), bf),
            pltpu.VMEM((20, 112, 512), bf),
            pltpu.VMEM((4, 64, KEYS), jnp.float32),
            pltpu.VMEM((4, 64, KEYS), jnp.float32),
            pltpu.VMEM((16, 96, 512), bf),
        ],
        compiler_params=pltpu.CompilerParams(vmem_limit_bytes=48 * 1024 * 1024),
        cost_estimate=pl.CostEstimate(flops=10**10, bytes_accessed=8 * 10**6, transcendentals=0),
        name="attend",
    )(x, gain, w, wo, bias, reach)


def legendre_kernel(m_ref, d_ref, cos_ref, out_ref):
    m = m_ref[...]
    cosine = cos_ref[...]
    diagonal = d_ref[...]

    def step(l, carry):
        previous, earlier = carry
        deg = l.astype(jnp.float32)
        upper = jnp.sqrt(jnp.maximum(4.0 * deg * deg - 1.0, 0.0) / jnp.maximum(deg * deg - m * m, 1.0))
        less = deg - 1.0
        lower = jnp.sqrt(jnp.maximum(less * less - m * m, 0.0) / jnp.maximum(4.0 * less * less - 1.0, 1.0))
        value = upper * (cosine * previous - lower * earlier)
        current = jnp.where(m == deg, diagonal, jnp.where(m < deg, value, 0.0))
        for k in range(3):
            out_ref[k, pl.ds(l, 1), :] = current[k : k + 1, :]
        return current, previous

    zero = diagonal * 0.0
    lax.fori_loop(0, DEG, step, (zero, zero))


def legendre_rows(lat, colatitude):
    pair = lat * 3 + jnp.arange(8, dtype=jnp.int32)
    order = jnp.minimum(pair // 2, DEG - 1)
    factors = jnp.arange(1, DEG, dtype=jnp.float32)
    log_ratio = jnp.log((2.0 * factors - 1.0) / (2.0 * factors))
    log_product = jnp.concatenate([jnp.zeros((1,), jnp.float32), jnp.cumsum(log_ratio)])
    orders = jnp.arange(DEG, dtype=jnp.float32)
    base = 0.5 * (jnp.log((2.0 * orders + 1.0) / (4.0 * math.pi)) + log_product)
    pick = order[:, None] == jnp.arange(DEG, dtype=jnp.int32)[None, :]
    mine = jnp.sum(jnp.where(pick, base[None, :], 0.0), axis=1)
    m = order.astype(jnp.float32)
    diagonal = jnp.exp(mine[:, None] + m[:, None] * jnp.log(jnp.sin(colatitude))[None, :])
    vmem = pl.BlockSpec(memory_space=pltpu.VMEM)
    return pl.pallas_call(
        legendre_kernel,
        out_shape=jax.ShapeDtypeStruct((3, DEG, NLAT), jnp.float32),
        in_specs=[vmem] * 3,
        out_specs=vmem,
        name="legendre",
    )(
        jnp.broadcast_to(m[:, None], (8, NLAT)),
        diagonal,
        jnp.broadcast_to(jnp.cos(colatitude)[None, :], (8, NLAT)),
    )


def wave_table():
    coarse = jnp.arange(45, dtype=jnp.int32) * 32
    fine = jnp.arange(32, dtype=jnp.int32)
    order = jnp.arange(2 * DEG, dtype=jnp.int32) // 2

    def angle(cells):
        return (cells[:, None] * order[None, :] % NLON).astype(jnp.float32) * (2.0 * math.pi / NLON)

    a, b = angle(coarse)[:, None, :], angle(fine)[None, :, :]
    ca, sa, cb, sb = jnp.cos(a), jnp.sin(a), jnp.cos(b), jnp.sin(b)
    even = (jnp.arange(2 * DEG) % 2 == 0)[None, None, :]
    return jnp.where(even, ca * cb - sa * sb, -(sa * cb + ca * sb)).astype(jnp.bfloat16).reshape(NLON, 2 * DEG)


def spectral_modes(fields, norm_gain, mode_gain, w_spec, table):
    bf, f32 = jnp.bfloat16, jnp.float32
    lat = lax.axis_index("lat")
    x = fields.astype(f32)
    squares = lax.psum(jnp.sum(x * x, axis=-1), "ch")
    scale = lax.rsqrt(squares / 512.0 + EPS)
    normed = (x * scale[..., None] * norm_gain.astype(f32)).astype(bf)
    freq = jnp.einsum("rjc,jk->krc", normed, table, preferred_element_type=f32)
    freq = jnp.pad(freq.reshape(64, 12, 128), ((0, 0), (0, 4), (0, 0))).astype(bf)
    got = lax.all_to_all(freq, "lat", 0, 0, tiled=True)[:, :12].reshape(64, 3, 4, 128)
    got = jnp.moveaxis(got, 1, 0).reshape(3, NLAT, 128)
    colatitude = (jnp.arange(NLAT, dtype=jnp.int32).astype(f32) + 0.5) * (math.pi / NLAT)
    legendre = legendre_rows(lat, colatitude)
    weight = jnp.sin(colatitude) * (math.pi / NLAT * 2.0 * math.pi / NLON)
    coef = jnp.einsum("kli,kic->klc", (legendre * weight).astype(bf), got, preferred_element_type=f32)
    gained = (coef * mode_gain[None]).astype(bf).reshape(3 * DEG, 128)
    gained = lax.all_gather(gained, "ch", axis=1, tiled=True)
    mixed = jnp.dot(gained, w_spec.astype(bf), preferred_element_type=f32).astype(bf).reshape(3, DEG, 128)
    modes = jnp.einsum("kli,klc->ikc", legendre.astype(bf), mixed, preferred_element_type=f32)
    factor = jnp.where(lat * 3 + jnp.arange(3) < 2, 1.0, 2.0).astype(f32)
    modes = modes * factor[None, :, None]
    modes = jnp.pad(modes.reshape(64, 12, 128), ((0, 0), (0, 4), (0, 0))).astype(bf)
    modes = lax.all_to_all(modes, "lat", 0, 0, tiled=True)[:, :12].reshape(64, 4, 3, 128)
    return jnp.moveaxis(modes, 1, 0).reshape(4, 2 * DEG, 128)


def per_device(fields, norm_gain, w_qkv, w_out, rel_bias, stencil_reach, mode_gain, w_spec):
    bf, f32 = jnp.bfloat16, jnp.float32
    group = lax.axis_index("lat") // 4
    meta = jnp.concatenate(
        [norm_gain.astype(f32), rel_bias.reshape(170), jnp.zeros((86,), f32), stencil_reach.astype(f32).reshape(20), jnp.zeros((620,), f32)]
    ).reshape(8, 128)
    weights = jnp.concatenate([w_qkv, w_out[:, None, :]], axis=1)
    weights = lax.all_gather(weights, "ch", axis=0, tiled=False)
    x, metas = exchange(fields, meta)
    w_all = jnp.moveaxis(weights, 0, 2)
    w_all = w_all.reshape(512, 2048)
    gain = metas[:4, 0]
    bias = metas[:4, 1:3].reshape(4, 256)[:, :170].reshape(8, 5, 17) * LOG2E
    bias = jnp.repeat(jnp.moveaxis(bias, 1, 2), KB, axis=2)
    reach = metas[::4, 3, :20].reshape(16, 5)
    row = group * 16 + jnp.arange(16, dtype=jnp.int32)[:, None] + jnp.arange(5, dtype=jnp.int32)[None, :] - 2
    reach = jnp.where((row >= 0) & (row < NLAT), reach, -1.0)
    reach = jnp.repeat(reach, KB, axis=1)
    y = attend(x, gain, w_all[:, :1536], w_all[:, 1536:], bias, reach)
    local = back(y)
    table = wave_table()
    modes = spectral_modes(fields, norm_gain, mode_gain, w_spec, table)
    spectral = jnp.einsum("jk,rkc->rjc", table, modes, preferred_element_type=f32)
    return (local.astype(f32) + spectral).astype(bf)


def solution(mesh):
    in_specs = (
        P("lat", None, "ch"),
        P("ch"),
        P(None, None, "ch"),
        P(None, "ch"),
        P("ch", None, None),
        P("lat", None),
        P(None, "ch"),
        P(None, "ch"),
    )
    return jax.shard_map(
        per_device, mesh=mesh, in_specs=in_specs, out_specs=P("lat", None, "ch"), check_vma=False
    )
```

```python
import math

import jax
import jax.numpy as jnp
from jax import lax
from jax.experimental import pallas as pl
from jax.experimental.pallas import tpu as pltpu
from jax.sharding import PartitionSpec as P

MESH = pl.DeviceIdType.MESH
NLON = 1440
NLAT = 256
DEG = 96
OCT = 180
LOG2E = 1.4426950408889634
NEG = -1e30
EPS = 1e-05
KB = 48
KEYS = 5 * KB
F32 = jnp.float32
BF = jnp.bfloat16
DMA = pltpu.SemaphoreType.DMA
VMEM = pl.BlockSpec(memory_space=pltpu.VMEM)
ANY = pl.BlockSpec(memory_space=pl.ANY)
TN = (((0,), (0,)), ((), ()))
NT = (((1,), (1,)), ((), ()))


def win_start(w):
    return 45 * w // 4


def ring_dev(w, group):
    return (group * 4 + w // 4, w % 4)


def place():
    lat = lax.axis_index("lat")
    ch = lax.axis_index("ch")
    return lat, ch, lat // 4, lat % 4


def signal(device):
    pl.semaphore_signal(pltpu.get_barrier_semaphore(), inc=1, device_id=device, device_id_type=MESH)


def remote(src, dst, ss, rs, device):
    pltpu.make_async_remote_copy(
        src_ref=src, dst_ref=dst, send_sem=ss, recv_sem=rs, device_id=device, device_id_type=MESH
    ).start()


def wait_bytes(ref, sem):
    pltpu.make_async_copy(ref, ref, sem).wait()


def loop(lo, hi, body):
    def step(i, c):
        body(i)
        return c

    lax.fori_loop(lo, hi, step, 0)


def sort_rows():
    n = lax.broadcasted_iota(jnp.int32, (1024, 1), 0)
    slot = n % 16
    source = jnp.where(slot < 12, (slot % 4) * 192 + (slot // 4) * 64 + n // 16, -1)
    return (lax.broadcasted_iota(jnp.int32, (1024, 768), 1) == source).astype(F32).astype(BF)


def gather_kernel(
    f_ref, sq_ref, meta_ref, gw_ref, ca_ref, sa_ref, u_ref, v_ref, m_ref, diag_ref, cos_ref,
    win_ref, metas_ref, modes_ref, e_ref, t_ref,
    x_s, stat_s, tab_s, leg_s, send_s,
    lsem, ssem, rsem, hssem, hrsem, mssem, mrsem, qssem, qrsem, assem, arsem,
):
    lat, ch, group, zlo = place()
    me = zlo * 4 + ch
    has_next = group < 15
    has_prev = group > 0
    up = has_next & (zlo == 3)
    down = has_prev & (zlo == 0)
    loop(1, 64, lambda d: signal(((lat + d) % 64, ch)))
    loop(1, 16, lambda d: signal(ring_dev((me + d) % 16, group)))

    @pl.when(has_next)
    def _():
        for k in range(4):
            signal(((group + 1) * 4, k))

    @pl.when(has_prev)
    def _():
        for k in range(4):
            signal(((group - 1) * 4 + 3, k))

    def interleave(c):
        lon = pl.ds(pl.multiple_of(c * 144, 16), 144)
        for a in range(2):
            two = [f_ref[2 * a + b, lon, :].astype(F32).reshape(18, 8, 128) for b in range(2)]
            x_s[a, pl.ds(c * 18, 18)] = jnp.stack(two, axis=1).reshape(18, 16, 128).astype(BF)

    loop(0, 10, interleave)
    stat_s[ch] = sq_ref[...]
    pl.semaphore_wait(pltpu.get_barrier_semaphore(), jnp.where(up | down, 94, 78))

    for d in range(1, 4):
        remote(sq_ref, stat_s.at[ch], qssem, qrsem, (lat, (ch + d) % 4))
    for d in range(1, 4):
        remote(meta_ref, metas_ref.at[me], mssem, mrsem, (lat, (ch + d) % 4))
        remote(meta_ref, metas_ref.at[me], mssem, mrsem, (group * 4 + (zlo + d) % 4, ch))
    mcopy = pltpu.make_async_copy(meta_ref, metas_ref.at[me], lsem.at[2])
    mcopy.start()

    def move(w, src_pair, pairs, dst_pair, to_group, start):
        s = win_start(w)
        src, dst = pl.ds(src_pair, pairs), pl.ds(dst_pair, pairs)
        edge = (w == 0) | (w == 15)

        @pl.when(edge)
        def _():
            a_src = jnp.where(w == 0, 0, s - 1)
            a_dst = jnp.where(w == 0, 1, 0)
            b_src = jnp.where(w == 0, OCT - 1, 0)
            b_dst = jnp.where(w == 0, 0, 13)
            start(x_s.at[src, pl.ds(a_src, 13)], win_ref.at[dst, ch, pl.ds(a_dst, 13)], 0)
            start(x_s.at[src, pl.ds(b_src, 1)], win_ref.at[dst, ch, pl.ds(b_dst, 1)], 1)

        @pl.when(jnp.logical_not(edge))
        def _():
            start(x_s.at[src, pl.ds(s - 1, 14)], win_ref.at[dst, ch], 0)

    def send(w, src_pair, pairs, dst_pair, to_group, ss, rs):
        move(w, src_pair, pairs, dst_pair, to_group,
             lambda a, b, n: remote(a, b, ss, rs, ring_dev(w, to_group)))

    @pl.when(up)
    def _():
        loop(0, 16, lambda d: send((me + d) % 16, 1, 1, 0, group + 1, hssem.at[0], hrsem.at[0]))

    @pl.when(down)
    def _():
        loop(0, 16, lambda d: send((me + d) % 16, 0, 1, 9, group - 1, hssem.at[1], hrsem.at[1]))

    pair0 = 1 + 2 * zlo
    loop(1, 16, lambda d: send((me + d) % 16, 0, 2, pair0, group, ssem, rsem))
    move(me, 0, 2, pair0, group, lambda a, b, n: pltpu.make_async_copy(a, b, lsem.at[n]).start())

    for a in range(12):
        n = min(128, NLON - a * 128)
        tab = ca_ref[:, a : a + 1] * u_ref[...] + sa_ref[:, a : a + 1] * v_ref[...]
        tab_s[:, a * 128 : a * 128 + n] = tab[:, :n]
        t_ref[:, a * 128 : a * 128 + n] = tab[:, :n].astype(BF)

    m = m_ref[...]
    cosine = cos_ref[...]
    diagonal = diag_ref[...]

    def degree(l, carry):
        previous, earlier = carry
        deg = l.astype(F32)
        less = deg - 1.0
        upper = jnp.sqrt(jnp.maximum(4.0 * deg * deg - 1.0, 0.0) / jnp.maximum(deg * deg - m * m, 1.0))
        lower = jnp.sqrt(jnp.maximum(less * less - m * m, 0.0) / jnp.maximum(4.0 * less * less - 1.0, 1.0))
        value = upper * (cosine * previous - lower * earlier)
        current = jnp.where(m == deg, diagonal, jnp.where(m < deg, value, 0.0))
        leg_s[l] = current
        return current, previous

    zero = diagonal * 0.0

    wait_bytes(stat_s.at[pl.ds(0, 3)], qrsem)
    scale = lax.rsqrt((stat_s[0] + stat_s[1] + stat_s[2] + stat_s[3]) * (1.0 / 512.0) + EPS)
    freq = []
    for r in range(4):
        lhs = (tab_s[...] * scale[r : r + 1, :]).astype(BF)
        out = jnp.dot(lhs, f_ref[r], preferred_element_type=F32)
        freq.append((out * gw_ref[r : r + 1, :]).astype(BF))
    out = jnp.dot(sort_rows(), jnp.concatenate(freq, axis=0), preferred_element_type=F32)
    send_s[...] = out.astype(BF).reshape(64, 16, 128)
    loop(1, 64, lambda d: remote(send_s.at[(lat + d) % 64], modes_ref.at[lat], assem, arsem, ((lat + d) % 64, ch)))
    acopy = pltpu.make_async_copy(send_s.at[lat], modes_ref.at[lat], lsem.at[3])
    acopy.start()

    lax.fori_loop(0, DEG, degree, (zero, zero))
    kind = (lax.broadcasted_iota(jnp.int32, (DEG, 128), 1) % 16) // 4
    for c in range(8):
        part = leg_s[:, c, :]
        for k in range(3):
            e_ref[k * DEG : k * DEG + DEG, c * 128 : c * 128 + 128] = jnp.where(kind == k, part, 0.0).astype(BF)

    mcopy.wait()
    acopy.wait()
    pair = win_ref.at[pl.ds(pair0, 2), ch]

    @pl.when((me == 0) | (me == 15))
    def _():
        wait_bytes(win_ref.at[pl.ds(pair0, 2), ch, pl.ds(0, 13)], lsem.at[0])
        wait_bytes(win_ref.at[pl.ds(pair0, 2), ch, pl.ds(0, 1)], lsem.at[1])

    @pl.when((me != 0) & (me != 15))
    def _():
        wait_bytes(pair, lsem.at[0])

    wait_bytes(stat_s.at[pl.ds(0, 3)], qssem)
    wait_bytes(metas_ref.at[pl.ds(0, 6)], mssem)
    wait_bytes(metas_ref.at[pl.ds(0, 6)], mrsem)
    wait_bytes(modes_ref.at[pl.ds(0, 63)], assem)
    wait_bytes(modes_ref.at[pl.ds(0, 63)], arsem)
    most = win_ref.at[:, pl.ds(0, 3)]
    wait_bytes(most, ssem)
    wait_bytes(most, rsem)
    pl.when(up)(lambda: wait_bytes(win_ref.at[pl.ds(0, 4)], hssem.at[0]))
    pl.when(down)(lambda: wait_bytes(win_ref.at[pl.ds(0, 4)], hssem.at[1]))
    pl.when(has_prev)(lambda: wait_bytes(win_ref.at[0], hrsem.at[0]))
    pl.when(has_next)(lambda: wait_bytes(win_ref.at[0], hrsem.at[1]))


def gather(*args):
    shape = jax.ShapeDtypeStruct
    return pl.pallas_call(
        gather_kernel,
        out_shape=(
            shape((10, 4, 14, 16, 128), BF),
            shape((16, 24, 128), F32),
            shape((64, 16, 128), BF),
            shape((3 * DEG, 1024), BF),
            shape((2 * DEG, NLON), BF),
        ),
        in_specs=[VMEM] * 11,
        out_specs=[ANY, ANY, ANY, VMEM, VMEM],
        scratch_shapes=[
            pltpu.VMEM((2, OCT, 16, 128), BF),
            pltpu.VMEM((4, 4, NLON), F32),
            pltpu.VMEM((2 * DEG, NLON), F32),
            pltpu.VMEM((DEG, 8, 128), F32),
            pltpu.VMEM((64, 16, 128), BF),
            DMA((4,)), DMA, DMA, DMA((2,)), DMA((2,)), DMA, DMA, DMA, DMA, DMA, DMA,
        ],
        compiler_params=pltpu.CompilerParams(
            collective_id=0, has_side_effects=True, vmem_limit_bytes=40 * 1024 * 1024
        ),
        name="gather",
    )(*args)


def attend_kernel(
    x_ref, metas_ref, w_ref, got_ref, e_ref, mg_ref, ws_ref,
    out_ref, modes_ref,
    q_s, k_s, v_s, b_s, t_s, a_s, s_s, p_s, l_s, r_s, w_s, y_s, g_s, send_s,
    lsem, ssem, rsem, gssem, grsem, assem, arsem,
):
    lat, ch, group, zlo = place()
    me = zlo * 4 + ch
    loop(1, 64, lambda d: signal(((lat + d) % 64, ch)))
    loop(1, 16, lambda d: signal(ring_dev((me + d) % 16, group)))

    coef = jnp.dot(e_ref[...], got_ref[...].reshape(1024, 128), preferred_element_type=F32)
    coef = coef.reshape(3, DEG, 128) * mg_ref[...][None]
    g_s[ch] = coef.reshape(3 * DEG, 128).astype(BF)
    pl.semaphore_wait(pltpu.get_barrier_semaphore(), 78)
    for d in range(1, 4):
        remote(g_s.at[ch], g_s.at[ch], gssem, grsem, (lat, (ch + d) % 4))

    for t in range(4):
        for k in range(4):
            w_s[t, :, k * 128 : k * 128 + 128] = w_ref[k, t]

    lane = lax.broadcasted_iota(jnp.int32, (32, KEYS), 1)
    query = lax.broadcasted_iota(jnp.int32, (32, KEYS), 0)
    row_of = sum((lane >= KB * a).astype(jnp.int32) for a in range(1, 5))
    delta = lane - KB * row_of - query - 8
    dist = jnp.abs(delta).astype(F32)
    lane8 = lax.broadcasted_iota(jnp.int32, (8, KEYS), 1)
    row8 = sum((lane8 >= KB * a).astype(jnp.int32) for a in range(1, 5))
    spread = (row8 == lax.broadcasted_iota(jnp.int32, (8, KEYS), 0)).astype(F32)
    for h in range(8):
        mine = metas_ref[zlo * 4 + h // 2, (h % 2) * 8 : (h % 2) * 8 + 8, :]
        vec = lax.dot_general(mine, spread, TN, precision=lax.Precision.HIGHEST, preferred_element_type=F32)
        tile = jnp.full((32, KEYS), NEG, F32)
        for b in range(17):
            tile = jnp.where(delta == b - 8, vec[b : b + 1, :] * LOG2E, tile)
        b_s[h // 2, (h % 2) * 32 : (h % 2) * 32 + 32, :] = tile
    lane128 = lax.broadcasted_iota(jnp.int32, (128, KEYS), 1)
    row128 = sum((lane128 >= KB * a).astype(jnp.int32) for a in range(1, 5))
    pick = (row128 == lax.broadcasted_iota(jnp.int32, (128, KEYS), 0)).astype(F32)
    for z in range(4):
        reach = jnp.dot(metas_ref[z * 4 + ch, 16:24, :], pick, preferred_element_type=F32)
        r_s[z * 8 : z * 8 + 8, :] = reach

    def project(step):
        rows = pl.ds(step * 4, 4)
        parts = []
        for k in range(4):
            p = x_ref[pl.ds(step * 2, 2), k].astype(F32).reshape(2, 14, 2, 8, 128)
            p = jnp.stack([p[r // 2, :, r % 2].reshape(112, 128) for r in range(4)])
            parts.append(p.reshape(448, 128))
        square = jnp.sum(sum(p * p for p in parts), axis=1, keepdims=True)
        scale = lax.rsqrt(square * (1.0 / 512.0) + EPS)
        row = lax.broadcasted_iota(jnp.int32, (448, 1), 0)
        drop = ((step == 0) & (group == 0) & (row < 224)) | ((step == 4) & (group == 15) & (row >= 224))
        normed = jnp.concatenate(
            [
                jnp.where(drop, 0.0, p * scale * metas_ref[zlo * 4 + k, 20:21, :]).astype(BF)
                for k, p in enumerate(parts)
            ],
            axis=1,
        )
        for t, dst, lo, n in ((0, q_s, 8, 96), (1, k_s, 0, 112), (2, v_s, 0, 112)):
            out = jnp.dot(normed, w_s[t], preferred_element_type=F32).reshape(4, 112, 512)[:, lo : lo + n, :]
            if t == 0:
                out = out * (LOG2E / 8.0)
            dst[rows] = out.astype(BF)

    loop(0, 5, project)

    wait_bytes(g_s.at[pl.ds(0, 3)], grsem)
    gained = jnp.concatenate([g_s[k] for k in range(4)], axis=1)
    mixed = jnp.dot(gained, ws_ref[...].astype(BF), preferred_element_type=F32)
    parts = []
    for k in range(3):
        twice = jnp.where((lat + 64 * k) % DEG == 0, 1.0, 2.0).astype(F32)
        parts.append((mixed[k * DEG : k * DEG + DEG] * twice).astype(BF))
    rows_out = lax.dot_general(e_ref[...], jnp.concatenate(parts, axis=0), TN, preferred_element_type=F32)
    send_s[...] = rows_out.astype(BF).reshape(64, 16, 128)
    loop(1, 64, lambda d: remote(send_s.at[(lat + d) % 64], modes_ref.at[lat], assem, arsem, ((lat + d) % 64, ch)))
    acopy = pltpu.make_async_copy(send_s.at[lat], modes_ref.at[lat], lsem.at[0])
    acopy.start()

    left = lax.broadcasted_iota(jnp.int32, (32, 128), 1) < 64
    blocks = [(j, hp) for j in range(3) for hp in range(4)]
    lane1 = row_of[0:1, :]

    def attend_row(i):
        at = group * 16 + i - 2 + lane1
        inside = (at >= 0) & (at < NLAT)
        reach = jnp.where(inside, r_s[pl.ds((i // 4) * 8 + i % 4, 1), :], -1.0)
        allowed = dist <= reach
        for hp in range(4):
            t_s[hp, 0:32, :] = jnp.where(allowed, b_s[hp, 0:32, :], NEG)
            t_s[hp, 32:64, :] = jnp.where(allowed, b_s[hp, 32:64, :], NEG)
        for n, (j, hp) in enumerate(blocks):
            cols = slice(hp * 128, hp * 128 + 128)
            qb = q_s[i + 2, j * 32 : j * 32 + 32, cols]
            zero = jnp.zeros_like(qb)
            qq = jnp.concatenate([jnp.where(left, qb, zero), jnp.where(left, zero, qb)], axis=0)
            kb = k_s[pl.ds(i, 5), j * 32 : j * 32 + KB, cols].reshape(KEYS, 128)
            s_s[n] = lax.dot_general(qq, kb, NT, preferred_element_type=F32) + t_s[hp]
        for n in range(12):
            s = s_s[n]
            p = jnp.exp2(s - jnp.max(s, axis=1, keepdims=True))
            l_s[n] = jnp.broadcast_to(jnp.sum(p, axis=1, keepdims=True), (64, 128))
            p_s[n] = p.astype(BF)
        for n, (j, hp) in enumerate(blocks):
            cols = slice(hp * 128, hp * 128 + 128)
            vb = v_s[pl.ds(i, 5), j * 32 : j * 32 + KB, cols].reshape(KEYS, 128)
            o = jnp.dot(p_s[n], vb, preferred_element_type=F32) / l_s[n]
            a_s[i % 4, j * 32 : j * 32 + 32, cols] = jnp.where(left, o[:32], o[32:]).astype(BF)

    s = win_start(me)
    wide = win_start(me + 1) - s == 12

    def rows_of(step):
        rg = (zlo + step) % 4
        loop(0, 4, lambda r: attend_row(rg * 4 + r))
        out = jnp.dot(a_s[...].reshape(384, 512), w_s[3], preferred_element_type=F32).reshape(2, 2, 12, 8, 512)
        for k in range(4):
            for a in range(2):
                both = jnp.stack([out[a, b, :, :, k * 128 : k * 128 + 128] for b in range(2)], axis=1)
                y_s[rg * 2 + a, k] = both.reshape(12, 16, 128).astype(BF)

        def give(k, n, start):
            start(y_s.at[pl.ds(rg * 2, 2), k, pl.ds(0, n)], out_ref.at[:, pl.ds(s, n)])

        def both(k, start):
            pl.when(wide)(lambda: give(k, 12, start))
            pl.when(jnp.logical_not(wide))(lambda: give(k, 11, start))

        for d in range(1, 4):
            k = (ch + d) % 4
            both(k, lambda a, b, k=k: remote(a, b, ssem, rsem, (group * 4 + rg, k)))
        pl.when(step == 0)(lambda: both(ch, lambda a, b: pltpu.make_async_copy(a, b, lsem.at[1]).start()))
        pl.when(step > 0)(lambda: both(ch, lambda a, b: remote(a, b, ssem, rsem, (group * 4 + rg, ch))))

    loop(0, 4, rows_of)
    acopy.wait()
    wait_bytes(g_s.at[pl.ds(0, 3)], gssem)
    wait_bytes(modes_ref.at[pl.ds(0, 63)], assem)
    wait_bytes(modes_ref.at[pl.ds(0, 63)], arsem)

    def finish(n):
        wait_bytes(out_ref.at[:, pl.ds(0, n)], lsem.at[1])
        wait_bytes(out_ref.at[:, pl.ds(0, 15 * n)], ssem)
        wait_bytes(out_ref.at[:, pl.ds(0, OCT - n)], rsem)

    pl.when(wide)(lambda: finish(12))
    pl.when(jnp.logical_not(wide))(lambda: finish(11))


def attend(*args):
    shape = jax.ShapeDtypeStruct
    return pl.pallas_call(
        attend_kernel,
        out_shape=(shape((2, OCT, 16, 128), BF), shape((64, 16, 128), BF)),
        in_specs=[VMEM] * 7,
        out_specs=[ANY, ANY],
        scratch_shapes=[
            pltpu.VMEM((20, 96, 512), BF),
            pltpu.VMEM((20, 112, 512), BF),
            pltpu.VMEM((20, 112, 512), BF),
            pltpu.VMEM((4, 64, KEYS), F32),
            pltpu.VMEM((4, 64, KEYS), F32),
            pltpu.VMEM((4, 96, 512), BF),
            pltpu.VMEM((12, 64, KEYS), F32),
            pltpu.VMEM((12, 64, KEYS), BF),
            pltpu.VMEM((12, 64, 128), F32),
            pltpu.VMEM((32, KEYS), F32),
            pltpu.VMEM((4, 512, 512), BF),
            pltpu.VMEM((8, 4, 12, 16, 128), BF),
            pltpu.VMEM((4, 3 * DEG, 128), BF),
            pltpu.VMEM((64, 16, 128), BF),
            DMA((2,)), DMA, DMA, DMA, DMA, DMA, DMA,
        ],
        compiler_params=pltpu.CompilerParams(
            collective_id=1, has_side_effects=True, vmem_limit_bytes=48 * 1024 * 1024
        ),
        name="attend",
    )(*args)


def finish_kernel(local_ref, t_ref, got_ref, out_ref):
    modes = lax.dot_general(sort_rows(), got_ref[...].reshape(1024, 128), TN, preferred_element_type=F32).astype(BF)
    for r in range(4):
        wave = lax.dot_general(t_ref[...], modes[r * 192 : r * 192 + 192], TN, preferred_element_type=F32)
        local = local_ref[r // 2].astype(F32).reshape(OCT, 2, 8, 128)[:, r % 2].reshape(NLON, 128)
        out_ref[r] = (wave + local).astype(BF)


def finish(*args):
    return pl.pallas_call(
        finish_kernel,
        out_shape=jax.ShapeDtypeStruct((4, NLON, 128), BF),
        in_specs=[VMEM] * 3,
        out_specs=VMEM,
        compiler_params=pltpu.CompilerParams(vmem_limit_bytes=40 * 1024 * 1024),
        name="finish",
    )(*args)


def small_tables(lat):
    pair = jnp.arange(2 * DEG, dtype=jnp.int32)
    order = (pair % DEG)[:, None]

    def angle(cells):
        return (cells[None, :] * order % NLON).astype(F32) * (2.0 * math.pi / NLON)

    coarse = angle(jnp.arange(128, dtype=jnp.int32) * 128 % NLON)
    fine = angle(jnp.arange(128, dtype=jnp.int32))
    first = (pair < DEG)[:, None]
    cb, sb = jnp.cos(fine), jnp.sin(fine)
    u = jnp.where(first, cb, -sb)
    v = jnp.where(first, -sb, -cb)
    n = jnp.arange(1024, dtype=jnp.int32)
    row = (n // 16) * 4 + n % 4
    theta = (row.astype(F32) + 0.5) * (math.pi / NLAT)
    mine = (lat + 64 * jnp.arange(4, dtype=jnp.int32)) % DEG
    factors = jnp.arange(1, DEG, dtype=F32)
    log_ratio = jnp.log((2.0 * factors - 1.0) / (2.0 * factors))
    log_product = jnp.concatenate([jnp.zeros((1,), F32), jnp.cumsum(log_ratio)])
    orders = jnp.arange(DEG, dtype=F32)
    base = 0.5 * (jnp.log((2.0 * orders + 1.0) / (4.0 * math.pi)) + log_product)
    pick = mine[:, None] == jnp.arange(DEG, dtype=jnp.int32)[None, :]
    start = jnp.sum(jnp.where(pick, base[None, :], 0.0), axis=1)
    kind = (n % 16) // 4
    m = sum(jnp.where(kind == k, mine[k], 0) for k in range(4)).astype(F32)
    begin = sum(jnp.where(kind == k, start[k], 0.0) for k in range(4))
    diagonal = jnp.where(kind < 3, jnp.exp(begin + m * jnp.log(jnp.sin(theta))), 0.0)
    square = lambda a: a.reshape(8, 128)
    return jnp.cos(coarse), jnp.sin(coarse), u, v, square(m), square(diagonal), square(jnp.cos(theta))


def per_device(fields, norm_gain, w_qkv, w_out, rel_bias, stencil_reach, mode_gain, w_spec):
    lat = lax.axis_index("lat")
    weights = jnp.concatenate([jnp.moveaxis(w_qkv, 1, 0), w_out[None]], axis=0)
    weights = lax.all_gather(weights, "ch", axis=0, tiled=False)
    gain = norm_gain.astype(F32)
    bias = jnp.pad(rel_bias, ((0, 0), (0, 3), (0, 111))).reshape(16, 128)
    reach = jnp.pad(stencil_reach.astype(F32), ((0, 0), (0, 123)))
    meta = jnp.concatenate([bias, reach, gain[None], jnp.zeros((3, 128), F32)], axis=0)
    x = fields.astype(F32)
    squares = jnp.sum(x * x, axis=-1)
    colatitude = ((lat * 4 + jnp.arange(4, dtype=jnp.int32)).astype(F32) + 0.5) * (math.pi / NLAT)
    weight = jnp.sin(colatitude) * (math.pi / NLAT * 2.0 * math.pi / NLON)
    gain_weight = weight[:, None] * gain[None, :]
    window, metas, got, legendre, table = gather(fields, squares, meta, gain_weight, *small_tables(lat))
    local, modes = attend(window, metas, weights, got, legendre, mode_gain, w_spec)
    return finish(local, table, modes)


def solution(mesh):
    in_specs = (
        P("lat", None, "ch"),
        P("ch"),
        P(None, None, "ch"),
        P(None, "ch"),
        P("ch", None, None),
        P("lat", None),
        P(None, "ch"),
        P(None, "ch"),
    )
    return jax.shard_map(
        per_device, mesh=mesh, in_specs=in_specs, out_specs=P("lat", None, "ch"), check_vma=False
    )
```

```python
import math

import jax
import jax.numpy as jnp
from jax import lax
from jax.experimental import pallas as pl
from jax.experimental.pallas import tpu as pltpu
from jax.sharding import PartitionSpec as P

MESH = pl.DeviceIdType.MESH
NLON = 1440
NLAT = 256
DEG = 96
OCT = 180
LOG2E = 1.4426950408889634
NEG = -1e30
EPS = 1e-05
KB = 48
KEYS = 5 * KB
F32 = jnp.float32
BF = jnp.bfloat16
DMA = pltpu.SemaphoreType.DMA
VMEM = pl.BlockSpec(memory_space=pltpu.VMEM)
ANY = pl.BlockSpec(memory_space=pl.ANY)
TN = (((0,), (0,)), ((), ()))
NT = (((1,), (1,)), ((), ()))


def win_start(w):
    return 45 * w // 4


def ring_dev(w, group):
    return (group * 4 + w // 4, w % 4)


def place():
    lat = lax.axis_index("lat")
    ch = lax.axis_index("ch")
    return lat, ch, lat // 4, lat % 4


def signal(device):
    pl.semaphore_signal(pltpu.get_barrier_semaphore(), inc=1, device_id=device, device_id_type=MESH)


def remote(src, dst, ss, rs, device):
    pltpu.make_async_remote_copy(
        src_ref=src, dst_ref=dst, send_sem=ss, recv_sem=rs, device_id=device, device_id_type=MESH
    ).start()


def wait_bytes(ref, sem):
    pltpu.make_async_copy(ref, ref, sem).wait()


def loop(lo, hi, body):
    def step(i, c):
        body(i)
        return c

    lax.fori_loop(lo, hi, step, 0)


def sort_rows():
    n = lax.broadcasted_iota(jnp.int32, (1024, 1), 0)
    slot = n % 16
    source = jnp.where(slot < 12, (slot % 4) * 192 + (slot // 4) * 64 + n // 16, -1)
    return (lax.broadcasted_iota(jnp.int32, (1024, 768), 1) == source).astype(F32).astype(BF)


def tables(tab_s, t_ref):
    row = lax.broadcasted_iota(jnp.int32, (2 * DEG, 128), 0)
    lane = lax.broadcasted_iota(jnp.int32, (2 * DEG, 128), 1).astype(F32)
    first = row < DEG
    order = jnp.where(first, row, row - DEG).astype(F32)

    def angle(cells):
        turns = cells * order
        turns = turns - NLON * jnp.floor((turns + 0.5) * (1.0 / NLON))
        return turns * (2.0 * math.pi / NLON)

    coarse, fine = angle(jnp.where(lane < 12, lane * 128.0, 0.0)), angle(lane)
    ca, sa, cb, sb = jnp.cos(coarse), jnp.sin(coarse), jnp.cos(fine), jnp.sin(fine)
    u = jnp.where(first, cb, -sb)
    v = jnp.where(first, -sb, -cb)
    for a in range(12):
        n = min(128, NLON - a * 128)
        tab = ca[:, a : a + 1] * u + sa[:, a : a + 1] * v
        tab_s[:, a * 128 : a * 128 + n] = tab[:, :n]
        t_ref[:, a * 128 : a * 128 + n] = tab[:, :n].astype(BF)


def legendre(lat, leg_s, e_s):
    lane = lax.broadcasted_iota(jnp.int32, (8, 128), 1)
    n = lax.broadcasted_iota(jnp.int32, (8, 128), 0) * 128 + lane
    kind = (n % 16) // 4
    row = (n // 16) * 4 + n % 4
    theta = (row.astype(F32) + 0.5) * (math.pi / NLAT)
    factor = lax.broadcasted_iota(jnp.int32, (1, 128), 1)
    number = jnp.maximum(factor, 1).astype(F32)
    log_ratio = jnp.log((2.0 * number - 1.0) / (2.0 * number))
    m = jnp.zeros((8, 128), F32)
    begin = jnp.zeros((8, 128), F32)
    for k in range(3):
        order = (lat + 64 * k) % DEG
        total = jnp.sum(jnp.where((factor >= 1) & (factor <= order), log_ratio, 0.0), axis=1, keepdims=True)
        m = jnp.where(kind == k, order.astype(F32), m)
        begin = jnp.where(kind == k, total, begin)
    begin = 0.5 * (begin + jnp.log((2.0 * m + 1.0) / (4.0 * math.pi)))
    diagonal = jnp.where(kind < 3, jnp.exp(begin + m * jnp.log(jnp.sin(theta))), 0.0)
    cosine = jnp.cos(theta)

    def degree(l, carry):
        previous, earlier = carry
        deg = l.astype(F32)
        less = deg - 1.0
        upper = jnp.sqrt(jnp.maximum(4.0 * deg * deg - 1.0, 0.0) / jnp.maximum(deg * deg - m * m, 1.0))
        lower = jnp.sqrt(jnp.maximum(less * less - m * m, 0.0) / jnp.maximum(4.0 * less * less - 1.0, 1.0))
        value = upper * (cosine * previous - lower * earlier)
        current = jnp.where(m == deg, diagonal, jnp.where(m < deg, value, 0.0))
        leg_s[l] = current
        return current, previous

    zero = diagonal * 0.0
    lax.fori_loop(0, DEG, degree, (zero, zero))
    kind = (lax.broadcasted_iota(jnp.int32, (DEG, 128), 1) % 16) // 4
    for c in range(8):
        part = leg_s[:, c, :]
        for k in range(3):
            e_s[k * DEG : k * DEG + DEG, c * 128 : c * 128 + 128] = jnp.where(kind == k, part, 0.0).astype(BF)


def layer_kernel(
    f_ref, sq_ref, gain_ref, wq_ref, wo_ref, bias_ref, reach_ref, mg_ref, ws_ref,
    out_ref, modes_ref, t_ref,
    x_s, win_s, w_s, meta_s, metas_s, stat_s, tab_s, leg_s, e_s, send1_s, got_s, g_s, send2_s,
    q_s, k_s, v_s, b_s, t_s, a_s, s_s, p_s, l_s, r_s, y_s,
    lsem, statsem, metasem, w1sem, wbsem, w2sem, ssem, usem, nsem, hsem, a1sem, a2sem, gsem, bsem,
):
    lat, ch, group, zlo = place()
    me = zlo * 4 + ch
    has_next = group < 15
    has_prev = group > 0
    quarter = pl.ds(pl.multiple_of((group // 4) * 128, 128), 128)
    sib = ch + 1 - 2 * (ch % 2)
    across = (ch + 2) % 4
    loop(1, 64, lambda d: signal(((lat + d) % 64, ch)))
    for z in range(4):
        for d in range(1, 4):
            signal((group * 4 + z, (ch + d) % 4))
    for d in range(1, 4):
        signal(((lat + 16 * d) % 64, sib))

    stat_s[ch] = sq_ref[...]
    gain = gain_ref[...].astype(F32)
    meta_s[...] = jnp.zeros_like(meta_s)
    for a in range(5):
        for h in range(2):
            meta_s[h * 8 + a : h * 8 + a + 1, 0:17] = bias_ref[a, h : h + 1, :]
    meta_s[16:20, 0:5] = reach_ref[...].astype(F32)
    meta_s[20:21, :] = gain

    def interleave(c):
        lon = pl.ds(pl.multiple_of(c * 144, 16), 144)
        for a in range(2):
            two = [f_ref[2 * a + b, lon, :].astype(F32).reshape(18, 8, 128) for b in range(2)]
            x_s[a, pl.ds(c * 18, 18)] = jnp.stack(two, axis=1).reshape(18, 16, 128).astype(BF)

    loop(0, 10, interleave)

    @pl.when(jnp.logical_not(has_prev))
    def _():
        win_s[0] = jnp.zeros_like(win_s[0])

    @pl.when(jnp.logical_not(has_next))
    def _():
        win_s[9] = jnp.zeros_like(win_s[9])

    pl.semaphore_wait(pltpu.get_barrier_semaphore(), 78)

    for d in range(1, 4):
        remote(sq_ref, stat_s.at[ch], statsem.at[0], statsem.at[1], (lat, (ch + d) % 4))
    for d in range(1, 4):
        remote(meta_s, metas_s.at[me], metasem.at[0], metasem.at[1], (lat, (ch + d) % 4))
        remote(meta_s, metas_s.at[me], metasem.at[0], metasem.at[1], (group * 4 + (zlo + d) % 4, ch))
    remote(wq_ref.at[:, quarter], w_s.at[pl.ds(ch * 4, 3), quarter], w1sem.at[0], w1sem.at[1], (lat, across))
    remote(wo_ref.at[quarter], w_s.at[ch * 4 + 3, quarter], w1sem.at[0], w1sem.at[1], (lat, across))
    remote(wq_ref, w_s.at[pl.ds(ch * 4, 3)], wbsem.at[0], wbsem.at[1], (lat, sib))
    remote(wo_ref, w_s.at[ch * 4 + 3], wbsem.at[0], wbsem.at[1], (lat, sib))
    own = [
        pltpu.make_async_copy(meta_s, metas_s.at[me], lsem.at[2]),
        pltpu.make_async_copy(wq_ref, w_s.at[pl.ds(ch * 4, 3)], lsem.at[3]),
        pltpu.make_async_copy(wo_ref, w_s.at[ch * 4 + 3], lsem.at[4]),
    ]
    for copy in own:
        copy.start()

    def move(w, src_pair, pairs, dst_pair, start):
        s = win_start(w)
        src, dst = pl.ds(src_pair, pairs), pl.ds(dst_pair, pairs)
        edge = (w == 0) | (w == 15)

        @pl.when(edge)
        def _():
            a_src = jnp.where(w == 0, 0, s - 1)
            a_dst = jnp.where(w == 0, 1, 0)
            b_src = jnp.where(w == 0, OCT - 1, 0)
            b_dst = jnp.where(w == 0, 0, 13)
            start(x_s.at[src, pl.ds(a_src, 13)], win_s.at[dst, ch, pl.ds(a_dst, 13)], 0)
            start(x_s.at[src, pl.ds(b_src, 1)], win_s.at[dst, ch, pl.ds(b_dst, 1)], 1)

        @pl.when(jnp.logical_not(edge))
        def _():
            start(x_s.at[src, pl.ds(s - 1, 14)], win_s.at[dst, ch], 0)

    def spread(pair, ss, rs):
        def one(d):
            w = (me + d) % 16
            move(w, pair, 1, 1 + 2 * zlo + pair, lambda a, b, n: remote(a, b, ss, rs, ring_dev(w, group)))

        loop(1, 16, one)

    move(me, 0, 2, 1 + 2 * zlo, lambda a, b, n: pltpu.make_async_copy(a, b, lsem.at[n]).start())
    urgent = jnp.where(zlo == 3, 1, 0)
    spread(urgent, ssem.at[0], usem.at[jnp.where(zlo == 0, 1, jnp.where(zlo == 3, 2, 0))])

    tables(tab_s, t_ref)
    wait_bytes(stat_s.at[pl.ds(0, 3)], statsem.at[1])
    scale = lax.rsqrt((stat_s[0] + stat_s[1] + stat_s[2] + stat_s[3]) * (1.0 / 512.0) + EPS)
    theta = ((lat * 4 + lax.broadcasted_iota(jnp.int32, (4, 128), 0)).astype(F32) + 0.5) * (math.pi / NLAT)
    weight = jnp.sin(theta) * (math.pi / NLAT * 2.0 * math.pi / NLON) * gain
    freq = []
    for r in range(4):
        lhs = (tab_s[...] * scale[r : r + 1, :]).astype(BF)
        out = jnp.dot(lhs, f_ref[r], preferred_element_type=F32)
        freq.append((out * weight[r : r + 1, :]).astype(BF))
    out = jnp.dot(sort_rows(), jnp.concatenate(freq, axis=0), preferred_element_type=F32)
    send1_s[...] = out.astype(BF).reshape(64, 16, 128)
    loop(1, 64, lambda d: remote(send1_s.at[(lat + d) % 64], got_s.at[lat], a1sem.at[0], a1sem.at[1], ((lat + d) % 64, ch)))
    got_s[lat] = send1_s[lat]

    spread(1 - urgent, ssem.at[1], nsem)

    part = w_s.at[pl.ds(across * 4, 4), quarter]
    wait_bytes(part, w1sem.at[1])
    remote(part, part, w2sem.at[0], w2sem.at[1], (lat, sib))
    for d in range(1, 4):
        remote(part, part, w2sem.at[0], w2sem.at[1], ((lat + 16 * d) % 64, ch))
        remote(part, part, w2sem.at[0], w2sem.at[1], ((lat + 16 * d) % 64, sib))

    legendre(lat, leg_s, e_s)

    for copy in own:
        copy.wait()
    wait_bytes(metas_s.at[pl.ds(0, 6)], metasem.at[1])
    lane = lax.broadcasted_iota(jnp.int32, (32, KEYS), 1)
    query = lax.broadcasted_iota(jnp.int32, (32, KEYS), 0)
    row_of = sum((lane >= KB * a).astype(jnp.int32) for a in range(1, 5))
    delta = lane - KB * row_of - query - 8
    dist = jnp.abs(delta).astype(F32)
    lane8 = lax.broadcasted_iota(jnp.int32, (8, KEYS), 1)
    row8 = sum((lane8 >= KB * a).astype(jnp.int32) for a in range(1, 5))
    onto = (row8 == lax.broadcasted_iota(jnp.int32, (8, KEYS), 0)).astype(F32)
    for h in range(8):
        mine = metas_s[zlo * 4 + h // 2, (h % 2) * 8 : (h % 2) * 8 + 8, :]
        vec = lax.dot_general(mine, onto, TN, precision=lax.Precision.HIGHEST, preferred_element_type=F32)
        tile = jnp.full((32, KEYS), NEG, F32)
        for b in range(17):
            tile = jnp.where(delta == b - 8, vec[b : b + 1, :] * LOG2E, tile)
        b_s[h // 2, (h % 2) * 32 : (h % 2) * 32 + 32, :] = tile
    lane128 = lax.broadcasted_iota(jnp.int32, (128, KEYS), 1)
    row128 = sum((lane128 >= KB * a).astype(jnp.int32) for a in range(1, 5))
    pick = (row128 == lax.broadcasted_iota(jnp.int32, (128, KEYS), 0)).astype(F32)
    for z in range(4):
        r_s[z * 8 : z * 8 + 8, :] = jnp.dot(metas_s[z * 4 + ch, 16:24, :], pick, preferred_element_type=F32)

    @pl.when((me == 0) | (me == 15))
    def _():
        wait_bytes(win_s.at[pl.ds(0, 2), 0, pl.ds(0, 13)], lsem.at[0])
        wait_bytes(win_s.at[pl.ds(0, 2), 0, pl.ds(0, 1)], lsem.at[1])

    @pl.when((me != 0) & (me != 15))
    def _():
        wait_bytes(win_s.at[pl.ds(0, 2), 0], lsem.at[0])

    def arrived(own_here, full, sem):
        pl.when(own_here)(lambda: wait_bytes(win_s.at[pl.ds(0, full - 1), 0], sem))
        pl.when(jnp.logical_not(own_here))(lambda: wait_bytes(win_s.at[pl.ds(0, full), 0], sem))

    arrived(zlo == 0, 4, usem.at[1])
    arrived(zlo == 3, 4, usem.at[2])
    pl.when(has_next)(lambda: remote(win_s.at[8], win_s.at[0], hsem.at[0], hsem.at[1], ((lat + 4) % 64, ch)))
    pl.when(has_prev)(lambda: remote(win_s.at[1], win_s.at[9], hsem.at[2], hsem.at[3], ((lat + 60) % 64, ch)))

    wait_bytes(got_s.at[pl.ds(0, 63)], a1sem.at[1])
    coef = jnp.dot(e_s[...], got_s[...].reshape(1024, 128), preferred_element_type=F32)
    coef = coef.reshape(3, DEG, 128) * mg_ref[...][None]
    g_s[ch] = coef.reshape(3 * DEG, 128).astype(BF)
    for d in range(1, 4):
        remote(g_s.at[ch], g_s.at[ch], gsem.at[0], gsem.at[1], (lat, (ch + d) % 4))

    def weights(t):
        return jnp.concatenate([w_s[k * 4 + t] for k in range(4)], axis=1)

    def project(pair, inner):
        parts = []
        for k in range(4):
            p = win_s[pair, k].astype(F32).reshape(14, 2, 8, 128)
            parts.append(jnp.concatenate([p[:, r].reshape(112, 128) for r in range(2)], axis=0))
        square = jnp.sum(sum(p * p for p in parts), axis=1, keepdims=True)
        scale = lax.rsqrt(square * (1.0 / 512.0) + EPS)
        normed = jnp.concatenate(
            [(p * scale * metas_s[zlo * 4 + k, 20:21, :]).astype(BF) for k, p in enumerate(parts)], axis=1
        )
        rows = pl.ds(pair * 2, 2)
        for t, dst, lo, n in ((0, q_s, 8, 96), (1, k_s, 0, 112), (2, v_s, 0, 112)):
            if t == 0 and not inner:
                continue
            out = jnp.dot(normed, weights(t), preferred_element_type=F32).reshape(2, 112, 512)[:, lo : lo + n, :]
            if t == 0:
                out = out * (LOG2E / 8.0)
            dst[rows] = out.astype(BF)

    wait_bytes(w_s.at[pl.ds(0, 4)], wbsem.at[1])
    wait_bytes(w_s.at[pl.ds(0, 7)], w2sem.at[1])
    arrived((zlo == 1) | (zlo == 2), 8, usem.at[0])
    loop(0, 4, lambda i: project(1 + 2 * i + i // 3, True))

    wait_bytes(g_s.at[pl.ds(0, 3)], gsem.at[1])
    gained = jnp.concatenate([g_s[k] for k in range(4)], axis=1)
    mixed = jnp.dot(gained, ws_ref[...].astype(BF), preferred_element_type=F32)
    parts = []
    for k in range(3):
        twice = jnp.where((lat + 64 * k) % DEG == 0, 1.0, 2.0).astype(F32)
        parts.append((mixed[k * DEG : k * DEG + DEG] * twice).astype(BF))
    rows_out = lax.dot_general(e_s[...], jnp.concatenate(parts, axis=0), TN, preferred_element_type=F32)
    send2_s[...] = rows_out.astype(BF).reshape(64, 16, 128)
    loop(1, 64, lambda d: remote(send2_s.at[(lat + d) % 64], modes_ref.at[lat], a2sem.at[0], a2sem.at[1], ((lat + d) % 64, ch)))
    acopy = pltpu.make_async_copy(send2_s.at[lat], modes_ref.at[lat], lsem.at[5])
    acopy.start()

    wait_bytes(win_s.at[pl.ds(0, 5), pl.ds(0, 3)], nsem)
    loop(0, 4, lambda i: project(2 + 2 * i - i // 3, True))
    pl.when(has_prev)(lambda: wait_bytes(win_s.at[0], hsem.at[1]))
    project(0, False)
    pl.when(has_next)(lambda: wait_bytes(win_s.at[0], hsem.at[3]))
    project(9, False)

    left = lax.broadcasted_iota(jnp.int32, (32, 128), 1) < 64
    blocks = [(j, hp) for j in range(3) for hp in range(4)]
    lane1 = row_of[0:1, :]

    def attend_row(i):
        at = group * 16 + i - 2 + lane1
        inside = (at >= 0) & (at < NLAT)
        reach = jnp.where(inside, r_s[pl.ds((i // 4) * 8 + i % 4, 1), :], -1.0)
        allowed = dist <= reach
        for hp in range(4):
            t_s[hp, 0:32, :] = jnp.where(allowed, b_s[hp, 0:32, :], NEG)
            t_s[hp, 32:64, :] = jnp.where(allowed, b_s[hp, 32:64, :], NEG)
        for n, (j, hp) in enumerate(blocks):
            cols = slice(hp * 128, hp * 128 + 128)
            qb = q_s[i + 2, j * 32 : j * 32 + 32, cols]
            zero = jnp.zeros_like(qb)
            qq = jnp.concatenate([jnp.where(left, qb, zero), jnp.where(left, zero, qb)], axis=0)
            kb = k_s[pl.ds(i, 5), j * 32 : j * 32 + KB, cols].reshape(KEYS, 128)
            s_s[n] = lax.dot_general(qq, kb, NT, preferred_element_type=F32) + t_s[hp]
        for n in range(12):
            s = s_s[n]
            p = jnp.exp2(s - jnp.max(s, axis=1, keepdims=True))
            l_s[n] = jnp.broadcast_to(jnp.sum(p, axis=1, keepdims=True), (64, 128))
            p_s[n] = p.astype(BF)
        for n, (j, hp) in enumerate(blocks):
            cols = slice(hp * 128, hp * 128 + 128)
            vb = v_s[pl.ds(i, 5), j * 32 : j * 32 + KB, cols].reshape(KEYS, 128)
            o = jnp.dot(p_s[n], vb, preferred_element_type=F32) / l_s[n]
            a_s[i % 4, j * 32 : j * 32 + 32, cols] = jnp.where(left, o[:32], o[32:]).astype(BF)

    s = win_start(me)
    wide = win_start(me + 1) - s == 12

    def rows_of(step):
        rg = (zlo + step) % 4
        loop(0, 4, lambda r: attend_row(rg * 4 + r))
        out = jnp.dot(a_s[...].reshape(384, 512), weights(3), preferred_element_type=F32).reshape(2, 2, 12, 8, 512)
        for k in range(4):
            for a in range(2):
                both = jnp.stack([out[a, b, :, :, k * 128 : k * 128 + 128] for b in range(2)], axis=1)
                y_s[rg * 2 + a, k] = both.reshape(12, 16, 128).astype(BF)

        def give(k, n, start):
            start(y_s.at[pl.ds(rg * 2, 2), k, pl.ds(0, n)], out_ref.at[:, pl.ds(s, n)])

        def both(k, start):
            pl.when(wide)(lambda: give(k, 12, start))
            pl.when(jnp.logical_not(wide))(lambda: give(k, 11, start))

        for d in range(1, 4):
            k = (ch + d) % 4
            both(k, lambda a, b, k=k: remote(a, b, bsem.at[0], bsem.at[1], (group * 4 + rg, k)))
        pl.when(step == 0)(lambda: both(ch, lambda a, b: pltpu.make_async_copy(a, b, lsem.at[6]).start()))
        pl.when(step > 0)(
            lambda: both(ch, lambda a, b: remote(a, b, bsem.at[0], bsem.at[1], (group * 4 + rg, ch)))
        )

    loop(0, 4, rows_of)

    wait_bytes(stat_s.at[pl.ds(0, 3)], statsem.at[0])
    wait_bytes(metas_s.at[pl.ds(0, 6)], metasem.at[0])
    wait_bytes(part, w1sem.at[0])
    wait_bytes(w_s.at[pl.ds(0, 4)], wbsem.at[0])
    wait_bytes(w_s.at[pl.ds(0, 7)], w2sem.at[0])
    wait_bytes(win_s.at[pl.ds(0, 5), pl.ds(0, 3)], ssem.at[0])
    wait_bytes(win_s.at[pl.ds(0, 5), pl.ds(0, 3)], ssem.at[1])
    pl.when(has_next)(lambda: wait_bytes(win_s.at[0], hsem.at[0]))
    pl.when(has_prev)(lambda: wait_bytes(win_s.at[0], hsem.at[2]))
    wait_bytes(got_s.at[pl.ds(0, 63)], a1sem.at[0])
    wait_bytes(g_s.at[pl.ds(0, 3)], gsem.at[0])
    acopy.wait()
    wait_bytes(modes_ref.at[pl.ds(0, 63)], a2sem.at[0])
    wait_bytes(modes_ref.at[pl.ds(0, 63)], a2sem.at[1])

    def last(n):
        wait_bytes(out_ref.at[:, pl.ds(0, n)], lsem.at[6])
        wait_bytes(out_ref.at[:, pl.ds(0, 15 * n)], bsem.at[0])
        wait_bytes(out_ref.at[:, pl.ds(0, OCT - n)], bsem.at[1])

    pl.when(wide)(lambda: last(12))
    pl.when(jnp.logical_not(wide))(lambda: last(11))


def layer(*args):
    shape = jax.ShapeDtypeStruct
    vm = pltpu.VMEM
    return pl.pallas_call(
        layer_kernel,
        out_shape=(shape((2, OCT, 16, 128), BF), shape((64, 16, 128), BF), shape((2 * DEG, NLON), BF)),
        in_specs=[VMEM] * 9,
        out_specs=[ANY, ANY, VMEM],
        scratch_shapes=[
            vm((2, OCT, 16, 128), BF),
            vm((10, 4, 14, 16, 128), BF),
            vm((16, 512, 128), BF),
            vm((24, 128), F32),
            vm((16, 24, 128), F32),
            vm((4, 4, NLON), F32),
            vm((2 * DEG, NLON), F32),
            vm((DEG, 8, 128), F32),
            vm((3 * DEG, 1024), BF),
            vm((64, 16, 128), BF),
            vm((64, 16, 128), BF),
            vm((4, 3 * DEG, 128), BF),
            vm((64, 16, 128), BF),
            vm((20, 96, 512), BF),
            vm((20, 112, 512), BF),
            vm((20, 112, 512), BF),
            vm((4, 64, KEYS), F32),
            vm((4, 64, KEYS), F32),
            vm((4, 96, 512), BF),
            vm((12, 64, KEYS), F32),
            vm((12, 64, KEYS), BF),
            vm((12, 64, 128), F32),
            vm((32, KEYS), F32),
            vm((8, 4, 12, 16, 128), BF),
            DMA((7,)), DMA((2,)), DMA((2,)), DMA((2,)), DMA((2,)), DMA((2,)), DMA((2,)), DMA((3,)), DMA,
            DMA((4,)), DMA((2,)), DMA((2,)), DMA((2,)), DMA((2,)),
        ],
        compiler_params=pltpu.CompilerParams(
            collective_id=0, has_side_effects=True, vmem_limit_bytes=56 * 1024 * 1024
        ),
        name="layer",
    )(*args)


def finish_kernel(local_ref, t_ref, got_ref, out_ref):
    modes = lax.dot_general(sort_rows(), got_ref[...].reshape(1024, 128), TN, preferred_element_type=F32).astype(BF)
    for r in range(4):
        wave = lax.dot_general(t_ref[...], modes[r * 192 : r * 192 + 192], TN, preferred_element_type=F32)
        local = local_ref[r // 2].astype(F32).reshape(OCT, 2, 8, 128)[:, r % 2].reshape(NLON, 128)
        out_ref[r] = (wave + local).astype(BF)


def finish(*args):
    return pl.pallas_call(
        finish_kernel,
        out_shape=jax.ShapeDtypeStruct((4, NLON, 128), BF),
        in_specs=[VMEM] * 3,
        out_specs=VMEM,
        compiler_params=pltpu.CompilerParams(vmem_limit_bytes=40 * 1024 * 1024),
        name="finish",
    )(*args)


def per_device(fields, norm_gain, w_qkv, w_out, rel_bias, stencil_reach, mode_gain, w_spec):
    x = fields.astype(F32)
    squares = jnp.sum(x * x, axis=-1)
    local, modes, table = layer(
        fields,
        squares,
        norm_gain.reshape(1, 128),
        jnp.transpose(w_qkv, (1, 0, 2)),
        w_out,
        jnp.transpose(rel_bias, (1, 0, 2)),
        stencil_reach,
        mode_gain,
        w_spec,
    )
    return finish(local, table, modes)


def solution(mesh):
    in_specs = (
        P("lat", None, "ch"),
        P("ch"),
        P(None, None, "ch"),
        P(None, "ch"),
        P("ch", None, None),
        P("lat", None),
        P(None, "ch"),
        P(None, "ch"),
    )
    return jax.shard_map(
        per_device, mesh=mesh, in_specs=in_specs, out_specs=P("lat", None, "ch"), check_vma=False
    )
```

```python
import math

import jax
import jax.numpy as jnp
from jax import lax
from jax.experimental import pallas as pl
from jax.experimental.pallas import tpu as pltpu
from jax.sharding import PartitionSpec as P

MESH = pl.DeviceIdType.MESH
NLON = 1440
NLAT = 256
DEG = 96
OCT = 180
LOG2E = 1.4426950408889634
NEG = -1e30
EPS = 1e-05
KB = 48
KEYS = 5 * KB
F32 = jnp.float32
BF = jnp.bfloat16
DMA = pltpu.SemaphoreType.DMA
VMEM = pl.BlockSpec(memory_space=pltpu.VMEM)
TN = (((0,), (0,)), ((), ()))
NT = (((1,), (1,)), ((), ()))


def win_start(w):
    return 45 * w // 4


def ring_dev(w, group):
    return (group * 4 + w // 4, w % 4)


def place():
    lat = lax.axis_index("lat")
    ch = lax.axis_index("ch")
    return lat, ch, lat // 4, lat % 4


def signal(device):
    pl.semaphore_signal(pltpu.get_barrier_semaphore(), inc=1, device_id=device, device_id_type=MESH)


def remote(src, dst, ss, rs, device):
    pltpu.make_async_remote_copy(
        src_ref=src, dst_ref=dst, send_sem=ss, recv_sem=rs, device_id=device, device_id_type=MESH
    ).start()


def wait_bytes(ref, sem):
    pltpu.make_async_copy(ref, ref, sem).wait()


def loop(lo, hi, body):
    def step(i, c):
        body(i)
        return c

    lax.fori_loop(lo, hi, step, 0)


def sort_rows():
    n = lax.broadcasted_iota(jnp.int32, (1024, 1), 0)
    slot = n % 16
    source = jnp.where(slot < 12, (slot % 4) * 192 + (slot // 4) * 64 + n // 16, -1)
    return (lax.broadcasted_iota(jnp.int32, (1024, 768), 1) == source).astype(F32).astype(BF)


def tables(tab_s, t_ref):
    row = lax.broadcasted_iota(jnp.int32, (2 * DEG, 128), 0)
    lane = lax.broadcasted_iota(jnp.int32, (2 * DEG, 128), 1).astype(F32)
    first = row < DEG
    order = jnp.where(first, row, row - DEG).astype(F32)

    def angle(cells):
        turns = cells * order
        turns = turns - NLON * jnp.floor((turns + 0.5) * (1.0 / NLON))
        return turns * (2.0 * math.pi / NLON)

    coarse, fine = angle(jnp.where(lane < 12, lane * 128.0, 0.0)), angle(lane)
    ca, sa, cb, sb = jnp.cos(coarse), jnp.sin(coarse), jnp.cos(fine), jnp.sin(fine)
    u = jnp.where(first, cb, -sb)
    v = jnp.where(first, -sb, -cb)
    for a in range(12):
        n = min(128, NLON - a * 128)
        tab = ca[:, a : a + 1] * u + sa[:, a : a + 1] * v
        tab_s[:, a * 128 : a * 128 + n] = tab[:, :n]
        t_ref[:, a * 128 : a * 128 + n] = tab[:, :n].astype(BF)


def legendre(lat, leg_s, e_s):
    lane = lax.broadcasted_iota(jnp.int32, (8, 128), 1)
    n = lax.broadcasted_iota(jnp.int32, (8, 128), 0) * 128 + lane
    kind = (n % 16) // 4
    row = (n // 16) * 4 + n % 4
    theta = (row.astype(F32) + 0.5) * (math.pi / NLAT)
    factor = lax.broadcasted_iota(jnp.int32, (1, 128), 1)
    number = jnp.maximum(factor, 1).astype(F32)
    log_ratio = jnp.log((2.0 * number - 1.0) / (2.0 * number))
    m = jnp.zeros((8, 128), F32)
    begin = jnp.zeros((8, 128), F32)
    for k in range(3):
        order = (lat + 64 * k) % DEG
        total = jnp.sum(jnp.where((factor >= 1) & (factor <= order), log_ratio, 0.0), axis=1, keepdims=True)
        m = jnp.where(kind == k, order.astype(F32), m)
        begin = jnp.where(kind == k, total, begin)
    begin = 0.5 * (begin + jnp.log((2.0 * m + 1.0) / (4.0 * math.pi)))
    diagonal = jnp.where(kind < 3, jnp.exp(begin + m * jnp.log(jnp.sin(theta))), 0.0)
    cosine = jnp.cos(theta)

    def degree(l, carry):
        previous, earlier = carry
        deg = l.astype(F32)
        less = deg - 1.0
        upper = jnp.sqrt(jnp.maximum(4.0 * deg * deg - 1.0, 0.0) / jnp.maximum(deg * deg - m * m, 1.0))
        lower = jnp.sqrt(jnp.maximum(less * less - m * m, 0.0) / jnp.maximum(4.0 * less * less - 1.0, 1.0))
        value = upper * (cosine * previous - lower * earlier)
        current = jnp.where(m == deg, diagonal, jnp.where(m < deg, value, 0.0))
        leg_s[l] = current
        return current, previous

    zero = diagonal * 0.0
    lax.fori_loop(0, DEG, degree, (zero, zero))
    kind = (lax.broadcasted_iota(jnp.int32, (DEG, 128), 1) % 16) // 4
    for c in range(8):
        part = leg_s[:, c, :]
        for k in range(3):
            e_s[k * DEG : k * DEG + DEG, c * 128 : c * 128 + 128] = jnp.where(kind == k, part, 0.0).astype(BF)


def layer_kernel(
    f_ref, gain_ref, wq_ref, wo_ref, bias_ref, reach_ref, mg_ref, ws_ref,
    out_ref,
    x_s, win_s, w_s, meta_s, metas_s, stat_s, tab_s, leg_s, e_s, send1_s, got_s, g_s, send2_s,
    q_s, k_s, v_s, b_s, t_s, a_s, s_s, p_s, l_s, r_s, y_s, got2_s, local_s, t16_s, wave_s,
    lsem, statsem, metasem, w1sem, wxsem, wbsem, w2sem, ssem, usem, nsem, hsem, a1sem, a2sem, gsem, bsem,
):
    lat, ch, group, zlo = place()
    me = zlo * 4 + ch
    has_next = group < 15
    has_prev = group > 0
    quarter = pl.ds(pl.multiple_of((group // 4) * 128, 128), 128)
    sixteenth = pl.ds(pl.multiple_of(group * 32, 32), 32)
    sib = ch + 1 - 2 * (ch % 2)
    across = (ch + 2) % 4
    loop(1, 64, lambda d: signal(((lat + d) % 64, ch)))
    for z in range(4):
        for d in range(1, 4):
            signal((group * 4 + z, (ch + d) % 4))
    for d in range(1, 4):
        signal(((lat + 16 * d) % 64, sib))

    ones = jnp.ones((8, 256), BF)
    for r in range(4):
        x = f_ref[r].astype(F32)
        x = x * x
        high = x.astype(BF)
        both = jnp.concatenate([high, (x - high.astype(F32)).astype(BF)], axis=1)
        sums = lax.dot_general(ones, both, NT, preferred_element_type=F32)
        stat_s[ch, r : r + 1, :] = sums[0:1]
    gain = gain_ref[...].astype(F32)
    meta_s[...] = jnp.zeros_like(meta_s)
    for a in range(5):
        for h in range(2):
            meta_s[h * 8 + a : h * 8 + a + 1, 0:17] = bias_ref[a, h : h + 1, :]
    meta_s[16:20, 0:5] = reach_ref[...].astype(F32)
    meta_s[20:21, :] = gain

    def interleave(c):
        lon = pl.ds(pl.multiple_of(c * 144, 16), 144)
        for a in range(2):
            two = [f_ref[2 * a + b, lon, :].astype(F32).reshape(18, 8, 128) for b in range(2)]
            x_s[a, pl.ds(c * 18, 18)] = jnp.stack(two, axis=1).reshape(18, 16, 128).astype(BF)

    loop(0, 10, interleave)

    @pl.when(jnp.logical_not(has_prev))
    def _():
        win_s[0] = jnp.zeros_like(win_s[0])

    @pl.when(jnp.logical_not(has_next))
    def _():
        win_s[9] = jnp.zeros_like(win_s[9])

    pl.semaphore_wait(pltpu.get_barrier_semaphore(), 78)

    for d in range(1, 4):
        remote(stat_s.at[ch], stat_s.at[ch], statsem.at[0], statsem.at[1], (lat, (ch + d) % 4))
    for d in range(1, 4):
        remote(meta_s, metas_s.at[me], metasem.at[0], metasem.at[1], (lat, (ch + d) % 4))
        remote(meta_s, metas_s.at[me], metasem.at[0], metasem.at[1], (group * 4 + (zlo + d) % 4, ch))
    remote(wq_ref.at[:, sixteenth], w_s.at[pl.ds(ch * 4, 3), sixteenth], w1sem.at[0], w1sem.at[1], (lat, across))
    remote(wo_ref.at[sixteenth], w_s.at[ch * 4 + 3, sixteenth], w1sem.at[0], w1sem.at[1], (lat, across))
    remote(wq_ref, w_s.at[pl.ds(ch * 4, 3)], wbsem.at[0], wbsem.at[1], (lat, sib))
    remote(wo_ref, w_s.at[ch * 4 + 3], wbsem.at[0], wbsem.at[1], (lat, sib))
    own = [
        pltpu.make_async_copy(meta_s, metas_s.at[me], lsem.at[2]),
        pltpu.make_async_copy(wq_ref, w_s.at[pl.ds(ch * 4, 3)], lsem.at[3]),
        pltpu.make_async_copy(wo_ref, w_s.at[ch * 4 + 3], lsem.at[4]),
    ]
    for copy in own:
        copy.start()

    def move(w, src_pair, pairs, dst_pair, start):
        s = win_start(w)
        src, dst = pl.ds(src_pair, pairs), pl.ds(dst_pair, pairs)
        edge = (w == 0) | (w == 15)

        @pl.when(edge)
        def _():
            a_src = jnp.where(w == 0, 0, s - 1)
            a_dst = jnp.where(w == 0, 1, 0)
            b_src = jnp.where(w == 0, OCT - 1, 0)
            b_dst = jnp.where(w == 0, 0, 13)
            start(x_s.at[src, pl.ds(a_src, 13)], win_s.at[dst, ch, pl.ds(a_dst, 13)], 0)
            start(x_s.at[src, pl.ds(b_src, 1)], win_s.at[dst, ch, pl.ds(b_dst, 1)], 1)

        @pl.when(jnp.logical_not(edge))
        def _():
            start(x_s.at[src, pl.ds(s - 1, 14)], win_s.at[dst, ch], 0)

    def to(pair, ss, rs, dz, dc):
        z = ((ch // 2) * 4 + zlo + dz) % 8
        w = (z % 4) * 4 + (z // 4) * 2 + (ch + dc) % 2
        move(w, pair, 1, 1 + 2 * zlo + pair, lambda a, b, n: remote(a, b, ss, rs, ring_dev(w, group)))

    def near(pair, ss, rs):
        def one(t):
            u = t // 2
            dz = jnp.where(u == 4, 0, jnp.where(u % 2 == 0, u // 2 + 1, 7 - u // 2))
            to(pair, ss, rs, dz, jnp.where(t == 8, 1, t % 2))

        loop(0, 9, one)

    def far(pair, ss, rs):
        def one(t):
            u = t // 2
            to(pair, ss, rs, jnp.where(u == 0, 3, jnp.where(u == 1, 5, 4)), t % 2)

        loop(0, 6, one)

    move(me, 0, 2, 1 + 2 * zlo, lambda a, b, n: pltpu.make_async_copy(a, b, lsem.at[n]).start())
    urgent = jnp.where(zlo == 3, 1, 0)
    first = (urgent, ssem.at[0], usem.at[jnp.where(zlo == 0, 1, jnp.where(zlo == 3, 2, 0))])
    second = (1 - urgent, ssem.at[1], nsem)
    near(*first)
    far(*first)

    tables(tab_s, t16_s)
    wait_bytes(stat_s.at[pl.ds(0, 3)], statsem.at[1])
    scale = lax.rsqrt((stat_s[0] + stat_s[1] + stat_s[2] + stat_s[3]) * (1.0 / 512.0) + EPS)
    theta = ((lat * 4 + lax.broadcasted_iota(jnp.int32, (4, 128), 0)).astype(F32) + 0.5) * (math.pi / NLAT)
    weight = jnp.sin(theta) * (math.pi / NLAT * 2.0 * math.pi / NLON) * gain
    freq = []
    for r in range(4):
        lhs = (tab_s[...] * scale[r : r + 1, :]).astype(BF)
        out = jnp.dot(lhs, f_ref[r], preferred_element_type=F32)
        freq.append((out * weight[r : r + 1, :]).astype(BF))
    out = jnp.dot(sort_rows(), jnp.concatenate(freq, axis=0), preferred_element_type=F32)
    send1_s[...] = out.astype(BF).reshape(64, 16, 128)
    loop(1, 64, lambda d: remote(send1_s.at[(lat + d) % 64], got_s.at[lat], a1sem.at[0], a1sem.at[1], ((lat + d) % 64, ch)))
    got_s[lat] = send1_s[lat]

    near(*second)

    wait_bytes(w_s.at[pl.ds(across * 4, 4), sixteenth], w1sem.at[1])
    strip = w_s.at[pl.ds(across * 4, 4), sixteenth]
    for d in range(1, 4):
        remote(strip, strip, wxsem.at[0], wxsem.at[1], (lat - group % 4 * 4 + (group + d) % 4 * 4, ch))
    legendre(lat, leg_s, e_s)
    part = w_s.at[pl.ds(across * 4, 4), quarter]
    wait_bytes(w_s.at[pl.ds(0, 3), pl.ds(0, 128)], wxsem.at[1])
    remote(part, part, w2sem.at[0], w2sem.at[1], (lat, sib))
    for d in range(1, 4):
        remote(part, part, w2sem.at[0], w2sem.at[1], ((lat + 16 * d) % 64, ch))
        remote(part, part, w2sem.at[0], w2sem.at[1], ((lat + 16 * d) % 64, sib))

    @pl.when((me == 0) | (me == 15))
    def _():
        wait_bytes(win_s.at[pl.ds(0, 2), 0, pl.ds(0, 13)], lsem.at[0])
        wait_bytes(win_s.at[pl.ds(0, 2), 0, pl.ds(0, 1)], lsem.at[1])

    @pl.when((me != 0) & (me != 15))
    def _():
        wait_bytes(win_s.at[pl.ds(0, 2), 0], lsem.at[0])

    def arrived(own_here, full, sem):
        pl.when(own_here)(lambda: wait_bytes(win_s.at[pl.ds(0, full - 1), 0], sem))
        pl.when(jnp.logical_not(own_here))(lambda: wait_bytes(win_s.at[pl.ds(0, full), 0], sem))

    arrived(zlo == 0, 4, usem.at[1])
    arrived(zlo == 3, 4, usem.at[2])
    pl.when(has_next)(lambda: remote(win_s.at[8], win_s.at[0], hsem.at[0], hsem.at[1], ((lat + 4) % 64, ch)))
    pl.when(has_prev)(lambda: remote(win_s.at[1], win_s.at[9], hsem.at[2], hsem.at[3], ((lat + 60) % 64, ch)))

    far(*second)


    for copy in own:
        copy.wait()
    wait_bytes(metas_s.at[pl.ds(0, 6)], metasem.at[1])
    lane = lax.broadcasted_iota(jnp.int32, (32, KEYS), 1)
    query = lax.broadcasted_iota(jnp.int32, (32, KEYS), 0)
    row_of = sum((lane >= KB * a).astype(jnp.int32) for a in range(1, 5))
    delta = lane - KB * row_of - query - 8
    dist = jnp.abs(delta).astype(F32)
    lane8 = lax.broadcasted_iota(jnp.int32, (8, KEYS), 1)
    row8 = sum((lane8 >= KB * a).astype(jnp.int32) for a in range(1, 5))
    onto = (row8 == lax.broadcasted_iota(jnp.int32, (8, KEYS), 0)).astype(F32)
    for h in range(8):
        mine = metas_s[zlo * 4 + h // 2, (h % 2) * 8 : (h % 2) * 8 + 8, :]
        vec = lax.dot_general(mine, onto, TN, precision=lax.Precision.HIGHEST, preferred_element_type=F32)
        tile = jnp.full((32, KEYS), NEG, F32)
        for b in range(17):
            tile = jnp.where(delta == b - 8, vec[b : b + 1, :] * LOG2E, tile)
        b_s[h // 2, (h % 2) * 32 : (h % 2) * 32 + 32, :] = tile
    lane128 = lax.broadcasted_iota(jnp.int32, (128, KEYS), 1)
    row128 = sum((lane128 >= KB * a).astype(jnp.int32) for a in range(1, 5))
    pick = (row128 == lax.broadcasted_iota(jnp.int32, (128, KEYS), 0)).astype(F32)
    for z in range(4):
        r_s[z * 8 : z * 8 + 8, :] = jnp.dot(metas_s[z * 4 + ch, 16:24, :], pick, preferred_element_type=F32)

    def weights(t):
        return jnp.concatenate([w_s[k * 4 + t] for k in range(4)], axis=1)

    def project(pair, inner):
        parts = []
        for k in range(4):
            p = win_s[pair, k].astype(F32).reshape(14, 2, 8, 128)
            parts.append(jnp.concatenate([p[:, r].reshape(112, 128) for r in range(2)], axis=0))
        square = jnp.sum(sum(p * p for p in parts), axis=1, keepdims=True)
        scale = lax.rsqrt(square * (1.0 / 512.0) + EPS)
        normed = jnp.concatenate(
            [(p * scale * metas_s[zlo * 4 + k, 20:21, :]).astype(BF) for k, p in enumerate(parts)], axis=1
        )
        rows = pl.ds(pair * 2, 2)
        for t, dst, lo, n in ((0, q_s, 8, 96), (1, k_s, 0, 112), (2, v_s, 0, 112)):
            if t == 0 and not inner:
                continue
            out = jnp.dot(normed, weights(t), preferred_element_type=F32).reshape(2, 112, 512)[:, lo : lo + n, :]
            if t == 0:
                out = out * (LOG2E / 8.0)
            dst[rows] = out.astype(BF)

    wait_bytes(w_s.at[pl.ds(0, 4)], wbsem.at[1])
    wait_bytes(w_s.at[pl.ds(0, 7)], w2sem.at[1])
    arrived((zlo == 1) | (zlo == 2), 8, usem.at[0])
    loop(0, 4, lambda i: project(1 + 2 * i + i // 3, True))

    wait_bytes(win_s.at[pl.ds(0, 5), pl.ds(0, 3)], nsem)
    loop(0, 4, lambda i: project(2 + 2 * i - i // 3, True))
    pl.when(has_prev)(lambda: wait_bytes(win_s.at[0], hsem.at[1]))
    project(0, False)
    pl.when(has_next)(lambda: wait_bytes(win_s.at[0], hsem.at[3]))
    project(9, False)

    left = lax.broadcasted_iota(jnp.int32, (32, 128), 1) < 64
    blocks = [(j, hp) for j in range(3) for hp in range(4)]
    lane1 = row_of[0:1, :]

    def attend_row(i):
        at = group * 16 + i - 2 + lane1
        inside = (at >= 0) & (at < NLAT)
        reach = jnp.where(inside, r_s[pl.ds((i // 4) * 8 + i % 4, 1), :], -1.0)
        allowed = dist <= reach
        for hp in range(4):
            t_s[hp, 0:32, :] = jnp.where(allowed, b_s[hp, 0:32, :], NEG)
            t_s[hp, 32:64, :] = jnp.where(allowed, b_s[hp, 32:64, :], NEG)
        for n, (j, hp) in enumerate(blocks):
            cols = slice(hp * 128, hp * 128 + 128)
            qb = q_s[i + 2, j * 32 : j * 32 + 32, cols]
            zero = jnp.zeros_like(qb)
            qq = jnp.concatenate([jnp.where(left, qb, zero), jnp.where(left, zero, qb)], axis=0)
            kb = k_s[pl.ds(i, 5), j * 32 : j * 32 + KB, cols].reshape(KEYS, 128)
            s_s[n] = lax.dot_general(qq, kb, NT, preferred_element_type=F32) + t_s[hp]
        for n in range(12):
            s = s_s[n]
            p = jnp.exp2(s - jnp.max(s, axis=1, keepdims=True))
            l_s[n] = jnp.broadcast_to(jnp.sum(p, axis=1, keepdims=True), (64, 128))
            p_s[n] = p.astype(BF)
        for n, (j, hp) in enumerate(blocks):
            cols = slice(hp * 128, hp * 128 + 128)
            vb = v_s[pl.ds(i, 5), j * 32 : j * 32 + KB, cols].reshape(KEYS, 128)
            o = jnp.dot(p_s[n], vb, preferred_element_type=F32) / l_s[n]
            a_s[i % 2, j * 32 : j * 32 + 32, cols] = jnp.where(left, o[:32], o[32:]).astype(BF)

    s = win_start(me)
    wide = win_start(me + 1) - s == 12

    def rows_of(step):
        pair = (2 * zlo + step) % 8
        loop(0, 2, lambda r: attend_row(pair * 2 + r))
        out = jnp.dot(a_s[...].reshape(192, 512), weights(3), preferred_element_type=F32).reshape(2, 12, 8, 512)
        for k in range(4):
            both = jnp.stack([out[b, :, :, k * 128 : k * 128 + 128] for b in range(2)], axis=1)
            y_s[pair, k] = both.reshape(12, 16, 128).astype(BF)

        def give(k, n, start):
            start(y_s.at[pair, k, pl.ds(0, n)], local_s.at[pair % 2, pl.ds(s, n)])

        def both(k, start):
            pl.when(wide)(lambda: give(k, 12, start))
            pl.when(jnp.logical_not(wide))(lambda: give(k, 11, start))

        for d in range(1, 4):
            k = (ch + d) % 4
            both(k, lambda a, b, k=k: remote(a, b, bsem.at[0], bsem.at[1], (group * 4 + pair // 2, k)))
        if isinstance(step, int):
            both(ch, lambda a, b: pltpu.make_async_copy(a, b, lsem.at[5 + step]).start())
        else:
            both(ch, lambda a, b: remote(a, b, bsem.at[0], bsem.at[1], (group * 4 + pair // 2, ch)))

    wait_bytes(got_s.at[pl.ds(0, 63)], a1sem.at[1])
    coef = jnp.dot(e_s[...], got_s[...].reshape(1024, 128), preferred_element_type=F32)
    coef = coef.reshape(3, DEG, 128) * mg_ref[...][None]
    g_s[ch] = coef.reshape(3 * DEG, 128).astype(BF)
    remote(g_s.at[ch], g_s.at[ch], gsem.at[0], gsem.at[1], (lat, across))
    remote(g_s.at[ch], g_s.at[ch], gsem.at[2], gsem.at[3], (lat, sib))

    rows_of(0)
    wait_bytes(g_s.at[0], gsem.at[1])
    remote(g_s.at[across], g_s.at[across], gsem.at[2], gsem.at[3], (lat, sib))
    rows_of(1)
    wait_bytes(g_s.at[pl.ds(0, 2)], gsem.at[3])
    gained = jnp.concatenate([g_s[k] for k in range(4)], axis=1)
    mixed = jnp.dot(gained, ws_ref[...].astype(BF), preferred_element_type=F32)
    parts = []
    for k in range(3):
        twice = jnp.where((lat + 64 * k) % DEG == 0, 1.0, 2.0).astype(F32)
        parts.append((mixed[k * DEG : k * DEG + DEG] * twice).astype(BF))
    rows_out = lax.dot_general(e_s[...], jnp.concatenate(parts, axis=0), TN, preferred_element_type=F32)
    send2_s[...] = rows_out.astype(BF).reshape(64, 16, 128)
    loop(1, 64, lambda d: remote(send2_s.at[(lat + d) % 64], got2_s.at[lat], a2sem.at[0], a2sem.at[1], ((lat + d) % 64, ch)))
    got2_s[lat] = send2_s[lat]

    loop(2, 8, rows_of)

    wait_bytes(got2_s.at[pl.ds(0, 63)], a2sem.at[1])
    modes = lax.dot_general(sort_rows(), got2_s[...].reshape(1024, 128), TN, preferred_element_type=F32).astype(BF)
    for r in range(4):
        wave_s[r] = lax.dot_general(t16_s[...], modes[r * 192 : r * 192 + 192], TN, preferred_element_type=F32)

    wait_bytes(stat_s.at[pl.ds(0, 3)], statsem.at[0])
    wait_bytes(metas_s.at[pl.ds(0, 6)], metasem.at[0])
    wait_bytes(strip, w1sem.at[0])
    wait_bytes(w_s.at[pl.ds(0, 3), pl.ds(0, 128)], wxsem.at[0])
    wait_bytes(w_s.at[pl.ds(0, 4)], wbsem.at[0])
    wait_bytes(w_s.at[pl.ds(0, 7)], w2sem.at[0])
    wait_bytes(win_s.at[pl.ds(0, 5), pl.ds(0, 3)], ssem.at[0])
    wait_bytes(win_s.at[pl.ds(0, 5), pl.ds(0, 3)], ssem.at[1])
    pl.when(has_next)(lambda: wait_bytes(win_s.at[0], hsem.at[0]))
    pl.when(has_prev)(lambda: wait_bytes(win_s.at[0], hsem.at[2]))
    wait_bytes(got_s.at[pl.ds(0, 63)], a1sem.at[0])
    wait_bytes(g_s.at[0], gsem.at[0])
    wait_bytes(g_s.at[pl.ds(0, 2)], gsem.at[2])
    wait_bytes(got2_s.at[pl.ds(0, 63)], a2sem.at[0])

    def last(n):
        wait_bytes(local_s.at[0, pl.ds(0, n)], lsem.at[5])
        wait_bytes(local_s.at[0, pl.ds(0, n)], lsem.at[6])
        wait_bytes(local_s.at[:, pl.ds(0, 15 * n)], bsem.at[0])
        wait_bytes(local_s.at[:, pl.ds(0, OCT - n)], bsem.at[1])

    pl.when(wide)(lambda: last(12))
    pl.when(jnp.logical_not(wide))(lambda: last(11))

    def total(c):
        lon = pl.ds(pl.multiple_of(c * 144, 16), 144)
        for a in range(2):
            part = local_s[a, pl.ds(c * 18, 18)].astype(F32).reshape(18, 2, 8, 128)
            for b in range(2):
                out_ref[2 * a + b, lon, :] = (wave_s[2 * a + b, lon, :] + part[:, b].reshape(144, 128)).astype(BF)

    loop(0, 10, total)


def layer(*args):
    shape = jax.ShapeDtypeStruct
    vm = pltpu.VMEM
    return pl.pallas_call(
        layer_kernel,
        out_shape=shape((4, NLON, 128), BF),
        in_specs=[VMEM] * 8,
        out_specs=VMEM,
        scratch_shapes=[
            vm((2, OCT, 16, 128), BF),
            vm((10, 4, 14, 16, 128), BF),
            vm((16, 512, 128), BF),
            vm((24, 128), F32),
            vm((16, 24, 128), F32),
            vm((4, 4, NLON), F32),
            vm((2 * DEG, NLON), F32),
            vm((DEG, 8, 128), F32),
            vm((3 * DEG, 1024), BF),
            vm((64, 16, 128), BF),
            vm((64, 16, 128), BF),
            vm((4, 3 * DEG, 128), BF),
            vm((64, 16, 128), BF),
            vm((20, 96, 512), BF),
            vm((20, 112, 512), BF),
            vm((20, 112, 512), BF),
            vm((4, 64, KEYS), F32),
            vm((4, 64, KEYS), F32),
            vm((2, 96, 512), BF),
            vm((12, 64, KEYS), F32),
            vm((12, 64, KEYS), BF),
            vm((12, 64, 128), F32),
            vm((32, KEYS), F32),
            vm((8, 4, 12, 16, 128), BF),
            vm((64, 16, 128), BF),
            vm((2, OCT, 16, 128), BF),
            vm((2 * DEG, NLON), BF),
            vm((4, NLON, 128), F32),
            DMA((7,)), DMA((2,)), DMA((2,)), DMA((2,)), DMA((2,)), DMA((2,)), DMA((2,)), DMA((2,)), DMA((3,)), DMA,
            DMA((4,)), DMA((2,)), DMA((2,)), DMA((4,)), DMA((2,)),
        ],
        compiler_params=pltpu.CompilerParams(
            collective_id=0, has_side_effects=True, vmem_limit_bytes=56 * 1024 * 1024
        ),
        name="layer",
    )(*args)


def per_device(fields, norm_gain, w_qkv, w_out, rel_bias, stencil_reach, mode_gain, w_spec):
    return layer(
        fields,
        norm_gain.reshape(1, 128),
        jnp.transpose(w_qkv, (1, 0, 2)),
        w_out,
        jnp.transpose(rel_bias, (1, 0, 2)),
        stencil_reach,
        mode_gain,
        w_spec,
    )


def solution(mesh):
    in_specs = (
        P("lat", None, "ch"),
        P("ch"),
        P(None, None, "ch"),
        P(None, "ch"),
        P("ch", None, None),
        P("lat", None),
        P(None, "ch"),
        P(None, "ch"),
    )
    return jax.shard_map(
        per_device, mesh=mesh, in_specs=in_specs, out_specs=P("lat", None, "ch"), check_vma=False
    )
```

```python
import math

import jax
import jax.numpy as jnp
from jax import lax
from jax.experimental import pallas as pl
from jax.experimental.pallas import tpu as pltpu
from jax.sharding import PartitionSpec as P

MESH = pl.DeviceIdType.MESH
NLON = 1440
NLAT = 256
DEG = 96
OCT = 180
LOG2E = 1.4426950408889634
NEG = -1e30
EPS = 1e-05
KB = 48
KEYS = 5 * KB
F32 = jnp.float32
BF = jnp.bfloat16
DMA = pltpu.SemaphoreType.DMA
VMEM = pl.BlockSpec(memory_space=pltpu.VMEM)
TN = (((0,), (0,)), ((), ()))
NT = (((1,), (1,)), ((), ()))


def win_start(w):
    return 45 * w // 4


def ring_dev(w, group):
    return (group * 4 + w // 4, w % 4)


def place():
    lat = lax.axis_index("lat")
    ch = lax.axis_index("ch")
    return lat, ch, lat // 4, lat % 4


def signal(device):
    pl.semaphore_signal(pltpu.get_barrier_semaphore(), inc=1, device_id=device, device_id_type=MESH)


def remote(src, dst, ss, rs, device):
    pltpu.make_async_remote_copy(
        src_ref=src, dst_ref=dst, send_sem=ss, recv_sem=rs, device_id=device, device_id_type=MESH
    ).start()


def wait_bytes(ref, sem):
    pltpu.make_async_copy(ref, ref, sem).wait()


def loop(lo, hi, body):
    def step(i, c):
        body(i)
        return c

    lax.fori_loop(lo, hi, step, 0)


def sort_rows():
    n = lax.broadcasted_iota(jnp.int32, (1024, 1), 0)
    slot = n % 16
    source = jnp.where(slot < 12, (slot % 4) * 192 + (slot // 4) * 64 + n // 16, -1)
    return (lax.broadcasted_iota(jnp.int32, (1024, 768), 1) == source).astype(F32).astype(BF)


def tables(tab_s, t_ref):
    row = lax.broadcasted_iota(jnp.int32, (2 * DEG, 128), 0)
    lane = lax.broadcasted_iota(jnp.int32, (2 * DEG, 128), 1).astype(F32)
    first = row < DEG
    order = jnp.where(first, row, row - DEG).astype(F32)

    def angle(cells):
        turns = cells * order
        turns = turns - NLON * jnp.floor((turns + 0.5) * (1.0 / NLON))
        return turns * (2.0 * math.pi / NLON)

    coarse, fine = angle(jnp.where(lane < 12, lane * 128.0, 0.0)), angle(lane)
    ca, sa, cb, sb = jnp.cos(coarse), jnp.sin(coarse), jnp.cos(fine), jnp.sin(fine)
    u = jnp.where(first, cb, -sb)
    v = jnp.where(first, -sb, -cb)
    for a in range(12):
        n = min(128, NLON - a * 128)
        tab = ca[:, a : a + 1] * u + sa[:, a : a + 1] * v
        tab_s[:, a * 128 : a * 128 + n] = tab[:, :n]
        t_ref[:, a * 128 : a * 128 + n] = tab[:, :n].astype(BF)


def legendre(lat, leg_s, e_s):
    lane = lax.broadcasted_iota(jnp.int32, (8, 128), 1)
    n = lax.broadcasted_iota(jnp.int32, (8, 128), 0) * 128 + lane
    kind = (n % 16) // 4
    row = (n // 16) * 4 + n % 4
    theta = (row.astype(F32) + 0.5) * (math.pi / NLAT)
    factor = lax.broadcasted_iota(jnp.int32, (1, 128), 1)
    number = jnp.maximum(factor, 1).astype(F32)
    log_ratio = jnp.log((2.0 * number - 1.0) / (2.0 * number))
    m = jnp.zeros((8, 128), F32)
    begin = jnp.zeros((8, 128), F32)
    for k in range(3):
        order = (lat + 64 * k) % DEG
        total = jnp.sum(jnp.where((factor >= 1) & (factor <= order), log_ratio, 0.0), axis=1, keepdims=True)
        m = jnp.where(kind == k, order.astype(F32), m)
        begin = jnp.where(kind == k, total, begin)
    begin = 0.5 * (begin + jnp.log((2.0 * m + 1.0) / (4.0 * math.pi)))
    diagonal = jnp.where(kind < 3, jnp.exp(begin + m * jnp.log(jnp.sin(theta))), 0.0)
    cosine = jnp.cos(theta)

    def degree(l, carry):
        previous, earlier = carry
        deg = l.astype(F32)
        less = deg - 1.0
        upper = jnp.sqrt(jnp.maximum(4.0 * deg * deg - 1.0, 0.0) / jnp.maximum(deg * deg - m * m, 1.0))
        lower = jnp.sqrt(jnp.maximum(less * less - m * m, 0.0) / jnp.maximum(4.0 * less * less - 1.0, 1.0))
        value = upper * (cosine * previous - lower * earlier)
        current = jnp.where(m == deg, diagonal, jnp.where(m < deg, value, 0.0))
        leg_s[l] = current
        return current, previous

    zero = diagonal * 0.0
    lax.fori_loop(0, DEG, degree, (zero, zero))
    kind = (lax.broadcasted_iota(jnp.int32, (DEG, 128), 1) % 16) // 4
    for c in range(8):
        part = leg_s[:, c, :]
        for k in range(3):
            e_s[k * DEG : k * DEG + DEG, c * 128 : c * 128 + 128] = jnp.where(kind == k, part, 0.0).astype(BF)


def layer_kernel(
    f_ref, gain_ref, wq_ref, wo_ref, bias_ref, reach_ref, mg_ref, ws_ref,
    out_ref,
    x_s, win_s, w_s, meta_s, metas_s, stat_s, tab_s, leg_s, e_s, send1_s, got_s, g_s, send2_s,
    q_s, k_s, v_s, b_s, t_s, a_s, s_s, p_s, l_s, r_s, y_s, got2_s, local_s, t16_s, wave_s,
    lsem, statsem, metasem, w1sem, wxsem, wbsem, w2sem, ssem, usem, nsem, hsem, a1sem, a2sem, gsem, bsem,
):
    lat, ch, group, zlo = place()
    me = zlo * 4 + ch
    has_next = group < 15
    has_prev = group > 0
    quarter = pl.ds(pl.multiple_of((group // 4) * 128, 128), 128)
    sixteenth = pl.ds(pl.multiple_of(group * 32, 32), 32)
    sib = ch + 1 - 2 * (ch % 2)
    across = (ch + 2) % 4
    loop(1, 64, lambda d: signal(((lat + d) % 64, ch)))
    for z in range(4):
        for d in range(1, 4):
            signal((group * 4 + z, (ch + d) % 4))
    for d in range(1, 4):
        signal(((lat + 16 * d) % 64, sib))

    ones = jnp.ones((8, 256), BF)
    for r in range(4):
        x = f_ref[r].astype(F32)
        x = x * x
        high = x.astype(BF)
        both = jnp.concatenate([high, (x - high.astype(F32)).astype(BF)], axis=1)
        sums = lax.dot_general(ones, both, NT, preferred_element_type=F32)
        stat_s[ch, r : r + 1, :] = sums[0:1]
    gain = gain_ref[...].astype(F32)
    meta_s[...] = jnp.zeros_like(meta_s)
    for a in range(5):
        for h in range(2):
            meta_s[h * 8 + a : h * 8 + a + 1, 0:17] = bias_ref[a, h : h + 1, :]
    meta_s[16:20, 0:5] = reach_ref[...].astype(F32)
    meta_s[20:21, :] = gain

    def interleave(c):
        lon = pl.ds(pl.multiple_of(c * 144, 16), 144)
        for a in range(2):
            two = [f_ref[2 * a + b, lon, :].astype(F32).reshape(18, 8, 128) for b in range(2)]
            x_s[a, pl.ds(c * 18, 18)] = jnp.stack(two, axis=1).reshape(18, 16, 128).astype(BF)

    loop(0, 10, interleave)

    @pl.when(jnp.logical_not(has_prev))
    def _():
        win_s[0] = jnp.zeros_like(win_s[0])

    @pl.when(jnp.logical_not(has_next))
    def _():
        win_s[9] = jnp.zeros_like(win_s[9])

    pl.semaphore_wait(pltpu.get_barrier_semaphore(), 78)

    for d in range(1, 4):
        remote(stat_s.at[ch], stat_s.at[ch], statsem.at[0], statsem.at[1], (lat, (ch + d) % 4))
    for d in range(1, 4):
        remote(meta_s, metas_s.at[me], metasem.at[0], metasem.at[1], (lat, (ch + d) % 4))
        remote(meta_s, metas_s.at[me], metasem.at[0], metasem.at[1], (group * 4 + (zlo + d) % 4, ch))
    remote(wq_ref.at[:, sixteenth], w_s.at[pl.ds(ch * 4, 3), sixteenth], w1sem.at[0], w1sem.at[1], (lat, across))
    remote(wo_ref.at[sixteenth], w_s.at[ch * 4 + 3, sixteenth], w1sem.at[0], w1sem.at[1], (lat, across))
    remote(wq_ref, w_s.at[pl.ds(ch * 4, 3)], wbsem.at[0], wbsem.at[1], (lat, sib))
    remote(wo_ref, w_s.at[ch * 4 + 3], wbsem.at[0], wbsem.at[1], (lat, sib))
    own = [
        pltpu.make_async_copy(meta_s, metas_s.at[me], lsem.at[2]),
        pltpu.make_async_copy(wq_ref, w_s.at[pl.ds(ch * 4, 3)], lsem.at[3]),
        pltpu.make_async_copy(wo_ref, w_s.at[ch * 4 + 3], lsem.at[4]),
    ]
    for copy in own:
        copy.start()

    def move(w, src_pair, pairs, dst_pair, start):
        s = win_start(w)
        src, dst = pl.ds(src_pair, pairs), pl.ds(dst_pair, pairs)
        edge = (w == 0) | (w == 15)

        @pl.when(edge)
        def _():
            a_src = jnp.where(w == 0, 0, s - 1)
            a_dst = jnp.where(w == 0, 1, 0)
            b_src = jnp.where(w == 0, OCT - 1, 0)
            b_dst = jnp.where(w == 0, 0, 13)
            start(x_s.at[src, pl.ds(a_src, 13)], win_s.at[dst, ch, pl.ds(a_dst, 13)], 0)
            start(x_s.at[src, pl.ds(b_src, 1)], win_s.at[dst, ch, pl.ds(b_dst, 1)], 1)

        @pl.when(jnp.logical_not(edge))
        def _():
            start(x_s.at[src, pl.ds(s - 1, 14)], win_s.at[dst, ch], 0)

    def to(pair, ss, rs, dz, dc):
        z = ((ch // 2) * 4 + zlo + dz) % 8
        w = (z % 4) * 4 + (z // 4) * 2 + (ch + dc) % 2
        move(w, pair, 1, 1 + 2 * zlo + pair, lambda a, b, n: remote(a, b, ss, rs, ring_dev(w, group)))

    def near(pair, ss, rs):
        def one(t):
            u = t // 2
            dz = jnp.where(u == 4, 0, jnp.where(u % 2 == 0, u // 2 + 1, 7 - u // 2))
            to(pair, ss, rs, dz, jnp.where(t == 8, 1, t % 2))

        loop(0, 9, one)

    def far(pair, ss, rs):
        def one(t):
            u = t // 2
            to(pair, ss, rs, jnp.where(u == 0, 3, jnp.where(u == 1, 5, 4)), t % 2)

        loop(0, 6, one)

    move(me, 0, 2, 1 + 2 * zlo, lambda a, b, n: pltpu.make_async_copy(a, b, lsem.at[n]).start())
    urgent = jnp.where(zlo == 3, 1, 0)
    first = (urgent, ssem.at[0], usem.at[jnp.where(zlo == 0, 1, jnp.where(zlo == 3, 2, 0))])
    second = (1 - urgent, ssem.at[1], nsem)
    near(*first)
    far(*first)

    tables(tab_s, t16_s)
    wait_bytes(stat_s.at[pl.ds(0, 3)], statsem.at[1])
    scale = lax.rsqrt((stat_s[0] + stat_s[1] + stat_s[2] + stat_s[3]) * (1.0 / 512.0) + EPS)
    theta = ((lat * 4 + lax.broadcasted_iota(jnp.int32, (4, 128), 0)).astype(F32) + 0.5) * (math.pi / NLAT)
    weight = jnp.sin(theta) * (math.pi / NLAT * 2.0 * math.pi / NLON) * gain
    freq = []
    for r in range(4):
        lhs = (tab_s[...] * scale[r : r + 1, :]).astype(BF)
        out = jnp.dot(lhs, f_ref[r], preferred_element_type=F32)
        freq.append((out * weight[r : r + 1, :]).astype(BF))
    out = jnp.dot(sort_rows(), jnp.concatenate(freq, axis=0), preferred_element_type=F32)
    send1_s[...] = out.astype(BF).reshape(64, 16, 128)
    loop(1, 64, lambda d: remote(send1_s.at[(lat + d) % 64], got_s.at[lat], a1sem.at[0], a1sem.at[1], ((lat + d) % 64, ch)))
    got_s[lat] = send1_s[lat]

    near(*second)

    wait_bytes(w_s.at[pl.ds(across * 4, 4), sixteenth], w1sem.at[1])
    strip = w_s.at[pl.ds(across * 4, 4), sixteenth]
    for d in range(1, 4):
        remote(strip, strip, wxsem.at[0], wxsem.at[1], (lat - group % 4 * 4 + (group + d) % 4 * 4, ch))
    legendre(lat, leg_s, e_s)
    part = w_s.at[pl.ds(across * 4, 4), quarter]
    wait_bytes(w_s.at[pl.ds(0, 3), pl.ds(0, 128)], wxsem.at[1])
    remote(part, part, w2sem.at[0], w2sem.at[1], (lat, sib))
    for d in range(1, 4):
        remote(part, part, w2sem.at[0], w2sem.at[1], ((lat + 16 * d) % 64, ch))
        remote(part, part, w2sem.at[0], w2sem.at[1], ((lat + 16 * d) % 64, sib))

    @pl.when((me == 0) | (me == 15))
    def _():
        wait_bytes(win_s.at[pl.ds(0, 2), 0, pl.ds(0, 13)], lsem.at[0])
        wait_bytes(win_s.at[pl.ds(0, 2), 0, pl.ds(0, 1)], lsem.at[1])

    @pl.when((me != 0) & (me != 15))
    def _():
        wait_bytes(win_s.at[pl.ds(0, 2), 0], lsem.at[0])

    def arrived(own_here, full, sem):
        pl.when(own_here)(lambda: wait_bytes(win_s.at[pl.ds(0, full - 1), 0], sem))
        pl.when(jnp.logical_not(own_here))(lambda: wait_bytes(win_s.at[pl.ds(0, full), 0], sem))

    arrived(zlo == 0, 4, usem.at[1])
    arrived(zlo == 3, 4, usem.at[2])
    pl.when(has_next)(lambda: remote(win_s.at[8], win_s.at[0], hsem.at[0], hsem.at[1], ((lat + 4) % 64, ch)))
    pl.when(has_prev)(lambda: remote(win_s.at[1], win_s.at[9], hsem.at[2], hsem.at[3], ((lat + 60) % 64, ch)))

    far(*second)


    for copy in own:
        copy.wait()
    wait_bytes(metas_s.at[pl.ds(0, 6)], metasem.at[1])
    lane = lax.broadcasted_iota(jnp.int32, (32, KEYS), 1)
    query = lax.broadcasted_iota(jnp.int32, (32, KEYS), 0)
    row_of = sum((lane >= KB * a).astype(jnp.int32) for a in range(1, 5))
    delta = lane - KB * row_of - query - 8
    dist = jnp.abs(delta).astype(F32)
    lane8 = lax.broadcasted_iota(jnp.int32, (8, KEYS), 1)
    row8 = sum((lane8 >= KB * a).astype(jnp.int32) for a in range(1, 5))
    onto = (row8 == lax.broadcasted_iota(jnp.int32, (8, KEYS), 0)).astype(F32)
    for h in range(8):
        mine = metas_s[zlo * 4 + h // 2, (h % 2) * 8 : (h % 2) * 8 + 8, :]
        vec = lax.dot_general(mine, onto, TN, precision=lax.Precision.HIGHEST, preferred_element_type=F32)
        tile = jnp.full((32, KEYS), NEG, F32)
        for b in range(17):
            tile = jnp.where(delta == b - 8, vec[b : b + 1, :] * LOG2E, tile)
        b_s[h // 2, (h % 2) * 32 : (h % 2) * 32 + 32, :] = tile
    lane128 = lax.broadcasted_iota(jnp.int32, (128, KEYS), 1)
    row128 = sum((lane128 >= KB * a).astype(jnp.int32) for a in range(1, 5))
    pick = (row128 == lax.broadcasted_iota(jnp.int32, (128, KEYS), 0)).astype(F32)
    for z in range(4):
        r_s[z * 8 : z * 8 + 8, :] = jnp.dot(metas_s[z * 4 + ch, 16:24, :], pick, preferred_element_type=F32)

    def weights(t):
        return jnp.concatenate([w_s[k * 4 + t] for k in range(4)], axis=1)

    def project(pair, inner):
        parts = []
        for k in range(4):
            p = win_s[pair, k].astype(F32).reshape(14, 2, 8, 128)
            parts.append(jnp.concatenate([p[:, r].reshape(112, 128) for r in range(2)], axis=0))
        square = jnp.sum(sum(p * p for p in parts), axis=1, keepdims=True)
        scale = lax.rsqrt(square * (1.0 / 512.0) + EPS)
        normed = jnp.concatenate(
            [(p * scale * metas_s[zlo * 4 + k, 20:21, :]).astype(BF) for k, p in enumerate(parts)], axis=1
        )
        rows = pl.ds(pair * 2, 2)
        for t, dst, lo, n in ((0, q_s, 8, 96), (1, k_s, 0, 112), (2, v_s, 0, 112)):
            if t == 0 and not inner:
                continue
            out = jnp.dot(normed, weights(t), preferred_element_type=F32).reshape(2, 112, 512)[:, lo : lo + n, :]
            if t == 0:
                out = out * (LOG2E / 8.0)
            dst[rows] = out.astype(BF)

    wait_bytes(w_s.at[pl.ds(0, 4)], wbsem.at[1])
    wait_bytes(w_s.at[pl.ds(0, 7)], w2sem.at[1])
    arrived((zlo == 1) | (zlo == 2), 8, usem.at[0])
    loop(0, 4, lambda i: project(1 + 2 * i + i // 3, True))

    wait_bytes(win_s.at[pl.ds(0, 5), pl.ds(0, 3)], nsem)
    pl.when(has_prev)(lambda: wait_bytes(win_s.at[0], hsem.at[1]))
    pl.when(has_next)(lambda: wait_bytes(win_s.at[0], hsem.at[3]))
    loop(0, 2, lambda i: project(2 * zlo + i * jnp.where(zlo == 3, 1, 2), True))

    left = lax.broadcasted_iota(jnp.int32, (32, 128), 1) < 64
    blocks = [(j, hp) for j in range(3) for hp in range(4)]
    lane1 = row_of[0:1, :]

    def attend_row(i):
        at = group * 16 + i - 2 + lane1
        inside = (at >= 0) & (at < NLAT)
        reach = jnp.where(inside, r_s[pl.ds((i // 4) * 8 + i % 4, 1), :], -1.0)
        allowed = dist <= reach
        for hp in range(4):
            t_s[hp, 0:32, :] = jnp.where(allowed, b_s[hp, 0:32, :], NEG)
            t_s[hp, 32:64, :] = jnp.where(allowed, b_s[hp, 32:64, :], NEG)
        for n, (j, hp) in enumerate(blocks):
            cols = slice(hp * 128, hp * 128 + 128)
            qb = q_s[i + 2, j * 32 : j * 32 + 32, cols]
            zero = jnp.zeros_like(qb)
            qq = jnp.concatenate([jnp.where(left, qb, zero), jnp.where(left, zero, qb)], axis=0)
            kb = k_s[pl.ds(i, 5), j * 32 : j * 32 + KB, cols].reshape(KEYS, 128)
            s_s[n] = lax.dot_general(qq, kb, NT, preferred_element_type=F32) + t_s[hp]
        for n in range(12):
            s = s_s[n]
            p = jnp.exp2(s - jnp.max(s, axis=1, keepdims=True))
            l_s[n] = jnp.broadcast_to(jnp.sum(p, axis=1, keepdims=True), (64, 128))
            p_s[n] = p.astype(BF)
        for n, (j, hp) in enumerate(blocks):
            cols = slice(hp * 128, hp * 128 + 128)
            vb = v_s[pl.ds(i, 5), j * 32 : j * 32 + KB, cols].reshape(KEYS, 128)
            o = jnp.dot(p_s[n], vb, preferred_element_type=F32) / l_s[n]
            a_s[i % 2, j * 32 : j * 32 + 32, cols] = jnp.where(left, o[:32], o[32:]).astype(BF)

    s = win_start(me)
    wide = win_start(me + 1) - s == 12

    def rows_of(step):
        pair = (2 * zlo + step) % 8
        loop(0, 2, lambda r: attend_row(pair * 2 + r))
        out = jnp.dot(a_s[...].reshape(192, 512), weights(3), preferred_element_type=F32).reshape(2, 12, 8, 512)
        for k in range(4):
            both = jnp.stack([out[b, :, :, k * 128 : k * 128 + 128] for b in range(2)], axis=1)
            y_s[pair, k] = both.reshape(12, 16, 128).astype(BF)

        def give(k, n, start):
            start(y_s.at[pair, k, pl.ds(0, n)], local_s.at[pair % 2, pl.ds(s, n)])

        def both(k, start):
            pl.when(wide)(lambda: give(k, 12, start))
            pl.when(jnp.logical_not(wide))(lambda: give(k, 11, start))

        for d in range(1, 4):
            k = (ch + d) % 4
            both(k, lambda a, b, k=k: remote(a, b, bsem.at[0], bsem.at[1], (group * 4 + pair // 2, k)))
        if isinstance(step, int):
            both(ch, lambda a, b: pltpu.make_async_copy(a, b, lsem.at[5 + step]).start())
        else:
            both(ch, lambda a, b: remote(a, b, bsem.at[0], bsem.at[1], (group * 4 + pair // 2, ch)))

    wait_bytes(got_s.at[pl.ds(0, 63)], a1sem.at[1])
    coef = jnp.dot(e_s[...], got_s[...].reshape(1024, 128), preferred_element_type=F32)
    coef = coef.reshape(3, DEG, 128) * mg_ref[...][None]
    g_s[ch] = coef.reshape(3 * DEG, 128).astype(BF)
    remote(g_s.at[ch], g_s.at[ch], gsem.at[0], gsem.at[1], (lat, across))
    remote(g_s.at[ch], g_s.at[ch], gsem.at[2], gsem.at[3], (lat, sib))

    rows_of(0)
    loop(0, 3, lambda i: project(jnp.where(i < zlo, 2 * i, jnp.where(i == 2, 7, 4 + 2 * i)), True))
    project(9, False)
    rows_of(1)
    wait_bytes(g_s.at[0], gsem.at[1])
    remote(g_s.at[across], g_s.at[across], gsem.at[2], gsem.at[3], (lat, sib))
    loop(2, 5, rows_of)
    wait_bytes(g_s.at[pl.ds(0, 2)], gsem.at[3])
    gained = jnp.concatenate([g_s[k] for k in range(4)], axis=1)
    mixed = jnp.dot(gained, ws_ref[...].astype(BF), preferred_element_type=F32)
    parts = []
    for k in range(3):
        twice = jnp.where((lat + 64 * k) % DEG == 0, 1.0, 2.0).astype(F32)
        parts.append((mixed[k * DEG : k * DEG + DEG] * twice).astype(BF))
    rows_out = lax.dot_general(e_s[...], jnp.concatenate(parts, axis=0), TN, preferred_element_type=F32)
    send2_s[...] = rows_out.astype(BF).reshape(64, 16, 128)
    loop(1, 64, lambda d: remote(send2_s.at[(lat + d) % 64], got2_s.at[lat], a2sem.at[0], a2sem.at[1], ((lat + d) % 64, ch)))
    got2_s[lat] = send2_s[lat]

    loop(5, 8, rows_of)

    wait_bytes(got2_s.at[pl.ds(0, 63)], a2sem.at[1])
    modes = lax.dot_general(sort_rows(), got2_s[...].reshape(1024, 128), TN, preferred_element_type=F32).astype(BF)
    for r in range(4):
        wave_s[r] = lax.dot_general(t16_s[...], modes[r * 192 : r * 192 + 192], TN, preferred_element_type=F32)

    wait_bytes(stat_s.at[pl.ds(0, 3)], statsem.at[0])
    wait_bytes(metas_s.at[pl.ds(0, 6)], metasem.at[0])
    wait_bytes(strip, w1sem.at[0])
    wait_bytes(w_s.at[pl.ds(0, 3), pl.ds(0, 128)], wxsem.at[0])
    wait_bytes(w_s.at[pl.ds(0, 4)], wbsem.at[0])
    wait_bytes(w_s.at[pl.ds(0, 7)], w2sem.at[0])
    wait_bytes(win_s.at[pl.ds(0, 5), pl.ds(0, 3)], ssem.at[0])
    wait_bytes(win_s.at[pl.ds(0, 5), pl.ds(0, 3)], ssem.at[1])
    pl.when(has_next)(lambda: wait_bytes(win_s.at[0], hsem.at[0]))
    pl.when(has_prev)(lambda: wait_bytes(win_s.at[0], hsem.at[2]))
    wait_bytes(got_s.at[pl.ds(0, 63)], a1sem.at[0])
    wait_bytes(g_s.at[0], gsem.at[0])
    wait_bytes(g_s.at[pl.ds(0, 2)], gsem.at[2])
    wait_bytes(got2_s.at[pl.ds(0, 63)], a2sem.at[0])

    def last(n):
        wait_bytes(local_s.at[0, pl.ds(0, n)], lsem.at[5])
        wait_bytes(local_s.at[0, pl.ds(0, n)], lsem.at[6])
        wait_bytes(local_s.at[:, pl.ds(0, 15 * n)], bsem.at[0])
        wait_bytes(local_s.at[:, pl.ds(0, OCT - n)], bsem.at[1])

    pl.when(wide)(lambda: last(12))
    pl.when(jnp.logical_not(wide))(lambda: last(11))

    def total(c):
        lon = pl.ds(pl.multiple_of(c * 144, 16), 144)
        for a in range(2):
            part = local_s[a, pl.ds(c * 18, 18)].astype(F32).reshape(18, 2, 8, 128)
            for b in range(2):
                out_ref[2 * a + b, lon, :] = (wave_s[2 * a + b, lon, :] + part[:, b].reshape(144, 128)).astype(BF)

    loop(0, 10, total)


def layer(*args):
    shape = jax.ShapeDtypeStruct
    vm = pltpu.VMEM
    return pl.pallas_call(
        layer_kernel,
        out_shape=shape((4, NLON, 128), BF),
        in_specs=[VMEM] * 8,
        out_specs=VMEM,
        scratch_shapes=[
            vm((2, OCT, 16, 128), BF),
            vm((10, 4, 14, 16, 128), BF),
            vm((16, 512, 128), BF),
            vm((24, 128), F32),
            vm((16, 24, 128), F32),
            vm((4, 4, NLON), F32),
            vm((2 * DEG, NLON), F32),
            vm((DEG, 8, 128), F32),
            vm((3 * DEG, 1024), BF),
            vm((64, 16, 128), BF),
            vm((64, 16, 128), BF),
            vm((4, 3 * DEG, 128), BF),
            vm((64, 16, 128), BF),
            vm((20, 96, 512), BF),
            vm((20, 112, 512), BF),
            vm((20, 112, 512), BF),
            vm((4, 64, KEYS), F32),
            vm((4, 64, KEYS), F32),
            vm((2, 96, 512), BF),
            vm((12, 64, KEYS), F32),
            vm((12, 64, KEYS), BF),
            vm((12, 64, 128), F32),
            vm((32, KEYS), F32),
            vm((8, 4, 12, 16, 128), BF),
            vm((64, 16, 128), BF),
            vm((2, OCT, 16, 128), BF),
            vm((2 * DEG, NLON), BF),
            vm((4, NLON, 128), F32),
            DMA((7,)), DMA((2,)), DMA((2,)), DMA((2,)), DMA((2,)), DMA((2,)), DMA((2,)), DMA((2,)), DMA((3,)), DMA,
            DMA((4,)), DMA((2,)), DMA((2,)), DMA((4,)), DMA((2,)),
        ],
        compiler_params=pltpu.CompilerParams(
            collective_id=0, has_side_effects=True, vmem_limit_bytes=56 * 1024 * 1024
        ),
        name="layer",
    )(*args)


def per_device(fields, norm_gain, w_qkv, w_out, rel_bias, stencil_reach, mode_gain, w_spec):
    return layer(
        fields,
        norm_gain.reshape(1, 128),
        jnp.transpose(w_qkv, (1, 0, 2)),
        w_out,
        jnp.transpose(rel_bias, (1, 0, 2)),
        stencil_reach,
        mode_gain,
        w_spec,
    )


def solution(mesh):
    in_specs = (
        P("lat", None, "ch"),
        P("ch"),
        P(None, None, "ch"),
        P(None, "ch"),
        P("ch", None, None),
        P("lat", None),
        P(None, "ch"),
        P(None, "ch"),
    )
    return jax.shard_map(
        per_device, mesh=mesh, in_specs=in_specs, out_specs=P("lat", None, "ch"), check_vma=False
    )
```

```python
import math

import jax
import jax.numpy as jnp
from jax import lax
from jax.experimental import pallas as pl
from jax.experimental.pallas import tpu as pltpu
from jax.sharding import PartitionSpec as P

MESH = pl.DeviceIdType.MESH
NLON = 1440
NLAT = 256
DEG = 96
OCT = 180
LOG2E = 1.4426950408889634
NEG = -1e30
EPS = 1e-05
KB = 48
KEYS = 5 * KB
F32 = jnp.float32
BF = jnp.bfloat16
DMA = pltpu.SemaphoreType.DMA
VMEM = pl.BlockSpec(memory_space=pltpu.VMEM)
TN = (((0,), (0,)), ((), ()))
NT = (((1,), (1,)), ((), ()))


def win_start(w):
    return 45 * w // 4


def ring_dev(w, group):
    return (group * 4 + w // 4, w % 4)


def place():
    lat = lax.axis_index("lat")
    ch = lax.axis_index("ch")
    return lat, ch, lat // 4, lat % 4


def signal(device):
    pl.semaphore_signal(pltpu.get_barrier_semaphore(), inc=1, device_id=device, device_id_type=MESH)


def remote(src, dst, ss, rs, device):
    pltpu.make_async_remote_copy(
        src_ref=src, dst_ref=dst, send_sem=ss, recv_sem=rs, device_id=device, device_id_type=MESH
    ).start()


def wait_bytes(ref, sem):
    pltpu.make_async_copy(ref, ref, sem).wait()


def loop(lo, hi, body):
    def step(i, c):
        body(i)
        return c

    lax.fori_loop(lo, hi, step, 0)


def sort_rows():
    n = lax.broadcasted_iota(jnp.int32, (1024, 1), 0)
    slot = n % 16
    source = jnp.where(slot < 12, (slot % 4) * 192 + (slot // 4) * 64 + n // 16, -1)
    return (lax.broadcasted_iota(jnp.int32, (1024, 768), 1) == source).astype(F32).astype(BF)


def tables(tab_s, t_ref):
    row = lax.broadcasted_iota(jnp.int32, (2 * DEG, 128), 0)
    lane = lax.broadcasted_iota(jnp.int32, (2 * DEG, 128), 1).astype(F32)
    first = row < DEG
    order = jnp.where(first, row, row - DEG).astype(F32)

    def angle(cells):
        turns = cells * order
        turns = turns - NLON * jnp.floor((turns + 0.5) * (1.0 / NLON))
        return turns * (2.0 * math.pi / NLON)

    coarse, fine = angle(jnp.where(lane < 12, lane * 128.0, 0.0)), angle(lane)
    ca, sa, cb, sb = jnp.cos(coarse), jnp.sin(coarse), jnp.cos(fine), jnp.sin(fine)
    u = jnp.where(first, cb, -sb)
    v = jnp.where(first, -sb, -cb)
    for a in range(12):
        n = min(128, NLON - a * 128)
        tab = ca[:, a : a + 1] * u + sa[:, a : a + 1] * v
        tab_s[:, a * 128 : a * 128 + n] = tab[:, :n]
        t_ref[:, a * 128 : a * 128 + n] = tab[:, :n].astype(BF)


def legendre(lat, leg_s, e_s):
    lane = lax.broadcasted_iota(jnp.int32, (8, 128), 1)
    n = lax.broadcasted_iota(jnp.int32, (8, 128), 0) * 128 + lane
    kind = (n % 16) // 4
    row = (n // 16) * 4 + n % 4
    theta = (row.astype(F32) + 0.5) * (math.pi / NLAT)
    factor = lax.broadcasted_iota(jnp.int32, (1, 128), 1)
    number = jnp.maximum(factor, 1).astype(F32)
    log_ratio = jnp.log((2.0 * number - 1.0) / (2.0 * number))
    m = jnp.zeros((8, 128), F32)
    begin = jnp.zeros((8, 128), F32)
    for k in range(3):
        order = (lat + 64 * k) % DEG
        total = jnp.sum(jnp.where((factor >= 1) & (factor <= order), log_ratio, 0.0), axis=1, keepdims=True)
        m = jnp.where(kind == k, order.astype(F32), m)
        begin = jnp.where(kind == k, total, begin)
    begin = 0.5 * (begin + jnp.log((2.0 * m + 1.0) / (4.0 * math.pi)))
    diagonal = jnp.where(kind < 3, jnp.exp(begin + m * jnp.log(jnp.sin(theta))), 0.0)
    cosine = jnp.cos(theta)

    def degree(l, carry):
        previous, earlier = carry
        deg = l.astype(F32)
        less = deg - 1.0
        upper = jnp.sqrt(jnp.maximum(4.0 * deg * deg - 1.0, 0.0) / jnp.maximum(deg * deg - m * m, 1.0))
        lower = jnp.sqrt(jnp.maximum(less * less - m * m, 0.0) / jnp.maximum(4.0 * less * less - 1.0, 1.0))
        value = upper * (cosine * previous - lower * earlier)
        current = jnp.where(m == deg, diagonal, jnp.where(m < deg, value, 0.0))
        leg_s[l] = current
        return current, previous

    zero = diagonal * 0.0
    lax.fori_loop(0, DEG, degree, (zero, zero))
    kind = (lax.broadcasted_iota(jnp.int32, (DEG, 128), 1) % 16) // 4
    for c in range(8):
        part = leg_s[:, c, :]
        for k in range(3):
            e_s[k * DEG : k * DEG + DEG, c * 128 : c * 128 + 128] = jnp.where(kind == k, part, 0.0).astype(BF)


def layer_kernel(
    f_ref, gain_ref, wq_ref, wo_ref, bias_ref, reach_ref, mg_ref, ws_ref,
    out_ref,
    x_s, win_s, w_s, meta_s, metas_s, stat_s, tab_s, leg_s, e_s, send1_s, got_s, g_s, send2_s,
    q_s, k_s, v_s, b_s, t_s, a_s, s_s, p_s, l_s, r_s, y_s, got2_s, local_s, t16_s, wave_s,
    lsem, fsem, statsem, metasem, w1sem, wxsem, wbsem, w2sem, ssem, usem, nsem, hsem, a1sem, a2sem, gsem, bsem,
):
    lat, ch, group, zlo = place()
    me = zlo * 4 + ch
    has_next = group < 15
    has_prev = group > 0
    quarter = pl.ds(pl.multiple_of((group // 4) * 128, 128), 128)
    sixteenth = pl.ds(pl.multiple_of(group * 32, 32), 32)
    wide = ch == 3
    sib = ch + 1 - 2 * (ch % 2)
    across = (ch + 2) % 4
    loop(1, 64, lambda d: signal(((lat + d) % 64, ch)))
    for z in range(4):
        for d in range(1, 4):
            signal((group * 4 + z, (ch + d) % 4))
    for d in range(1, 4):
        signal(((lat + 16 * d) % 64, sib))

    ones = jnp.ones((8, 256), BF)
    for r in range(4):
        x = f_ref[r].astype(F32)
        x = x * x
        high = x.astype(BF)
        both = jnp.concatenate([high, (x - high.astype(F32)).astype(BF)], axis=1)
        sums = lax.dot_general(ones, both, NT, preferred_element_type=F32)
        stat_s[ch, r : r + 1, :] = sums[0:1]
    gain = gain_ref[...].astype(F32)
    meta_s[...] = jnp.zeros_like(meta_s)
    for a in range(5):
        for h in range(2):
            meta_s[h * 8 + a : h * 8 + a + 1, 0:17] = bias_ref[a, h : h + 1, :]
    meta_s[16:20, 0:5] = reach_ref[...].astype(F32)
    meta_s[20:21, :] = gain

    def interleave(c):
        lon = pl.ds(pl.multiple_of(c * 144, 16), 144)
        for a in range(2):
            two = [f_ref[2 * a + b, lon, :].astype(F32).reshape(18, 8, 128) for b in range(2)]
            x_s[pl.ds(a * OCT + c * 18, 18)] = jnp.stack(two, axis=1).reshape(18, 16, 128).astype(BF)

    loop(0, 10, interleave)

    @pl.when(jnp.logical_not(wide))
    def _():
        win_s[1:9, :, 13] = jnp.zeros_like(win_s[1:9, :, 13])

    @pl.when(jnp.logical_not(has_prev))
    def _():
        win_s[0] = jnp.zeros_like(win_s[0])

    @pl.when(jnp.logical_not(has_next))
    def _():
        win_s[9] = jnp.zeros_like(win_s[9])

    pl.semaphore_wait(pltpu.get_barrier_semaphore(), 78)

    for d in range(1, 4):
        remote(stat_s.at[ch], stat_s.at[ch], statsem.at[0], statsem.at[1], (lat, (ch + d) % 4))
    for d in range(1, 4):
        remote(meta_s, metas_s.at[me], metasem.at[0], metasem.at[1], (lat, (ch + d) % 4))
        remote(meta_s, metas_s.at[me], metasem.at[0], metasem.at[1], (group * 4 + (zlo + d) % 4, ch))
    remote(wq_ref.at[:, sixteenth], w_s.at[pl.ds(ch * 4, 3), sixteenth], w1sem.at[0], w1sem.at[1], (lat, across))
    remote(wo_ref.at[sixteenth], w_s.at[ch * 4 + 3, sixteenth], w1sem.at[0], w1sem.at[1], (lat, across))
    remote(wq_ref, w_s.at[pl.ds(ch * 4, 3)], wbsem.at[0], wbsem.at[1], (lat, sib))
    remote(wo_ref, w_s.at[ch * 4 + 3], wbsem.at[0], wbsem.at[1], (lat, sib))
    own = [
        pltpu.make_async_copy(meta_s, metas_s.at[me], lsem.at[2]),
        pltpu.make_async_copy(wq_ref, w_s.at[pl.ds(ch * 4, 3)], lsem.at[3]),
        pltpu.make_async_copy(wo_ref, w_s.at[ch * 4 + 3], lsem.at[4]),
    ]
    for copy in own:
        copy.start()

    def move(w, pair, start):
        s = win_start(w)
        src, dst = pair * OCT, 1 + 2 * zlo + pair

        def piece(at, n, to, sem):
            start(x_s.at[pl.ds(src + at, n)], win_s.at[dst, ch, pl.ds(to, n)], sem)

        @pl.when(w == 0)
        def _():
            piece(0, 12, 1, 0)
            piece(OCT - 1, 1, 0, 1)

        @pl.when(w == 15)
        def _():
            piece(s - 1, 13, 0, 0)
            piece(0, 1, 13, 1)

        pl.when((w % 4 == 3) & (w != 15))(lambda: piece(s - 1, 14, 0, 0))
        pl.when((w % 4 != 3) & (w != 0))(lambda: piece(s - 1, 13, 0, 0))

    def to(pair, ss, rs, dz, dc):
        z = ((ch // 2) * 4 + zlo + dz) % 8
        w = (z % 4) * 4 + (z // 4) * 2 + (ch + dc) % 2
        move(w, pair, lambda a, b, n: remote(a, b, ss, rs, ring_dev(w, group)))

    def near(pair, ss, rs):
        def one(t):
            u = t // 2
            dz = jnp.where(u == 4, 0, jnp.where(u % 2 == 0, u // 2 + 1, 7 - u // 2))
            to(pair, ss, rs, dz, jnp.where(t == 8, 1, t % 2))

        loop(0, 9, one)

    def far(pair, ss, rs):
        def one(t):
            u = t // 2
            to(pair, ss, rs, jnp.where(u == 0, 3, jnp.where(u == 1, 5, 4)), t % 2)

        loop(0, 6, one)

    for pair in range(2):
        move(me, pair, lambda a, b, n, pair=pair: pltpu.make_async_copy(a, b, fsem.at[pair * 2 + n]).start())
    urgent = jnp.where(zlo == 3, 1, 0)
    first = (urgent, ssem.at[0], usem.at[jnp.where(zlo == 0, 1, jnp.where(zlo == 3, 2, 0))])
    second = (1 - urgent, ssem.at[1], nsem)
    near(*first)
    far(*first)

    tables(tab_s, t16_s)
    wait_bytes(stat_s.at[pl.ds(0, 3)], statsem.at[1])
    scale = lax.rsqrt((stat_s[0] + stat_s[1] + stat_s[2] + stat_s[3]) * (1.0 / 512.0) + EPS)
    theta = ((lat * 4 + lax.broadcasted_iota(jnp.int32, (4, 128), 0)).astype(F32) + 0.5) * (math.pi / NLAT)
    weight = jnp.sin(theta) * (math.pi / NLAT * 2.0 * math.pi / NLON) * gain
    freq = []
    for r in range(4):
        lhs = (tab_s[...] * scale[r : r + 1, :]).astype(BF)
        out = jnp.dot(lhs, f_ref[r], preferred_element_type=F32)
        freq.append((out * weight[r : r + 1, :]).astype(BF))
    out = jnp.dot(sort_rows(), jnp.concatenate(freq, axis=0), preferred_element_type=F32)
    send1_s[...] = out.astype(BF).reshape(64, 16, 128)
    loop(1, 64, lambda d: remote(send1_s.at[(lat + d) % 64], got_s.at[lat], a1sem.at[0], a1sem.at[1], ((lat + d) % 64, ch)))
    got_s[lat] = send1_s[lat]

    near(*second)

    wait_bytes(w_s.at[pl.ds(across * 4, 4), sixteenth], w1sem.at[1])
    strip = w_s.at[pl.ds(across * 4, 4), sixteenth]
    for d in range(1, 4):
        remote(strip, strip, wxsem.at[0], wxsem.at[1], (lat - group % 4 * 4 + (group + d) % 4 * 4, ch))
    legendre(lat, leg_s, e_s)
    part = w_s.at[pl.ds(across * 4, 4), quarter]
    wait_bytes(w_s.at[pl.ds(0, 3), pl.ds(0, 128)], wxsem.at[1])
    remote(part, part, w2sem.at[0], w2sem.at[1], (lat, sib))
    for d in range(1, 4):
        remote(part, part, w2sem.at[0], w2sem.at[1], ((lat + 16 * d) % 64, ch))
        remote(part, part, w2sem.at[0], w2sem.at[1], ((lat + 16 * d) % 64, sib))

    for n in range(2):
        move(me, n, lambda a, b, part, n=n: wait_bytes(b, fsem.at[n * 2 + part]))

    def arrived(own_here, full, sem):
        for n in (full - 1, full):
            this = own_here if n < full else jnp.logical_not(own_here)
            pl.when(this & wide)(lambda n=n: wait_bytes(win_s.at[pl.ds(0, n), 0], sem))
            pl.when(this & jnp.logical_not(wide))(
                lambda n=n: wait_bytes(win_s.at[pl.ds(0, n), 0, pl.ds(0, 13)], sem)
            )

    arrived(zlo == 0, 4, usem.at[1])
    arrived(zlo == 3, 4, usem.at[2])
    pl.when(has_next)(lambda: remote(win_s.at[8], win_s.at[0], hsem.at[0], hsem.at[1], ((lat + 4) % 64, ch)))
    pl.when(has_prev)(lambda: remote(win_s.at[1], win_s.at[9], hsem.at[2], hsem.at[3], ((lat + 60) % 64, ch)))

    far(*second)


    for copy in own:
        copy.wait()
    wait_bytes(metas_s.at[pl.ds(0, 6)], metasem.at[1])
    lane = lax.broadcasted_iota(jnp.int32, (32, KEYS), 1)
    query = lax.broadcasted_iota(jnp.int32, (32, KEYS), 0)
    row_of = sum((lane >= KB * a).astype(jnp.int32) for a in range(1, 5))
    delta = lane - KB * row_of - query - 8
    dist = jnp.abs(delta).astype(F32)
    lane8 = lax.broadcasted_iota(jnp.int32, (8, KEYS), 1)
    row8 = sum((lane8 >= KB * a).astype(jnp.int32) for a in range(1, 5))
    onto = (row8 == lax.broadcasted_iota(jnp.int32, (8, KEYS), 0)).astype(F32)
    for h in range(8):
        mine = metas_s[zlo * 4 + h // 2, (h % 2) * 8 : (h % 2) * 8 + 8, :]
        vec = lax.dot_general(mine, onto, TN, precision=lax.Precision.HIGHEST, preferred_element_type=F32)
        tile = jnp.full((32, KEYS), NEG, F32)
        for b in range(17):
            tile = jnp.where(delta == b - 8, vec[b : b + 1, :] * LOG2E, tile)
        b_s[h // 2, (h % 2) * 32 : (h % 2) * 32 + 32, :] = tile
    lane128 = lax.broadcasted_iota(jnp.int32, (128, KEYS), 1)
    row128 = sum((lane128 >= KB * a).astype(jnp.int32) for a in range(1, 5))
    pick = (row128 == lax.broadcasted_iota(jnp.int32, (128, KEYS), 0)).astype(F32)
    for z in range(4):
        r_s[z * 8 : z * 8 + 8, :] = jnp.dot(metas_s[z * 4 + ch, 16:24, :], pick, preferred_element_type=F32)

    def weights(t):
        return jnp.concatenate([w_s[k * 4 + t] for k in range(4)], axis=1)

    def project(pair, inner):
        parts = []
        for k in range(4):
            p = win_s[pair, k].astype(F32).reshape(14, 2, 8, 128)
            parts.append(jnp.concatenate([p[:, r].reshape(112, 128) for r in range(2)], axis=0))
        square = jnp.sum(sum(p * p for p in parts), axis=1, keepdims=True)
        scale = lax.rsqrt(square * (1.0 / 512.0) + EPS)
        normed = jnp.concatenate(
            [(p * scale * metas_s[zlo * 4 + k, 20:21, :]).astype(BF) for k, p in enumerate(parts)], axis=1
        )
        rows = pl.ds(pair * 2, 2)
        for t, dst, lo, n in ((0, q_s, 8, 96), (1, k_s, 0, 112), (2, v_s, 0, 112)):
            if t == 0 and not inner:
                continue
            out = jnp.dot(normed, weights(t), preferred_element_type=F32).reshape(2, 112, 512)[:, lo : lo + n, :]
            if t == 0:
                out = out * (LOG2E / 8.0)
            dst[rows] = out.astype(BF)

    wait_bytes(w_s.at[pl.ds(0, 4)], wbsem.at[1])
    wait_bytes(w_s.at[pl.ds(0, 7)], w2sem.at[1])
    arrived((zlo == 1) | (zlo == 2), 8, usem.at[0])
    loop(0, 4, lambda i: project(1 + 2 * i + i // 3, True))

    pl.when(wide)(lambda: wait_bytes(win_s.at[pl.ds(0, 5), pl.ds(0, 3)], nsem))
    pl.when(jnp.logical_not(wide))(lambda: wait_bytes(win_s.at[pl.ds(0, 5), pl.ds(0, 3), pl.ds(0, 13)], nsem))
    pl.when(has_prev)(lambda: wait_bytes(win_s.at[0], hsem.at[1]))
    pl.when(has_next)(lambda: wait_bytes(win_s.at[0], hsem.at[3]))
    loop(0, 2, lambda i: project(2 * zlo + i * jnp.where(zlo == 3, 1, 2), True))

    left = lax.broadcasted_iota(jnp.int32, (32, 128), 1) < 64
    blocks = [(j, hp) for j in range(3) for hp in range(4)]
    lane1 = row_of[0:1, :]

    def attend_row(i):
        at = group * 16 + i - 2 + lane1
        inside = (at >= 0) & (at < NLAT)
        reach = jnp.where(inside, r_s[pl.ds((i // 4) * 8 + i % 4, 1), :], -1.0)
        allowed = dist <= reach
        for hp in range(4):
            t_s[hp, 0:32, :] = jnp.where(allowed, b_s[hp, 0:32, :], NEG)
            t_s[hp, 32:64, :] = jnp.where(allowed, b_s[hp, 32:64, :], NEG)
        for n, (j, hp) in enumerate(blocks):
            cols = slice(hp * 128, hp * 128 + 128)
            qb = q_s[i + 2, j * 32 : j * 32 + 32, cols]
            zero = jnp.zeros_like(qb)
            qq = jnp.concatenate([jnp.where(left, qb, zero), jnp.where(left, zero, qb)], axis=0)
            kb = k_s[pl.ds(i, 5), j * 32 : j * 32 + KB, cols].reshape(KEYS, 128)
            s_s[n] = lax.dot_general(qq, kb, NT, preferred_element_type=F32) + t_s[hp]
        for n in range(12):
            s = s_s[n]
            p = jnp.exp2(s - jnp.max(s, axis=1, keepdims=True))
            l_s[n] = jnp.broadcast_to(jnp.sum(p, axis=1, keepdims=True), (64, 128))
            p_s[n] = p.astype(BF)
        for n, (j, hp) in enumerate(blocks):
            cols = slice(hp * 128, hp * 128 + 128)
            vb = v_s[pl.ds(i, 5), j * 32 : j * 32 + KB, cols].reshape(KEYS, 128)
            o = jnp.dot(p_s[n], vb, preferred_element_type=F32) / l_s[n]
            a_s[i % 2, j * 32 : j * 32 + 32, cols] = jnp.where(left, o[:32], o[32:]).astype(BF)

    s = win_start(me)

    def rows_of(step):
        pair = (2 * zlo + step) % 8
        loop(0, 2, lambda r: attend_row(pair * 2 + r))
        out = jnp.dot(a_s[...].reshape(192, 512), weights(3), preferred_element_type=F32).reshape(2, 12, 8, 512)
        for k in range(4):
            both = jnp.stack([out[b, :, :, k * 128 : k * 128 + 128] for b in range(2)], axis=1)
            y_s[pair, k] = both.reshape(12, 16, 128).astype(BF)

        def give(k, n, start):
            start(y_s.at[pair, k, pl.ds(0, n)], local_s.at[pair % 2, pl.ds(s, n)])

        def both(k, start):
            pl.when(wide)(lambda: give(k, 12, start))
            pl.when(jnp.logical_not(wide))(lambda: give(k, 11, start))

        for d in range(1, 4):
            k = (ch + d) % 4
            both(k, lambda a, b, k=k: remote(a, b, bsem.at[0], bsem.at[1], (group * 4 + pair // 2, k)))
        if isinstance(step, int):
            both(ch, lambda a, b: pltpu.make_async_copy(a, b, lsem.at[5 + step]).start())
        else:
            both(ch, lambda a, b: remote(a, b, bsem.at[0], bsem.at[1], (group * 4 + pair // 2, ch)))

    wait_bytes(got_s.at[pl.ds(0, 63)], a1sem.at[1])
    coef = jnp.dot(e_s[...], got_s[...].reshape(1024, 128), preferred_element_type=F32)
    coef = coef.reshape(3, DEG, 128) * mg_ref[...][None]
    g_s[ch] = coef.reshape(3 * DEG, 128).astype(BF)
    remote(g_s.at[ch], g_s.at[ch], gsem.at[0], gsem.at[1], (lat, across))
    remote(g_s.at[ch], g_s.at[ch], gsem.at[2], gsem.at[3], (lat, sib))

    rows_of(0)
    loop(0, 3, lambda i: project(jnp.where(i < zlo, 2 * i, jnp.where(i == 2, 7, 4 + 2 * i)), True))
    project(9, False)
    rows_of(1)
    wait_bytes(g_s.at[0], gsem.at[1])
    remote(g_s.at[across], g_s.at[across], gsem.at[2], gsem.at[3], (lat, sib))
    loop(2, 5, rows_of)
    wait_bytes(g_s.at[pl.ds(0, 2)], gsem.at[3])
    gained = jnp.concatenate([g_s[k] for k in range(4)], axis=1)
    mixed = jnp.dot(gained, ws_ref[...].astype(BF), preferred_element_type=F32)
    parts = []
    for k in range(3):
        twice = jnp.where((lat + 64 * k) % DEG == 0, 1.0, 2.0).astype(F32)
        parts.append((mixed[k * DEG : k * DEG + DEG] * twice).astype(BF))
    rows_out = lax.dot_general(e_s[...], jnp.concatenate(parts, axis=0), TN, preferred_element_type=F32)
    send2_s[...] = rows_out.astype(BF).reshape(64, 16, 128)
    loop(1, 64, lambda d: remote(send2_s.at[(lat + d) % 64], got2_s.at[lat], a2sem.at[0], a2sem.at[1], ((lat + d) % 64, ch)))
    got2_s[lat] = send2_s[lat]

    loop(5, 8, rows_of)

    wait_bytes(got2_s.at[pl.ds(0, 63)], a2sem.at[1])
    modes = lax.dot_general(sort_rows(), got2_s[...].reshape(1024, 128), TN, preferred_element_type=F32).astype(BF)
    for r in range(4):
        wave_s[r] = lax.dot_general(t16_s[...], modes[r * 192 : r * 192 + 192], TN, preferred_element_type=F32)

    wait_bytes(stat_s.at[pl.ds(0, 3)], statsem.at[0])
    wait_bytes(metas_s.at[pl.ds(0, 6)], metasem.at[0])
    wait_bytes(strip, w1sem.at[0])
    wait_bytes(w_s.at[pl.ds(0, 3), pl.ds(0, 128)], wxsem.at[0])
    wait_bytes(w_s.at[pl.ds(0, 4)], wbsem.at[0])
    wait_bytes(w_s.at[pl.ds(0, 7)], w2sem.at[0])
    for n in range(2):
        pl.when(wide)(lambda n=n: wait_bytes(x_s.at[pl.ds(0, 198)], ssem.at[n]))
        pl.when(jnp.logical_not(wide))(lambda n=n: wait_bytes(x_s.at[pl.ds(0, 199)], ssem.at[n]))
    pl.when(has_next)(lambda: wait_bytes(win_s.at[0], hsem.at[0]))
    pl.when(has_prev)(lambda: wait_bytes(win_s.at[0], hsem.at[2]))
    wait_bytes(got_s.at[pl.ds(0, 63)], a1sem.at[0])
    wait_bytes(g_s.at[0], gsem.at[0])
    wait_bytes(g_s.at[pl.ds(0, 2)], gsem.at[2])
    wait_bytes(got2_s.at[pl.ds(0, 63)], a2sem.at[0])

    def last(n):
        wait_bytes(local_s.at[0, pl.ds(0, n)], lsem.at[5])
        wait_bytes(local_s.at[0, pl.ds(0, n)], lsem.at[6])
        wait_bytes(local_s.at[:, pl.ds(0, 15 * n)], bsem.at[0])
        wait_bytes(local_s.at[:, pl.ds(0, OCT - n)], bsem.at[1])

    pl.when(wide)(lambda: last(12))
    pl.when(jnp.logical_not(wide))(lambda: last(11))

    def total(c):
        lon = pl.ds(pl.multiple_of(c * 144, 16), 144)
        for a in range(2):
            part = local_s[a, pl.ds(c * 18, 18)].astype(F32).reshape(18, 2, 8, 128)
            for b in range(2):
                out_ref[2 * a + b, lon, :] = (wave_s[2 * a + b, lon, :] + part[:, b].reshape(144, 128)).astype(BF)

    loop(0, 10, total)


def layer(*args):
    shape = jax.ShapeDtypeStruct
    vm = pltpu.VMEM
    return pl.pallas_call(
        layer_kernel,
        out_shape=shape((4, NLON, 128), BF),
        in_specs=[VMEM] * 8,
        out_specs=VMEM,
        scratch_shapes=[
            vm((2 * OCT, 16, 128), BF),
            vm((10, 4, 14, 16, 128), BF),
            vm((16, 512, 128), BF),
            vm((24, 128), F32),
            vm((16, 24, 128), F32),
            vm((4, 4, NLON), F32),
            vm((2 * DEG, NLON), F32),
            vm((DEG, 8, 128), F32),
            vm((3 * DEG, 1024), BF),
            vm((64, 16, 128), BF),
            vm((64, 16, 128), BF),
            vm((4, 3 * DEG, 128), BF),
            vm((64, 16, 128), BF),
            vm((20, 96, 512), BF),
            vm((20, 112, 512), BF),
            vm((20, 112, 512), BF),
            vm((4, 64, KEYS), F32),
            vm((4, 64, KEYS), F32),
            vm((2, 96, 512), BF),
            vm((12, 64, KEYS), F32),
            vm((12, 64, KEYS), BF),
            vm((12, 64, 128), F32),
            vm((32, KEYS), F32),
            vm((8, 4, 12, 16, 128), BF),
            vm((64, 16, 128), BF),
            vm((2, OCT, 16, 128), BF),
            vm((2 * DEG, NLON), BF),
            vm((4, NLON, 128), F32),
            DMA((7,)), DMA((4,)), DMA((2,)), DMA((2,)), DMA((2,)), DMA((2,)), DMA((2,)), DMA((2,)), DMA((2,)), DMA((3,)), DMA,
            DMA((4,)), DMA((2,)), DMA((2,)), DMA((4,)), DMA((2,)),
        ],
        compiler_params=pltpu.CompilerParams(
            collective_id=0, has_side_effects=True, vmem_limit_bytes=56 * 1024 * 1024
        ),
        name="layer",
    )(*args)


def per_device(fields, norm_gain, w_qkv, w_out, rel_bias, stencil_reach, mode_gain, w_spec):
    return layer(
        fields,
        norm_gain.reshape(1, 128),
        jnp.transpose(w_qkv, (1, 0, 2)),
        w_out,
        jnp.transpose(rel_bias, (1, 0, 2)),
        stencil_reach,
        mode_gain,
        w_spec,
    )


def solution(mesh):
    in_specs = (
        P("lat", None, "ch"),
        P("ch"),
        P(None, None, "ch"),
        P(None, "ch"),
        P("ch", None, None),
        P("lat", None),
        P(None, "ch"),
        P(None, "ch"),
    )
    return jax.shard_map(
        per_device, mesh=mesh, in_specs=in_specs, out_specs=P("lat", None, "ch"), check_vma=False
    )
```

```python
import math

import jax
import jax.numpy as jnp
from jax import lax
from jax.experimental import pallas as pl
from jax.experimental.pallas import tpu as pltpu
from jax.sharding import PartitionSpec as P

MESH = pl.DeviceIdType.MESH
NLON = 1440
NLAT = 256
DEG = 96
OCT = 180
LOG2E = 1.4426950408889634
NEG = -1e30
EPS = 1e-05
KB = 48
KEYS = 5 * KB
F32 = jnp.float32
BF = jnp.bfloat16
DMA = pltpu.SemaphoreType.DMA
VMEM = pl.BlockSpec(memory_space=pltpu.VMEM)
TN = (((0,), (0,)), ((), ()))
NT = (((1,), (1,)), ((), ()))


def win_start(w):
    return 45 * w // 4


def ring_dev(w, group):
    return (group * 4 + w // 4, w % 4)


def place():
    lat = lax.axis_index("lat")
    ch = lax.axis_index("ch")
    return lat, ch, lat // 4, lat % 4


def signal(device):
    pl.semaphore_signal(pltpu.get_barrier_semaphore(), inc=1, device_id=device, device_id_type=MESH)


def remote(src, dst, ss, rs, device):
    pltpu.make_async_remote_copy(
        src_ref=src, dst_ref=dst, send_sem=ss, recv_sem=rs, device_id=device, device_id_type=MESH
    ).start()


def wait_bytes(ref, sem):
    pltpu.make_async_copy(ref, ref, sem).wait()


def loop(lo, hi, body):
    def step(i, c):
        body(i)
        return c

    lax.fori_loop(lo, hi, step, 0)


def sort_rows():
    n = lax.broadcasted_iota(jnp.int32, (1024, 1), 0)
    slot = n % 16
    source = jnp.where(slot < 12, (slot % 4) * 192 + (slot // 4) * 64 + n // 16, -1)
    return (lax.broadcasted_iota(jnp.int32, (1024, 768), 1) == source).astype(F32).astype(BF)


def tables(tab_s, t_ref):
    row = lax.broadcasted_iota(jnp.int32, (2 * DEG, 128), 0)
    lane = lax.broadcasted_iota(jnp.int32, (2 * DEG, 128), 1).astype(F32)
    first = row < DEG
    order = jnp.where(first, row, row - DEG).astype(F32)

    def angle(cells):
        turns = cells * order
        turns = turns - NLON * jnp.floor((turns + 0.5) * (1.0 / NLON))
        return turns * (2.0 * math.pi / NLON)

    coarse, fine = angle(jnp.where(lane < 12, lane * 128.0, 0.0)), angle(lane)
    ca, sa, cb, sb = jnp.cos(coarse), jnp.sin(coarse), jnp.cos(fine), jnp.sin(fine)
    u = jnp.where(first, cb, -sb)
    v = jnp.where(first, -sb, -cb)
    for a in range(12):
        n = min(128, NLON - a * 128)
        tab = ca[:, a : a + 1] * u + sa[:, a : a + 1] * v
        tab_s[:, a * 128 : a * 128 + n] = tab[:, :n]
        t_ref[:, a * 128 : a * 128 + n] = tab[:, :n].astype(BF)


def legendre(lat, leg_s, e_s):
    lane = lax.broadcasted_iota(jnp.int32, (8, 128), 1)
    n = lax.broadcasted_iota(jnp.int32, (8, 128), 0) * 128 + lane
    kind = (n % 16) // 4
    row = (n // 16) * 4 + n % 4
    theta = (row.astype(F32) + 0.5) * (math.pi / NLAT)
    factor = lax.broadcasted_iota(jnp.int32, (1, 128), 1)
    number = jnp.maximum(factor, 1).astype(F32)
    log_ratio = jnp.log((2.0 * number - 1.0) / (2.0 * number))
    m = jnp.zeros((8, 128), F32)
    begin = jnp.zeros((8, 128), F32)
    for k in range(3):
        order = (lat + 64 * k) % DEG
        total = jnp.sum(jnp.where((factor >= 1) & (factor <= order), log_ratio, 0.0), axis=1, keepdims=True)
        m = jnp.where(kind == k, order.astype(F32), m)
        begin = jnp.where(kind == k, total, begin)
    begin = 0.5 * (begin + jnp.log((2.0 * m + 1.0) / (4.0 * math.pi)))
    diagonal = jnp.where(kind < 3, jnp.exp(begin + m * jnp.log(jnp.sin(theta))), 0.0)
    cosine = jnp.cos(theta)

    def degree(l, carry):
        previous, earlier = carry
        deg = l.astype(F32)
        less = deg - 1.0
        upper = jnp.sqrt(jnp.maximum(4.0 * deg * deg - 1.0, 0.0) / jnp.maximum(deg * deg - m * m, 1.0))
        lower = jnp.sqrt(jnp.maximum(less * less - m * m, 0.0) / jnp.maximum(4.0 * less * less - 1.0, 1.0))
        value = upper * (cosine * previous - lower * earlier)
        current = jnp.where(m == deg, diagonal, jnp.where(m < deg, value, 0.0))
        leg_s[l] = current
        return current, previous

    zero = diagonal * 0.0
    lax.fori_loop(0, DEG, degree, (zero, zero))
    kind = (lax.broadcasted_iota(jnp.int32, (DEG, 128), 1) % 16) // 4
    for c in range(8):
        part = leg_s[:, c, :]
        for k in range(3):
            e_s[k * DEG : k * DEG + DEG, c * 128 : c * 128 + 128] = jnp.where(kind == k, part, 0.0).astype(BF)


def layer_kernel(
    f_ref, gain_ref, wq_ref, wo_ref, bias_ref, reach_ref, mg_ref, ws_ref,
    out_ref,
    x_s, win_s, w_s, meta_s, metas_s, stat_s, tab_s, leg_s, e_s, send1_s, got_s, g_s, send2_s,
    q_s, k_s, v_s, b_s, t_s, a_s, s_s, p_s, l_s, r_s, y_s, got2_s, local_s, t16_s, wave_s,
    lsem, statsem, metasem, w1sem, wxsem, wbsem, w2sem, ssem, usem, nsem, hsem, a1sem, a2sem, gsem, bsem,
):
    lat, ch, group, zlo = place()
    me = zlo * 4 + ch
    has_next = group < 15
    has_prev = group > 0
    quarter = pl.ds(pl.multiple_of((group // 4) * 128, 128), 128)
    sixteenth = pl.ds(pl.multiple_of(group * 32, 32), 32)
    sib = ch + 1 - 2 * (ch % 2)
    across = (ch + 2) % 4
    loop(1, 64, lambda d: signal(((lat + d) % 64, ch)))
    for z in range(4):
        for d in range(1, 4):
            signal((group * 4 + z, (ch + d) % 4))
    for d in range(1, 4):
        signal(((lat + 16 * d) % 64, sib))

    gain = gain_ref[...].astype(F32)
    meta_s[...] = jnp.zeros_like(meta_s)
    for a in range(5):
        for h in range(2):
            meta_s[h * 8 + a : h * 8 + a + 1, 0:17] = bias_ref[a, h : h + 1, :]
    meta_s[16:20, 0:5] = reach_ref[...].astype(F32)
    meta_s[20:21, :] = gain

    def interleave(c):
        lon = pl.ds(pl.multiple_of(c * 144, 16), 144)
        for a in range(2):
            two = [f_ref[2 * a + b, lon, :].astype(F32).reshape(18, 8, 128) for b in range(2)]
            x_s[a, pl.ds(c * 18, 18)] = jnp.stack(two, axis=1).reshape(18, 16, 128).astype(BF)

    loop(0, 10, interleave)

    @pl.when(jnp.logical_not(has_prev))
    def _():
        win_s[0] = jnp.zeros_like(win_s[0])

    @pl.when(jnp.logical_not(has_next))
    def _():
        win_s[9] = jnp.zeros_like(win_s[9])

    pl.semaphore_wait(pltpu.get_barrier_semaphore(), 78)

    for d in range(1, 4):
        remote(meta_s, metas_s.at[me], metasem.at[0], metasem.at[1], (lat, (ch + d) % 4))
        remote(meta_s, metas_s.at[me], metasem.at[0], metasem.at[1], (group * 4 + (zlo + d) % 4, ch))
    remote(wq_ref.at[:, sixteenth], w_s.at[pl.ds(ch * 4, 3), sixteenth], w1sem.at[0], w1sem.at[1], (lat, across))
    remote(wo_ref.at[sixteenth], w_s.at[ch * 4 + 3, sixteenth], w1sem.at[0], w1sem.at[1], (lat, across))
    remote(wq_ref, w_s.at[pl.ds(ch * 4, 3)], wbsem.at[0], wbsem.at[1], (lat, sib))
    remote(wo_ref, w_s.at[ch * 4 + 3], wbsem.at[0], wbsem.at[1], (lat, sib))
    own = [
        pltpu.make_async_copy(meta_s, metas_s.at[me], lsem.at[2]),
        pltpu.make_async_copy(wq_ref, w_s.at[pl.ds(ch * 4, 3)], lsem.at[3]),
        pltpu.make_async_copy(wo_ref, w_s.at[ch * 4 + 3], lsem.at[4]),
    ]
    for copy in own:
        copy.start()

    def move(w, src_pair, pairs, dst_pair, start):
        s = win_start(w)
        src, dst = pl.ds(src_pair, pairs), pl.ds(dst_pair, pairs)
        edge = (w == 0) | (w == 15)

        @pl.when(edge)
        def _():
            a_src = jnp.where(w == 0, 0, s - 1)
            a_dst = jnp.where(w == 0, 1, 0)
            b_src = jnp.where(w == 0, OCT - 1, 0)
            b_dst = jnp.where(w == 0, 0, 13)
            start(x_s.at[src, pl.ds(a_src, 13)], win_s.at[dst, ch, pl.ds(a_dst, 13)], 0)
            start(x_s.at[src, pl.ds(b_src, 1)], win_s.at[dst, ch, pl.ds(b_dst, 1)], 1)

        @pl.when(jnp.logical_not(edge))
        def _():
            start(x_s.at[src, pl.ds(s - 1, 14)], win_s.at[dst, ch], 0)

    def to(pair, ss, rs, dz, dc):
        z = ((ch // 2) * 4 + zlo + dz) % 8
        w = (z % 4) * 4 + (z // 4) * 2 + (ch + dc) % 2
        move(w, pair, 1, 1 + 2 * zlo + pair, lambda a, b, n: remote(a, b, ss, rs, ring_dev(w, group)))

    def near(pair, ss, rs):
        def one(t):
            u = t // 2
            dz = jnp.where(u == 4, 0, jnp.where(u % 2 == 0, u // 2 + 1, 7 - u // 2))
            to(pair, ss, rs, dz, jnp.where(t == 8, 1, t % 2))

        loop(0, 9, one)

    def far(pair, ss, rs):
        def one(t):
            u = t // 2
            to(pair, ss, rs, jnp.where(u == 0, 3, jnp.where(u == 1, 5, 4)), t % 2)

        loop(0, 6, one)

    move(me, 0, 2, 1 + 2 * zlo, lambda a, b, n: pltpu.make_async_copy(a, b, lsem.at[n]).start())
    urgent = jnp.where(zlo == 3, 1, 0)
    first = (urgent, ssem.at[0], usem.at[jnp.where(zlo == 0, 1, jnp.where(zlo == 3, 2, 0))])
    second = (1 - urgent, ssem.at[1], nsem)
    near(*first)

    ones = jnp.ones((8, 256), BF)
    for r in range(4):
        x = f_ref[r].astype(F32)
        x = x * x
        high = x.astype(BF)
        both = jnp.concatenate([high, (x - high.astype(F32)).astype(BF)], axis=1)
        sums = lax.dot_general(ones, both, NT, preferred_element_type=F32)
        stat_s[ch, r : r + 1, :] = sums[0:1]
    for d in range(1, 4):
        remote(stat_s.at[ch], stat_s.at[ch], statsem.at[0], statsem.at[1], (lat, (ch + d) % 4))
    far(*first)

    tables(tab_s, t16_s)
    wait_bytes(stat_s.at[pl.ds(0, 3)], statsem.at[1])
    scale = lax.rsqrt((stat_s[0] + stat_s[1] + stat_s[2] + stat_s[3]) * (1.0 / 512.0) + EPS)
    theta = ((lat * 4 + lax.broadcasted_iota(jnp.int32, (4, 128), 0)).astype(F32) + 0.5) * (math.pi / NLAT)
    weight = jnp.sin(theta) * (math.pi / NLAT * 2.0 * math.pi / NLON) * gain
    freq = []
    for r in range(4):
        lhs = (tab_s[...] * scale[r : r + 1, :]).astype(BF)
        out = jnp.dot(lhs, f_ref[r], preferred_element_type=F32)
        freq.append((out * weight[r : r + 1, :]).astype(BF))
    out = jnp.dot(sort_rows(), jnp.concatenate(freq, axis=0), preferred_element_type=F32)
    send1_s[...] = out.astype(BF).reshape(64, 16, 128)
    loop(1, 64, lambda d: remote(send1_s.at[(lat + d) % 64], got_s.at[lat], a1sem.at[0], a1sem.at[1], ((lat + d) % 64, ch)))
    got_s[lat] = send1_s[lat]

    near(*second)

    wait_bytes(w_s.at[pl.ds(across * 4, 4), sixteenth], w1sem.at[1])
    strip = w_s.at[pl.ds(across * 4, 4), sixteenth]
    for d in range(1, 4):
        remote(strip, strip, wxsem.at[0], wxsem.at[1], (lat - group % 4 * 4 + (group + d) % 4 * 4, ch))
    legendre(lat, leg_s, e_s)
    part = w_s.at[pl.ds(across * 4, 4), quarter]
    wait_bytes(w_s.at[pl.ds(0, 3), pl.ds(0, 128)], wxsem.at[1])
    remote(part, part, w2sem.at[0], w2sem.at[1], (lat, sib))
    for d in range(1, 4):
        remote(part, part, w2sem.at[0], w2sem.at[1], ((lat + 16 * d) % 64, ch))
        remote(part, part, w2sem.at[0], w2sem.at[1], ((lat + 16 * d) % 64, sib))

    @pl.when((me == 0) | (me == 15))
    def _():
        wait_bytes(win_s.at[pl.ds(0, 2), 0, pl.ds(0, 13)], lsem.at[0])
        wait_bytes(win_s.at[pl.ds(0, 2), 0, pl.ds(0, 1)], lsem.at[1])

    @pl.when((me != 0) & (me != 15))
    def _():
        wait_bytes(win_s.at[pl.ds(0, 2), 0], lsem.at[0])

    def arrived(own_here, full, sem):
        pl.when(own_here)(lambda: wait_bytes(win_s.at[pl.ds(0, full - 1), 0], sem))
        pl.when(jnp.logical_not(own_here))(lambda: wait_bytes(win_s.at[pl.ds(0, full), 0], sem))

    arrived(zlo == 0, 4, usem.at[1])
    arrived(zlo == 3, 4, usem.at[2])
    pl.when(has_next)(lambda: remote(win_s.at[8], win_s.at[0], hsem.at[0], hsem.at[1], ((lat + 4) % 64, ch)))
    pl.when(has_prev)(lambda: remote(win_s.at[1], win_s.at[9], hsem.at[2], hsem.at[3], ((lat + 60) % 64, ch)))

    far(*second)


    for copy in own:
        copy.wait()
    wait_bytes(metas_s.at[pl.ds(0, 6)], metasem.at[1])
    lane = lax.broadcasted_iota(jnp.int32, (32, KEYS), 1)
    query = lax.broadcasted_iota(jnp.int32, (32, KEYS), 0)
    row_of = sum((lane >= KB * a).astype(jnp.int32) for a in range(1, 5))
    delta = lane - KB * row_of - query - 8
    dist = jnp.abs(delta).astype(F32)
    lane8 = lax.broadcasted_iota(jnp.int32, (8, KEYS), 1)
    row8 = sum((lane8 >= KB * a).astype(jnp.int32) for a in range(1, 5))
    onto = (row8 == lax.broadcasted_iota(jnp.int32, (8, KEYS), 0)).astype(F32)
    for h in range(8):
        mine = metas_s[zlo * 4 + h // 2, (h % 2) * 8 : (h % 2) * 8 + 8, :]
        vec = lax.dot_general(mine, onto, TN, precision=lax.Precision.HIGHEST, preferred_element_type=F32)
        tile = jnp.full((32, KEYS), NEG, F32)
        for b in range(17):
            tile = jnp.where(delta == b - 8, vec[b : b + 1, :] * LOG2E, tile)
        b_s[h // 2, (h % 2) * 32 : (h % 2) * 32 + 32, :] = tile
    lane128 = lax.broadcasted_iota(jnp.int32, (128, KEYS), 1)
    row128 = sum((lane128 >= KB * a).astype(jnp.int32) for a in range(1, 5))
    pick = (row128 == lax.broadcasted_iota(jnp.int32, (128, KEYS), 0)).astype(F32)
    for z in range(4):
        r_s[z * 8 : z * 8 + 8, :] = jnp.dot(metas_s[z * 4 + ch, 16:24, :], pick, preferred_element_type=F32)

    def weights(t):
        return jnp.concatenate([w_s[k * 4 + t] for k in range(4)], axis=1)

    def project(pair, inner):
        parts = []
        for k in range(4):
            p = win_s[pair, k].astype(F32).reshape(14, 2, 8, 128)
            parts.append(jnp.concatenate([p[:, r].reshape(112, 128) for r in range(2)], axis=0))
        square = jnp.sum(sum(p * p for p in parts), axis=1, keepdims=True)
        scale = lax.rsqrt(square * (1.0 / 512.0) + EPS)
        normed = jnp.concatenate(
            [(p * scale * metas_s[zlo * 4 + k, 20:21, :]).astype(BF) for k, p in enumerate(parts)], axis=1
        )
        rows = pl.ds(pair * 2, 2)
        for t, dst, lo, n in ((0, q_s, 8, 96), (1, k_s, 0, 112), (2, v_s, 0, 112)):
            if t == 0 and not inner:
                continue
            out = jnp.dot(normed, weights(t), preferred_element_type=F32).reshape(2, 112, 512)[:, lo : lo + n, :]
            if t == 0:
                out = out * (LOG2E / 8.0)
            dst[rows] = out.astype(BF)

    wait_bytes(w_s.at[pl.ds(0, 4)], wbsem.at[1])
    wait_bytes(w_s.at[pl.ds(0, 7)], w2sem.at[1])
    arrived((zlo == 1) | (zlo == 2), 8, usem.at[0])
    loop(0, 4, lambda i: project(1 + 2 * i + i // 3, True))

    wait_bytes(win_s.at[pl.ds(0, 5), pl.ds(0, 3)], nsem)
    pl.when(has_prev)(lambda: wait_bytes(win_s.at[0], hsem.at[1]))
    pl.when(has_next)(lambda: wait_bytes(win_s.at[0], hsem.at[3]))
    loop(0, 2, lambda i: project(2 * zlo + i * jnp.where(zlo == 3, 1, 2), True))

    left = lax.broadcasted_iota(jnp.int32, (32, 128), 1) < 64
    blocks = [(j, hp) for j in range(3) for hp in range(4)]
    lane1 = row_of[0:1, :]

    def attend_row(i):
        at = group * 16 + i - 2 + lane1
        inside = (at >= 0) & (at < NLAT)
        reach = jnp.where(inside, r_s[pl.ds((i // 4) * 8 + i % 4, 1), :], -1.0)
        allowed = dist <= reach
        for hp in range(4):
            t_s[hp, 0:32, :] = jnp.where(allowed, b_s[hp, 0:32, :], NEG)
            t_s[hp, 32:64, :] = jnp.where(allowed, b_s[hp, 32:64, :], NEG)
        for n, (j, hp) in enumerate(blocks):
            cols = slice(hp * 128, hp * 128 + 128)
            qb = q_s[i + 2, j * 32 : j * 32 + 32, cols]
            zero = jnp.zeros_like(qb)
            qq = jnp.concatenate([jnp.where(left, qb, zero), jnp.where(left, zero, qb)], axis=0)
            kb = k_s[pl.ds(i, 5), j * 32 : j * 32 + KB, cols].reshape(KEYS, 128)
            s_s[n] = lax.dot_general(qq, kb, NT, preferred_element_type=F32) + t_s[hp]
        for n in range(12):
            s = s_s[n]
            p = jnp.exp2(s - jnp.max(s, axis=1, keepdims=True))
            l_s[n] = jnp.broadcast_to(jnp.sum(p, axis=1, keepdims=True), (64, 128))
            p_s[n] = p.astype(BF)
        for n, (j, hp) in enumerate(blocks):
            cols = slice(hp * 128, hp * 128 + 128)
            vb = v_s[pl.ds(i, 5), j * 32 : j * 32 + KB, cols].reshape(KEYS, 128)
            o = jnp.dot(p_s[n], vb, preferred_element_type=F32) / l_s[n]
            a_s[i % 2, j * 32 : j * 32 + 32, cols] = jnp.where(left, o[:32], o[32:]).astype(BF)

    s = win_start(me)
    wide = win_start(me + 1) - s == 12

    def rows_of(step):
        pair = (2 * zlo + step) % 8
        loop(0, 2, lambda r: attend_row(pair * 2 + r))
        out = jnp.dot(a_s[...].reshape(192, 512), weights(3), preferred_element_type=F32).reshape(2, 12, 8, 512)
        for k in range(4):
            both = jnp.stack([out[b, :, :, k * 128 : k * 128 + 128] for b in range(2)], axis=1)
            y_s[pair, k] = both.reshape(12, 16, 128).astype(BF)

        def give(k, n, start):
            start(y_s.at[pair, k, pl.ds(0, n)], local_s.at[pair % 2, pl.ds(s, n)])

        def both(k, start):
            pl.when(wide)(lambda: give(k, 12, start))
            pl.when(jnp.logical_not(wide))(lambda: give(k, 11, start))

        for d in range(1, 4):
            k = (ch + d) % 4
            both(k, lambda a, b, k=k: remote(a, b, bsem.at[0], bsem.at[1], (group * 4 + pair // 2, k)))
        if isinstance(step, int):
            both(ch, lambda a, b: pltpu.make_async_copy(a, b, lsem.at[5 + step]).start())
        else:
            both(ch, lambda a, b: remote(a, b, bsem.at[0], bsem.at[1], (group * 4 + pair // 2, ch)))

    wait_bytes(got_s.at[pl.ds(0, 63)], a1sem.at[1])
    coef = jnp.dot(e_s[...], got_s[...].reshape(1024, 128), preferred_element_type=F32)
    coef = coef.reshape(3, DEG, 128) * mg_ref[...][None]
    g_s[ch] = coef.reshape(3 * DEG, 128).astype(BF)
    remote(g_s.at[ch], g_s.at[ch], gsem.at[0], gsem.at[1], (lat, across))
    remote(g_s.at[ch], g_s.at[ch], gsem.at[2], gsem.at[3], (lat, sib))

    rows_of(0)
    loop(0, 3, lambda i: project(jnp.where(i < zlo, 2 * i, jnp.where(i == 2, 7, 4 + 2 * i)), True))
    project(9, False)
    rows_of(1)
    wait_bytes(g_s.at[0], gsem.at[1])
    remote(g_s.at[across], g_s.at[across], gsem.at[2], gsem.at[3], (lat, sib))
    loop(2, 5, rows_of)
    wait_bytes(g_s.at[pl.ds(0, 2)], gsem.at[3])
    gained = jnp.concatenate([g_s[k] for k in range(4)], axis=1)
    mixed = jnp.dot(gained, ws_ref[...].astype(BF), preferred_element_type=F32)
    parts = []
    for k in range(3):
        twice = jnp.where((lat + 64 * k) % DEG == 0, 1.0, 2.0).astype(F32)
        parts.append((mixed[k * DEG : k * DEG + DEG] * twice).astype(BF))
    rows_out = lax.dot_general(e_s[...], jnp.concatenate(parts, axis=0), TN, preferred_element_type=F32)
    send2_s[...] = rows_out.astype(BF).reshape(64, 16, 128)
    loop(1, 64, lambda d: remote(send2_s.at[(lat + d) % 64], got2_s.at[lat], a2sem.at[0], a2sem.at[1], ((lat + d) % 64, ch)))
    got2_s[lat] = send2_s[lat]

    loop(5, 8, rows_of)

    wait_bytes(got2_s.at[pl.ds(0, 63)], a2sem.at[1])
    modes = lax.dot_general(sort_rows(), got2_s[...].reshape(1024, 128), TN, preferred_element_type=F32).astype(BF)
    for r in range(4):
        wave_s[r] = lax.dot_general(t16_s[...], modes[r * 192 : r * 192 + 192], TN, preferred_element_type=F32)

    wait_bytes(stat_s.at[pl.ds(0, 3)], statsem.at[0])
    wait_bytes(metas_s.at[pl.ds(0, 6)], metasem.at[0])
    wait_bytes(strip, w1sem.at[0])
    wait_bytes(w_s.at[pl.ds(0, 3), pl.ds(0, 128)], wxsem.at[0])
    wait_bytes(w_s.at[pl.ds(0, 4)], wbsem.at[0])
    wait_bytes(w_s.at[pl.ds(0, 7)], w2sem.at[0])
    wait_bytes(win_s.at[pl.ds(0, 5), pl.ds(0, 3)], ssem.at[0])
    wait_bytes(win_s.at[pl.ds(0, 5), pl.ds(0, 3)], ssem.at[1])
    pl.when(has_next)(lambda: wait_bytes(win_s.at[0], hsem.at[0]))
    pl.when(has_prev)(lambda: wait_bytes(win_s.at[0], hsem.at[2]))
    wait_bytes(got_s.at[pl.ds(0, 63)], a1sem.at[0])
    wait_bytes(g_s.at[0], gsem.at[0])
    wait_bytes(g_s.at[pl.ds(0, 2)], gsem.at[2])
    wait_bytes(got2_s.at[pl.ds(0, 63)], a2sem.at[0])

    def last(n):
        wait_bytes(local_s.at[0, pl.ds(0, n)], lsem.at[5])
        wait_bytes(local_s.at[0, pl.ds(0, n)], lsem.at[6])
        wait_bytes(local_s.at[:, pl.ds(0, 15 * n)], bsem.at[0])
        wait_bytes(local_s.at[:, pl.ds(0, OCT - n)], bsem.at[1])

    pl.when(wide)(lambda: last(12))
    pl.when(jnp.logical_not(wide))(lambda: last(11))

    def total(c):
        lon = pl.ds(pl.multiple_of(c * 144, 16), 144)
        for a in range(2):
            part = local_s[a, pl.ds(c * 18, 18)].astype(F32).reshape(18, 2, 8, 128)
            for b in range(2):
                out_ref[2 * a + b, lon, :] = (wave_s[2 * a + b, lon, :] + part[:, b].reshape(144, 128)).astype(BF)

    loop(0, 10, total)


def layer(*args):
    shape = jax.ShapeDtypeStruct
    vm = pltpu.VMEM
    return pl.pallas_call(
        layer_kernel,
        out_shape=shape((4, NLON, 128), BF),
        in_specs=[VMEM] * 8,
        out_specs=VMEM,
        scratch_shapes=[
            vm((2, OCT, 16, 128), BF),
            vm((10, 4, 14, 16, 128), BF),
            vm((16, 512, 128), BF),
            vm((24, 128), F32),
            vm((16, 24, 128), F32),
            vm((4, 4, NLON), F32),
            vm((2 * DEG, NLON), F32),
            vm((DEG, 8, 128), F32),
            vm((3 * DEG, 1024), BF),
            vm((64, 16, 128), BF),
            vm((64, 16, 128), BF),
            vm((4, 3 * DEG, 128), BF),
            vm((64, 16, 128), BF),
            vm((20, 96, 512), BF),
            vm((20, 112, 512), BF),
            vm((20, 112, 512), BF),
            vm((4, 64, KEYS), F32),
            vm((4, 64, KEYS), F32),
            vm((2, 96, 512), BF),
            vm((12, 64, KEYS), F32),
            vm((12, 64, KEYS), BF),
            vm((12, 64, 128), F32),
            vm((32, KEYS), F32),
            vm((8, 4, 12, 16, 128), BF),
            vm((64, 16, 128), BF),
            vm((2, OCT, 16, 128), BF),
            vm((2 * DEG, NLON), BF),
            vm((4, NLON, 128), F32),
            DMA((7,)), DMA((2,)), DMA((2,)), DMA((2,)), DMA((2,)), DMA((2,)), DMA((2,)), DMA((2,)), DMA((3,)), DMA,
            DMA((4,)), DMA((2,)), DMA((2,)), DMA((4,)), DMA((2,)),
        ],
        compiler_params=pltpu.CompilerParams(
            collective_id=0, has_side_effects=True, vmem_limit_bytes=56 * 1024 * 1024
        ),
        name="layer",
    )(*args)


def per_device(fields, norm_gain, w_qkv, w_out, rel_bias, stencil_reach, mode_gain, w_spec):
    return layer(
        fields,
        norm_gain.reshape(1, 128),
        jnp.transpose(w_qkv, (1, 0, 2)),
        w_out,
        jnp.transpose(rel_bias, (1, 0, 2)),
        stencil_reach,
        mode_gain,
        w_spec,
    )


def solution(mesh):
    in_specs = (
        P("lat", None, "ch"),
        P("ch"),
        P(None, None, "ch"),
        P(None, "ch"),
        P("ch", None, None),
        P("lat", None),
        P(None, "ch"),
        P(None, "ch"),
    )
    return jax.shard_map(
        per_device, mesh=mesh, in_specs=in_specs, out_specs=P("lat", None, "ch"), check_vma=False
    )
```

```python
import math

import jax
import jax.numpy as jnp
from jax import lax
from jax.experimental import pallas as pl
from jax.experimental.pallas import tpu as pltpu
from jax.sharding import PartitionSpec as P

MESH = pl.DeviceIdType.MESH
NLON = 1440
NLAT = 256
DEG = 96
OCT = 180
LOG2E = 1.4426950408889634
NEG = -1e30
EPS = 1e-05
KB = 48
KEYS = 5 * KB
F32 = jnp.float32
BF = jnp.bfloat16
DMA = pltpu.SemaphoreType.DMA
VMEM = pl.BlockSpec(memory_space=pltpu.VMEM)
TN = (((0,), (0,)), ((), ()))
NT = (((1,), (1,)), ((), ()))


def win_start(w):
    return 45 * w // 4


def ring_dev(w, group):
    return (group * 4 + w // 4, w % 4)


def place():
    lat = lax.axis_index("lat")
    ch = lax.axis_index("ch")
    return lat, ch, lat // 4, lat % 4


def signal(device):
    pl.semaphore_signal(pltpu.get_barrier_semaphore(), inc=1, device_id=device, device_id_type=MESH)


def remote(src, dst, ss, rs, device):
    pltpu.make_async_remote_copy(
        src_ref=src, dst_ref=dst, send_sem=ss, recv_sem=rs, device_id=device, device_id_type=MESH
    ).start()


def wait_bytes(ref, sem):
    pltpu.make_async_copy(ref, ref, sem).wait()


def loop(lo, hi, body):
    def step(i, c):
        body(i)
        return c

    lax.fori_loop(lo, hi, step, 0)


def sort_rows():
    n = lax.broadcasted_iota(jnp.int32, (1024, 1), 0)
    slot = n % 16
    source = jnp.where(slot < 12, (slot % 4) * 192 + (slot // 4) * 64 + n // 16, -1)
    return (lax.broadcasted_iota(jnp.int32, (1024, 768), 1) == source).astype(F32).astype(BF)


def tables(tab_s, t_ref):
    row = lax.broadcasted_iota(jnp.int32, (2 * DEG, 128), 0)
    lane = lax.broadcasted_iota(jnp.int32, (2 * DEG, 128), 1).astype(F32)
    first = row < DEG
    order = jnp.where(first, row, row - DEG).astype(F32)

    def angle(cells):
        turns = cells * order
        turns = turns - NLON * jnp.floor((turns + 0.5) * (1.0 / NLON))
        return turns * (2.0 * math.pi / NLON)

    coarse, fine = angle(jnp.where(lane < 12, lane * 128.0, 0.0)), angle(lane)
    ca, sa, cb, sb = jnp.cos(coarse), jnp.sin(coarse), jnp.cos(fine), jnp.sin(fine)
    u = jnp.where(first, cb, -sb)
    v = jnp.where(first, -sb, -cb)
    for a in range(12):
        n = min(128, NLON - a * 128)
        tab = ca[:, a : a + 1] * u + sa[:, a : a + 1] * v
        tab_s[:, a * 128 : a * 128 + n] = tab[:, :n]
        t_ref[:, a * 128 : a * 128 + n] = tab[:, :n].astype(BF)


def legendre(lat, leg_s, e_s):
    lane = lax.broadcasted_iota(jnp.int32, (8, 128), 1)
    n = lax.broadcasted_iota(jnp.int32, (8, 128), 0) * 128 + lane
    kind = (n % 16) // 4
    row = (n // 16) * 4 + n % 4
    theta = (row.astype(F32) + 0.5) * (math.pi / NLAT)
    factor = lax.broadcasted_iota(jnp.int32, (1, 128), 1)
    number = jnp.maximum(factor, 1).astype(F32)
    log_ratio = jnp.log((2.0 * number - 1.0) / (2.0 * number))
    m = jnp.zeros((8, 128), F32)
    begin = jnp.zeros((8, 128), F32)
    for k in range(3):
        order = (lat + 64 * k) % DEG
        total = jnp.sum(jnp.where((factor >= 1) & (factor <= order), log_ratio, 0.0), axis=1, keepdims=True)
        m = jnp.where(kind == k, order.astype(F32), m)
        begin = jnp.where(kind == k, total, begin)
    begin = 0.5 * (begin + jnp.log((2.0 * m + 1.0) / (4.0 * math.pi)))
    diagonal = jnp.where(kind < 3, jnp.exp(begin + m * jnp.log(jnp.sin(theta))), 0.0)
    cosine = jnp.cos(theta)

    def degree(l, carry):
        previous, earlier = carry
        deg = l.astype(F32)
        less = deg - 1.0
        upper = jnp.sqrt(jnp.maximum(4.0 * deg * deg - 1.0, 0.0) / jnp.maximum(deg * deg - m * m, 1.0))
        lower = jnp.sqrt(jnp.maximum(less * less - m * m, 0.0) / jnp.maximum(4.0 * less * less - 1.0, 1.0))
        value = upper * (cosine * previous - lower * earlier)
        current = jnp.where(m == deg, diagonal, jnp.where(m < deg, value, 0.0))
        leg_s[l] = current
        return current, previous

    zero = diagonal * 0.0
    lax.fori_loop(0, DEG, degree, (zero, zero))
    kind = (lax.broadcasted_iota(jnp.int32, (DEG, 128), 1) % 16) // 4
    for c in range(8):
        part = leg_s[:, c, :]
        for k in range(3):
            e_s[k * DEG : k * DEG + DEG, c * 128 : c * 128 + 128] = jnp.where(kind == k, part, 0.0).astype(BF)


def layer_kernel(
    f_ref, gain_ref, wq_ref, wo_ref, bias_ref, reach_ref, mg_ref, ws_ref,
    out_ref,
    x_s, win_s, w_s, meta_s, metas_s, stat_s, tab_s, leg_s, e_s, send1_s, got_s, g_s, send2_s,
    q_s, k_s, v_s, b_s, t_s, a_s, s_s, p_s, l_s, r_s, y_s, got2_s, local_s, t16_s, wave_s,
    lsem, statsem, metasem, w1sem, wxsem, wbsem, w2sem, ssem, usem, nsem, hsem, a1sem, a2sem, gsem, bsem,
):
    lat, ch, group, zlo = place()
    me = zlo * 4 + ch
    has_next = group < 15
    has_prev = group > 0
    quarter = pl.ds(pl.multiple_of((group // 4) * 128, 128), 128)
    sixteenth = pl.ds(pl.multiple_of(group * 32, 32), 32)
    sib = ch + 1 - 2 * (ch % 2)
    across = (ch + 2) % 4
    loop(1, 64, lambda d: signal(((lat + d) % 64, ch)))
    for z in range(4):
        for d in range(1, 4):
            signal((group * 4 + z, (ch + d) % 4))
    for d in range(1, 4):
        signal(((lat + 16 * d) % 64, sib))

    ones = jnp.ones((8, 256), BF)
    for r in range(4):
        x = f_ref[r].astype(F32)
        x = x * x
        high = x.astype(BF)
        both = jnp.concatenate([high, (x - high.astype(F32)).astype(BF)], axis=1)
        sums = lax.dot_general(ones, both, NT, preferred_element_type=F32)
        stat_s[ch, r : r + 1, :] = sums[0:1]
    gain = gain_ref[...].astype(F32)
    meta_s[...] = jnp.zeros_like(meta_s)
    for a in range(5):
        for h in range(2):
            meta_s[h * 8 + a : h * 8 + a + 1, 0:17] = bias_ref[a, h : h + 1, :]
    meta_s[16:20, 0:5] = reach_ref[...].astype(F32)
    meta_s[20:21, :] = gain

    def interleave(c):
        lon = pl.ds(pl.multiple_of(c * 144, 16), 144)
        for a in range(2):
            two = [f_ref[2 * a + b, lon, :].astype(F32).reshape(18, 8, 128) for b in range(2)]
            x_s[a, pl.ds(c * 18, 18)] = jnp.stack(two, axis=1).reshape(18, 16, 128).astype(BF)

    loop(0, 10, interleave)

    @pl.when(jnp.logical_not(has_prev))
    def _():
        win_s[0] = jnp.zeros_like(win_s[0])

    @pl.when(jnp.logical_not(has_next))
    def _():
        win_s[9] = jnp.zeros_like(win_s[9])

    pl.semaphore_wait(pltpu.get_barrier_semaphore(), 78)

    for d in range(1, 4):
        remote(stat_s.at[ch], stat_s.at[ch], statsem.at[0], statsem.at[1], (lat, (ch + d) % 4))
    for d in range(1, 4):
        remote(meta_s, metas_s.at[me], metasem.at[0], metasem.at[1], (lat, (ch + d) % 4))
        remote(meta_s, metas_s.at[me], metasem.at[0], metasem.at[1], (group * 4 + (zlo + d) % 4, ch))
    remote(wq_ref.at[:, sixteenth], w_s.at[pl.ds(ch * 4, 3), sixteenth], w1sem.at[0], w1sem.at[1], (lat, across))
    remote(wo_ref.at[sixteenth], w_s.at[ch * 4 + 3, sixteenth], w1sem.at[0], w1sem.at[1], (lat, across))
    remote(wq_ref, w_s.at[pl.ds(ch * 4, 3)], wbsem.at[0], wbsem.at[1], (lat, sib))
    remote(wo_ref, w_s.at[ch * 4 + 3], wbsem.at[0], wbsem.at[1], (lat, sib))
    own = [
        pltpu.make_async_copy(meta_s, metas_s.at[me], lsem.at[2]),
        pltpu.make_async_copy(wq_ref, w_s.at[pl.ds(ch * 4, 3)], lsem.at[3]),
        pltpu.make_async_copy(wo_ref, w_s.at[ch * 4 + 3], lsem.at[4]),
    ]
    for copy in own:
        copy.start()

    def move(w, src_pair, pairs, dst_pair, start):
        s = win_start(w)
        src, dst = pl.ds(src_pair, pairs), pl.ds(dst_pair, pairs)
        edge = (w == 0) | (w == 15)

        @pl.when(edge)
        def _():
            a_src = jnp.where(w == 0, 0, s - 1)
            a_dst = jnp.where(w == 0, 1, 0)
            b_src = jnp.where(w == 0, OCT - 1, 0)
            b_dst = jnp.where(w == 0, 0, 13)
            start(x_s.at[src, pl.ds(a_src, 13)], win_s.at[dst, ch, pl.ds(a_dst, 13)], 0)
            start(x_s.at[src, pl.ds(b_src, 1)], win_s.at[dst, ch, pl.ds(b_dst, 1)], 1)

        @pl.when(jnp.logical_not(edge))
        def _():
            start(x_s.at[src, pl.ds(s - 1, 14)], win_s.at[dst, ch], 0)

    def to(pair, ss, rs, dz, dc):
        z = ((ch // 2) * 4 + zlo + dz) % 8
        w = (z % 4) * 4 + (z // 4) * 2 + (ch + dc) % 2
        move(w, pair, 1, 1 + 2 * zlo + pair, lambda a, b, n: remote(a, b, ss, rs, ring_dev(w, group)))

    def near(pair, ss, rs):
        def one(t):
            u = t // 2
            dz = jnp.where(u == 4, 0, jnp.where(u % 2 == 0, u // 2 + 1, 7 - u // 2))
            to(pair, ss, rs, dz, jnp.where(t == 8, 1, t % 2))

        loop(0, 9, one)

    def far(pair, ss, rs):
        def one(t):
            u = t // 2
            to(pair, ss, rs, jnp.where(u == 0, 3, jnp.where(u == 1, 5, 4)), t % 2)

        loop(0, 6, one)

    move(me, 0, 2, 1 + 2 * zlo, lambda a, b, n: pltpu.make_async_copy(a, b, lsem.at[n]).start())
    urgent = jnp.where(zlo == 3, 1, 0)
    first = (urgent, ssem.at[0], usem.at[jnp.where(zlo == 0, 1, jnp.where(zlo == 3, 2, 0))])
    second = (1 - urgent, ssem.at[1], nsem)
    near(*first)
    far(*first)

    tables(tab_s, t16_s)
    wait_bytes(stat_s.at[pl.ds(0, 3)], statsem.at[1])
    scale = lax.rsqrt((stat_s[0] + stat_s[1] + stat_s[2] + stat_s[3]) * (1.0 / 512.0) + EPS)
    theta = ((lat * 4 + lax.broadcasted_iota(jnp.int32, (4, 128), 0)).astype(F32) + 0.5) * (math.pi / NLAT)
    weight = jnp.sin(theta) * (math.pi / NLAT * 2.0 * math.pi / NLON) * gain
    freq = []
    for r in range(4):
        lhs = (tab_s[...] * scale[r : r + 1, :]).astype(BF)
        out = jnp.dot(lhs, f_ref[r], preferred_element_type=F32)
        freq.append((out * weight[r : r + 1, :]).astype(BF))
    out = jnp.dot(sort_rows(), jnp.concatenate(freq, axis=0), preferred_element_type=F32)
    send1_s[...] = out.astype(BF).reshape(64, 16, 128)
    loop(1, 64, lambda d: remote(send1_s.at[(lat + d) % 64], got_s.at[lat], a1sem.at[0], a1sem.at[1], ((lat + d) % 64, ch)))
    got_s[lat] = send1_s[lat]

    near(*second)

    wait_bytes(w_s.at[pl.ds(across * 4, 4), sixteenth], w1sem.at[1])
    strip = w_s.at[pl.ds(across * 4, 4), sixteenth]
    for d in range(1, 4):
        remote(strip, strip, wxsem.at[0], wxsem.at[1], (lat - group % 4 * 4 + (group + d) % 4 * 4, ch))
    legendre(lat, leg_s, e_s)
    part = w_s.at[pl.ds(across * 4, 4), quarter]
    wait_bytes(w_s.at[pl.ds(0, 3), pl.ds(0, 128)], wxsem.at[1])
    remote(part, part, w2sem.at[0], w2sem.at[1], (lat, sib))
    for d in range(1, 4):
        remote(part, part, w2sem.at[0], w2sem.at[1], ((lat + 16 * d) % 64, ch))
        remote(part, part, w2sem.at[0], w2sem.at[1], ((lat + 16 * d) % 64, sib))

    @pl.when((me == 0) | (me == 15))
    def _():
        wait_bytes(win_s.at[pl.ds(0, 2), 0, pl.ds(0, 13)], lsem.at[0])
        wait_bytes(win_s.at[pl.ds(0, 2), 0, pl.ds(0, 1)], lsem.at[1])

    @pl.when((me != 0) & (me != 15))
    def _():
        wait_bytes(win_s.at[pl.ds(0, 2), 0], lsem.at[0])

    def arrived(own_here, full, sem):
        pl.when(own_here)(lambda: wait_bytes(win_s.at[pl.ds(0, full - 1), 0], sem))
        pl.when(jnp.logical_not(own_here))(lambda: wait_bytes(win_s.at[pl.ds(0, full), 0], sem))

    arrived(zlo == 0, 4, usem.at[1])
    arrived(zlo == 3, 4, usem.at[2])
    pl.when(has_next)(lambda: remote(win_s.at[8], win_s.at[0], hsem.at[0], hsem.at[1], ((lat + 4) % 64, ch)))
    pl.when(has_prev)(lambda: remote(win_s.at[1], win_s.at[9], hsem.at[2], hsem.at[3], ((lat + 60) % 64, ch)))

    far(*second)


    for copy in own:
        copy.wait()
    wait_bytes(metas_s.at[pl.ds(0, 6)], metasem.at[1])
    lane = lax.broadcasted_iota(jnp.int32, (32, KEYS), 1)
    query = lax.broadcasted_iota(jnp.int32, (32, KEYS), 0)
    row_of = sum((lane >= KB * a).astype(jnp.int32) for a in range(1, 5))
    delta = lane - KB * row_of - query - 8
    dist = jnp.abs(delta).astype(F32)
    lane8 = lax.broadcasted_iota(jnp.int32, (8, KEYS), 1)
    row8 = sum((lane8 >= KB * a).astype(jnp.int32) for a in range(1, 5))
    onto = (row8 == lax.broadcasted_iota(jnp.int32, (8, KEYS), 0)).astype(F32)
    for h in range(8):
        mine = metas_s[zlo * 4 + h // 2, (h % 2) * 8 : (h % 2) * 8 + 8, :]
        vec = lax.dot_general(mine, onto, TN, precision=lax.Precision.HIGHEST, preferred_element_type=F32)
        tile = jnp.full((32, KEYS), NEG, F32)
        for b in range(17):
            tile = jnp.where(delta == b - 8, vec[b : b + 1, :] * LOG2E, tile)
        b_s[h // 2, (h % 2) * 32 : (h % 2) * 32 + 32, :] = tile
    lane128 = lax.broadcasted_iota(jnp.int32, (128, KEYS), 1)
    row128 = sum((lane128 >= KB * a).astype(jnp.int32) for a in range(1, 5))
    pick = (row128 == lax.broadcasted_iota(jnp.int32, (128, KEYS), 0)).astype(F32)
    for z in range(4):
        r_s[z * 8 : z * 8 + 8, :] = jnp.dot(metas_s[z * 4 + ch, 16:24, :], pick, preferred_element_type=F32)

    def weights(t):
        return jnp.concatenate([w_s[k * 4 + t] for k in range(4)], axis=1)

    def project(pair, inner):
        parts = []
        for k in range(4):
            p = win_s[pair, k].astype(F32).reshape(14, 2, 8, 128)
            parts.append(jnp.concatenate([p[:, r].reshape(112, 128) for r in range(2)], axis=0))
        square = jnp.sum(sum(p * p for p in parts), axis=1, keepdims=True)
        scale = lax.rsqrt(square * (1.0 / 512.0) + EPS)
        normed = jnp.concatenate(
            [(p * scale * metas_s[zlo * 4 + k, 20:21, :]).astype(BF) for k, p in enumerate(parts)], axis=1
        )
        rows = pl.ds(pair * 2, 2)
        for t, dst, lo, n in ((0, q_s, 8, 96), (1, k_s, 0, 112), (2, v_s, 0, 112)):
            if t == 0 and not inner:
                continue
            out = jnp.dot(normed, weights(t), preferred_element_type=F32).reshape(2, 112, 512)[:, lo : lo + n, :]
            if t == 0:
                out = out * (LOG2E / 8.0)
            dst[rows] = out.astype(BF)

    wait_bytes(w_s.at[pl.ds(0, 4)], wbsem.at[1])
    wait_bytes(w_s.at[pl.ds(0, 7)], w2sem.at[1])
    arrived((zlo == 1) | (zlo == 2), 8, usem.at[0])
    loop(0, 4, lambda i: project(1 + 2 * i + i // 3, True))

    wait_bytes(win_s.at[pl.ds(0, 5), pl.ds(0, 3)], nsem)
    pl.when(has_prev)(lambda: wait_bytes(win_s.at[0], hsem.at[1]))
    pl.when(has_next)(lambda: wait_bytes(win_s.at[0], hsem.at[3]))
    loop(0, 2, lambda i: project(2 * zlo + i * jnp.where(zlo == 3, 1, 2), True))

    left = lax.broadcasted_iota(jnp.int32, (32, 128), 1) < 64
    blocks = [(j, hp) for j in range(3) for hp in range(4)]
    lane1 = row_of[0:1, :]

    def attend_row(i):
        at = group * 16 + i - 2 + lane1
        inside = (at >= 0) & (at < NLAT)
        reach = jnp.where(inside, r_s[pl.ds((i // 4) * 8 + i % 4, 1), :], -1.0)
        allowed = dist <= reach
        for hp in range(4):
            t_s[hp, 0:32, :] = jnp.where(allowed, b_s[hp, 0:32, :], NEG)
            t_s[hp, 32:64, :] = jnp.where(allowed, b_s[hp, 32:64, :], NEG)
        for n, (j, hp) in enumerate(blocks):
            cols = slice(hp * 128, hp * 128 + 128)
            qb = q_s[i + 2, j * 32 : j * 32 + 32, cols]
            zero = jnp.zeros_like(qb)
            qq = jnp.concatenate([jnp.where(left, qb, zero), jnp.where(left, zero, qb)], axis=0)
            kb = k_s[pl.ds(i, 5), j * 32 : j * 32 + KB, cols].reshape(KEYS, 128)
            s_s[n] = lax.dot_general(qq, kb, NT, preferred_element_type=F32) + t_s[hp]
        for n in range(12):
            s = s_s[n]
            p = jnp.exp2(s - jnp.max(s, axis=1, keepdims=True))
            l_s[n] = jnp.broadcast_to(jnp.sum(p, axis=1, keepdims=True), (64, 128))
            p_s[n] = p.astype(BF)
        for n, (j, hp) in enumerate(blocks):
            cols = slice(hp * 128, hp * 128 + 128)
            vb = v_s[pl.ds(i, 5), j * 32 : j * 32 + KB, cols].reshape(KEYS, 128)
            o = jnp.dot(p_s[n], vb, preferred_element_type=F32) / l_s[n]
            a_s[i % 2, j * 32 : j * 32 + 32, cols] = jnp.where(left, o[:32], o[32:]).astype(BF)

    s = win_start(me)
    wide = win_start(me + 1) - s == 12

    def rows_of(step):
        pair = (2 * zlo + step) % 8
        loop(0, 2, lambda r: attend_row(pair * 2 + r))
        out = jnp.dot(a_s[...].reshape(192, 512), weights(3), preferred_element_type=F32).reshape(2, 12, 8, 512)
        for k in range(4):
            both = jnp.stack([out[b, :, :, k * 128 : k * 128 + 128] for b in range(2)], axis=1)
            y_s[pair, k] = both.reshape(12, 16, 128).astype(BF)

        def give(k, n, start):
            start(y_s.at[pair, k, pl.ds(0, n)], local_s.at[pair % 2, pl.ds(s, n)])

        def both(k, start):
            pl.when(wide)(lambda: give(k, 12, start))
            pl.when(jnp.logical_not(wide))(lambda: give(k, 11, start))

        for d in range(1, 4):
            k = (ch + d) % 4
            both(k, lambda a, b, k=k: remote(a, b, bsem.at[0], bsem.at[1], (group * 4 + pair // 2, k)))
        if isinstance(step, int):
            both(ch, lambda a, b: pltpu.make_async_copy(a, b, lsem.at[5 + step]).start())
        else:
            both(ch, lambda a, b: remote(a, b, bsem.at[0], bsem.at[1], (group * 4 + pair // 2, ch)))

    rows_of(0)

    wait_bytes(got_s.at[pl.ds(0, 63)], a1sem.at[1])
    coef = jnp.dot(e_s[...], got_s[...].reshape(1024, 128), preferred_element_type=F32)
    coef = coef.reshape(3, DEG, 128) * mg_ref[...][None]
    g_s[ch] = coef.reshape(3 * DEG, 128).astype(BF)
    remote(g_s.at[ch], g_s.at[ch], gsem.at[0], gsem.at[1], (lat, across))
    remote(g_s.at[ch], g_s.at[ch], gsem.at[2], gsem.at[3], (lat, sib))

    loop(0, 3, lambda i: project(jnp.where(i < zlo, 2 * i, jnp.where(i == 2, 7, 4 + 2 * i)), True))
    project(9, False)
    rows_of(1)
    wait_bytes(g_s.at[0], gsem.at[1])
    remote(g_s.at[across], g_s.at[across], gsem.at[2], gsem.at[3], (lat, sib))
    loop(2, 5, rows_of)
    wait_bytes(g_s.at[pl.ds(0, 2)], gsem.at[3])
    gained = jnp.concatenate([g_s[k] for k in range(4)], axis=1)
    mixed = jnp.dot(gained, ws_ref[...].astype(BF), preferred_element_type=F32)
    parts = []
    for k in range(3):
        twice = jnp.where((lat + 64 * k) % DEG == 0, 1.0, 2.0).astype(F32)
        parts.append((mixed[k * DEG : k * DEG + DEG] * twice).astype(BF))
    rows_out = lax.dot_general(e_s[...], jnp.concatenate(parts, axis=0), TN, preferred_element_type=F32)
    send2_s[...] = rows_out.astype(BF).reshape(64, 16, 128)
    loop(1, 64, lambda d: remote(send2_s.at[(lat + d) % 64], got2_s.at[lat], a2sem.at[0], a2sem.at[1], ((lat + d) % 64, ch)))
    got2_s[lat] = send2_s[lat]

    loop(5, 8, rows_of)

    wait_bytes(got2_s.at[pl.ds(0, 63)], a2sem.at[1])
    modes = lax.dot_general(sort_rows(), got2_s[...].reshape(1024, 128), TN, preferred_element_type=F32).astype(BF)
    for r in range(4):
        wave_s[r] = lax.dot_general(t16_s[...], modes[r * 192 : r * 192 + 192], TN, preferred_element_type=F32)

    wait_bytes(stat_s.at[pl.ds(0, 3)], statsem.at[0])
    wait_bytes(metas_s.at[pl.ds(0, 6)], metasem.at[0])
    wait_bytes(strip, w1sem.at[0])
    wait_bytes(w_s.at[pl.ds(0, 3), pl.ds(0, 128)], wxsem.at[0])
    wait_bytes(w_s.at[pl.ds(0, 4)], wbsem.at[0])
    wait_bytes(w_s.at[pl.ds(0, 7)], w2sem.at[0])
    wait_bytes(win_s.at[pl.ds(0, 5), pl.ds(0, 3)], ssem.at[0])
    wait_bytes(win_s.at[pl.ds(0, 5), pl.ds(0, 3)], ssem.at[1])
    pl.when(has_next)(lambda: wait_bytes(win_s.at[0], hsem.at[0]))
    pl.when(has_prev)(lambda: wait_bytes(win_s.at[0], hsem.at[2]))
    wait_bytes(got_s.at[pl.ds(0, 63)], a1sem.at[0])
    wait_bytes(g_s.at[0], gsem.at[0])
    wait_bytes(g_s.at[pl.ds(0, 2)], gsem.at[2])
    wait_bytes(got2_s.at[pl.ds(0, 63)], a2sem.at[0])

    def last(n):
        wait_bytes(local_s.at[0, pl.ds(0, n)], lsem.at[5])
        wait_bytes(local_s.at[0, pl.ds(0, n)], lsem.at[6])
        wait_bytes(local_s.at[:, pl.ds(0, 15 * n)], bsem.at[0])
        wait_bytes(local_s.at[:, pl.ds(0, OCT - n)], bsem.at[1])

    pl.when(wide)(lambda: last(12))
    pl.when(jnp.logical_not(wide))(lambda: last(11))

    def total(c):
        lon = pl.ds(pl.multiple_of(c * 144, 16), 144)
        for a in range(2):
            part = local_s[a, pl.ds(c * 18, 18)].astype(F32).reshape(18, 2, 8, 128)
            for b in range(2):
                out_ref[2 * a + b, lon, :] = (wave_s[2 * a + b, lon, :] + part[:, b].reshape(144, 128)).astype(BF)

    loop(0, 10, total)


def layer(*args):
    shape = jax.ShapeDtypeStruct
    vm = pltpu.VMEM
    return pl.pallas_call(
        layer_kernel,
        out_shape=shape((4, NLON, 128), BF),
        in_specs=[VMEM] * 8,
        out_specs=VMEM,
        scratch_shapes=[
            vm((2, OCT, 16, 128), BF),
            vm((10, 4, 14, 16, 128), BF),
            vm((16, 512, 128), BF),
            vm((24, 128), F32),
            vm((16, 24, 128), F32),
            vm((4, 4, NLON), F32),
            vm((2 * DEG, NLON), F32),
            vm((DEG, 8, 128), F32),
            vm((3 * DEG, 1024), BF),
            vm((64, 16, 128), BF),
            vm((64, 16, 128), BF),
            vm((4, 3 * DEG, 128), BF),
            vm((64, 16, 128), BF),
            vm((20, 96, 512), BF),
            vm((20, 112, 512), BF),
            vm((20, 112, 512), BF),
            vm((4, 64, KEYS), F32),
            vm((4, 64, KEYS), F32),
            vm((2, 96, 512), BF),
            vm((12, 64, KEYS), F32),
            vm((12, 64, KEYS), BF),
            vm((12, 64, 128), F32),
            vm((32, KEYS), F32),
            vm((8, 4, 12, 16, 128), BF),
            vm((64, 16, 128), BF),
            vm((2, OCT, 16, 128), BF),
            vm((2 * DEG, NLON), BF),
            vm((4, NLON, 128), F32),
            DMA((7,)), DMA((2,)), DMA((2,)), DMA((2,)), DMA((2,)), DMA((2,)), DMA((2,)), DMA((2,)), DMA((3,)), DMA,
            DMA((4,)), DMA((2,)), DMA((2,)), DMA((4,)), DMA((2,)),
        ],
        compiler_params=pltpu.CompilerParams(
            collective_id=0, has_side_effects=True, vmem_limit_bytes=56 * 1024 * 1024
        ),
        name="layer",
    )(*args)


def per_device(fields, norm_gain, w_qkv, w_out, rel_bias, stencil_reach, mode_gain, w_spec):
    return layer(
        fields,
        norm_gain.reshape(1, 128),
        jnp.transpose(w_qkv, (1, 0, 2)),
        w_out,
        jnp.transpose(rel_bias, (1, 0, 2)),
        stencil_reach,
        mode_gain,
        w_spec,
    )


def solution(mesh):
    in_specs = (
        P("lat", None, "ch"),
        P("ch"),
        P(None, None, "ch"),
        P(None, "ch"),
        P("ch", None, None),
        P("lat", None),
        P(None, "ch"),
        P(None, "ch"),
    )
    return jax.shard_map(
        per_device, mesh=mesh, in_specs=in_specs, out_specs=P("lat", None, "ch"), check_vma=False
    )
```
